32 devices in a mesh: batch: 16 (over z, x, core), mp: 2 (over y).
Axes of the slice: x: 2, y: 2, z: 4, core: 2. Of those that a mesh axis runs over, the one named last changes fastest.
Arguments:
- inputs: float32 [32, 2048, 512], P(('batch', 'mp')), may hold values from -6 to 6
- cotangent: float32 [32, 2048, 512], P(('batch', 'mp')), may hold values from -6 to 6
- block_perm: int32 [32, 64], P(('batch', 'mp')), may hold values from 0 to 63, each once within a row
- block_mask: int32 [32, 64], P(('batch', 'mp')), may hold values from 0 to 1, as said below
- pen_weight: float32 [1], replicated, may hold values from 131072 to 262144
- w_query: float32 [512, 512], replicated, may hold values from -0.25 to 0.25
- w_key: float32 [512, 512], replicated, may hold values from -0.25 to 0.25
- w_value: float32 [512, 512], replicated, may hold values from -0.25 to 0.25
- w_out: float32 [512, 512], replicated, may hold values from -1 to 1
- w_sort: float32 [512, 512], replicated, may hold values from -0.0625 to 0.0625
- gain_one: float32 [512], replicated, may hold values from 0.5 to 1.5
- gain_two: float32 [512], replicated, may hold values from 0.5 to 1.5
- w_up: float32 [512, 2048], P(None, 'mp'), may hold values from -0.25 to 0.25
- w_down: float32 [2048, 512], P('mp'), may hold values from -0.125 to 0.125
Outputs:
- output: float32 [32, 2048, 512], P(('batch', 'mp'))
- penalty: float32 [1], replicated
- grad_input: float32 [32, 2048, 512], P(('batch', 'mp'))
- grad_query: float32 [512, 512], replicated
- grad_key: float32 [512, 512], replicated
- grad_value: float32 [512, 512], replicated
- grad_out: float32 [512, 512], replicated
- grad_sort: float32 [512, 512], replicated
- grad_gain_one: float32 [512], replicated
- grad_gain_two: float32 [512], replicated
- grad_up: float32 [512, 2048], P(None, 'mp')
- grad_down: float32 [2048, 512], P('mp')
The draws below stay inside these ranges and needn't reach their ends.
Inputs may be any that keep to these rules, and one draw needn't show every extreme that they name: `block_mask`: block 0 of every sequence is real.
All inputs are finite; a program needn't handle non-finite values.
Results may differ from the reference program's by a relative error of at most 0.015.
Values may be sent and summed in bfloat16 or wider, within the bound.
No kernel may reach another device: no remote copies, remote signals or barrier semaphores. Data moves between devices by JAX's collectives and lax.ppermute only.
A program may use at most 384 MiB of HBM per device.

```python
import jax
import jax.numpy as jnp
from jax import lax

D = 512
HEADS = 8
HEAD_DIM = 64
FF = 2048
BLOCK = 32
ITERS = 8
LEN = 2048
NBLOCKS = 64
SEQS = 32


def draw_block_mask(key, part):
    key = jax.random.fold_in(key, 5)
    sequence = jnp.arange(SEQS, dtype=jnp.int32)
    threshold = 300 + 700 * sequence // max(SEQS - 1, 1)
    ticket = jax.random.randint(key, (SEQS, NBLOCKS), 0, 1000, dtype=jnp.int32)
    leading = jnp.arange(NBLOCKS, dtype=jnp.int32)[None, :] == 0
    return ((ticket < threshold[:, None]) | leading).astype(jnp.int32)


def block_levels(own_key, shape, pieces, low, top_value):
    level, own = 1.0, jax.random.fold_in(own_key, 6)
    for dim, blocks in pieces:
        draws = jnp.exp(jax.random.uniform(jax.random.fold_in(own, dim), (blocks,), jnp.float32, low / len(pieces), top_value / len(pieces)))
        level = level * jnp.repeat(draws, shape[dim] // blocks).reshape([-1 if axis == dim else 1 for axis in range(len(shape))])
    return level


def normal_values(key, shape, deviation, limit, shards=(), held_as=jnp.bfloat16):
    level = block_levels(key, shape, shards, -0.22, 0.18) if shards else 1.0
    values = jax.random.normal(key, shape, jnp.float32) * deviation * level
    return jnp.minimum(jnp.maximum(values, -limit), limit).astype(held_as)


def setup_inputs(seed: int = 0) -> dict:
    splits = jax.random.split(jax.random.key(seed), 15)
    return {
        "inputs": normal_values(splits[0], (SEQS, LEN, D), 1.0, 6.0, ((0, 32),), jnp.float32),
        "cotangent": normal_values(splits[1], (SEQS, LEN, D), 1.0, 6.0, ((0, 32),), jnp.float32),
        "block_perm": jax.vmap(lambda own: jax.random.permutation(own, NBLOCKS))(jax.random.split(splits[2], SEQS)).reshape((SEQS, NBLOCKS)).astype(jnp.int32),
        "block_mask": draw_block_mask(jax.random.fold_in(splits[14], 71), 0),
        "pen_weight": jnp.clip(jax.random.uniform(splits[4], (1,), jnp.float32, 131072.0, 262144.0), 131072.0, 262144.0),
        "w_query": normal_values(splits[5], (D, D), D ** -0.5, 0.25, (), jnp.float32),
        "w_key": normal_values(splits[6], (D, D), D ** -0.5, 0.25, (), jnp.float32),
        "w_value": normal_values(splits[7], (D, D), D ** -0.5, 0.25, (), jnp.float32),
        "w_out": normal_values(splits[8], (D, D), (D // 16) ** -0.5, 1.0, (), jnp.float32),
        "w_sort": normal_values(splits[9], (D, HEADS * NBLOCKS), (16 * D) ** -0.5, 0.0625, (), jnp.float32),
        "gain_one": jnp.clip(1.0 + 0.1 * jax.random.normal(splits[10], (D,), jnp.float32), 0.5, 1.5),
        "gain_two": jnp.clip(1.0 + 0.1 * jax.random.normal(splits[11], (D,), jnp.float32), 0.5, 1.5),
        "w_up": normal_values(splits[12], (D, FF), D ** -0.5, 0.25, ((1, 2),), jnp.float32),
        "w_down": normal_values(splits[13], (FF, D), FF ** -0.5, 0.125, ((0, 2),), jnp.float32),
    }


EPSILON = 1e-05
HIGHEST = lax.Precision.HIGHEST

@jax.custom_vjp
def low(v):
    return lax.optimization_barrier(v.astype(jnp.bfloat16)).astype(jnp.float32)

@jax.custom_vjp
def low_back(v):
    return v

def low_keep(v):
    return (low(v), None)

def low_pass(kept, grad):
    return (grad,)

def back_keep(v):
    return (v, None)

def back_low(kept, grad):
    return (low(grad),)
low.defvjp(low_keep, low_pass)
low_back.defvjp(back_keep, back_low)

def matrix_product(left, right):
    return jnp.dot(left, right, precision=HIGHEST, preferred_element_type=jnp.float32)

def layer_norm(values, gain):
    center = values - lax.optimization_barrier(jnp.mean(values, axis=-1, keepdims=True))
    variance = lax.optimization_barrier(jnp.mean(center * center, axis=-1, keepdims=True))
    return center * lax.rsqrt(variance + EPSILON) * gain

def balance_plans(sorting_logits):
    for iteration in range(ITERS):
        sorting_logits = sorting_logits - jax.scipy.special.logsumexp(sorting_logits, axis=-1, keepdims=True)
        sorting_logits = sorting_logits - jax.scipy.special.logsumexp(sorting_logits, axis=-2, keepdims=True)
    return sorting_logits

def forward(params, inputs, perm_rows, mask_rows, block_total):
    w_query, w_key, w_value, w_out, w_sort, gain_one, gain_two, w_up, w_down = params
    group_size, seq_len, model_width = inputs.shape
    block_count = seq_len // BLOCK
    token_count = group_size * seq_len
    head_shape = (group_size, block_count, BLOCK, HEADS, HEAD_DIM)
    normed_one = low(layer_norm(inputs, gain_one))
    flat_one = normed_one.reshape(token_count, model_width)
    query = low(low_back(matrix_product(flat_one, low(w_query)))).reshape(head_shape)
    key_rows = low(low_back(matrix_product(flat_one, low(w_key)))).reshape(head_shape)
    value_rows = low(low_back(matrix_product(flat_one, low(w_value)))).reshape(head_shape)
    block_sums = low(lax.optimization_barrier(jnp.sum(normed_one.reshape(group_size, block_count, BLOCK, model_width), axis=2)))
    block_sorting_logits = matrix_product(block_sums.reshape(-1, model_width), w_sort)
    block_sorting_logits = block_sorting_logits.reshape(group_size, block_count, HEADS, block_count).transpose(0, 2, 1, 3)
    plan_logarithm = balance_plans(block_sorting_logits)
    plan = jnp.exp(plan_logarithm)
    mask_float = mask_rows.astype(inputs.dtype)
    entropy = -jnp.sum(mask_float[:, None, :, None] * plan * plan_logarithm)
    positions = jnp.arange(block_count, dtype=jnp.int32)
    one_hot = (perm_rows[:, :, None] == positions[None, None, :]).astype(inputs.dtype)
    chosen = block_count * lax.optimization_barrier(jnp.sum(plan * one_hot[:, None, :, :], axis=-1))
    partner_real = jnp.take_along_axis(mask_rows, perm_rows, axis=1) > 0
    usable = partner_real & (perm_rows < positions[None, :])
    key_partner = jnp.einsum('gij,gjuhd->giuhd', one_hot, key_rows, precision=HIGHEST)
    value_partner = jnp.einsum('gij,gjuhd->giuhd', one_hot, value_rows, precision=HIGHEST)
    scaled = low(value_partner * chosen.transpose(0, 2, 1)[:, :, None, :, None])
    factor = HEAD_DIM ** (-0.5)
    own_scores = jnp.einsum('githd,giuhd->gihtu', query, key_rows, precision=HIGHEST) * factor
    far_scores = jnp.einsum('githd,giuhd->gihtu', query, key_partner, precision=HIGHEST) * factor
    scores = low_back(jnp.concatenate([own_scores, far_scores], axis=-1))
    lower_part = jnp.arange(BLOCK)[:, None] >= jnp.arange(BLOCK)[None, :]
    frame = (group_size, block_count, 1, BLOCK, BLOCK)
    allowed = jnp.concatenate([jnp.broadcast_to(lower_part, frame), jnp.broadcast_to(usable[:, :, None, None, None], frame)], axis=-1)
    scores = jnp.where(allowed, scores, -1e+30)
    weights = low(jax.nn.softmax(scores, axis=-1))
    attended = jnp.einsum('gihtu,giuhd->githd', weights[..., :BLOCK], value_rows, precision=HIGHEST)
    attended = attended + jnp.einsum('gihtu,giuhd->githd', weights[..., BLOCK:], scaled, precision=HIGHEST)
    attended = low(low_back(attended)).reshape(token_count, model_width)
    second = inputs.reshape(token_count, model_width) + low_back(matrix_product(attended, low(w_out)))
    normed_two = low(layer_norm(second, gain_two))
    hidden = low(jax.nn.gelu(low_back(matrix_product(normed_two, low(w_up)))))
    result = second + low_back(matrix_product(hidden, low(w_down)))
    return (result.reshape(inputs.shape), entropy / (HEADS * block_total))

def reference(inputs, cotangent, block_perm, block_mask, pen_weight, w_query, w_key, w_value, w_out, w_sort, gain_one, gain_two, w_up, w_down):
    block_total = jnp.sum(block_mask).astype(inputs.dtype)
    params = (w_query, w_key, w_value, w_out, w_sort, gain_one, gain_two, w_up, w_down)

    def regroup(values):
        return values.reshape((SEQS, 1) + values.shape[1:])

    def one_group(carry, item):
        grad_sum, pen_sum = carry
        group_in, group_cot, group_perm, group_mask = item

        def closed(weights_all, values):
            return forward(weights_all, values, group_perm, group_mask, block_total)
        (group_out, group_pen), pull_back = jax.vjp(closed, params, group_in)
        grads, group_grad = pull_back((group_cot, pen_weight[0]))
        return ((jax.tree.map(jnp.add, grad_sum, grads), pen_sum + group_pen), (group_out, group_grad))
    start = (jax.tree.map(jnp.zeros_like, params), jnp.zeros((), inputs.dtype))
    (grads, pen_total), (outputs, grad_rows) = lax.scan(one_group, start, (regroup(inputs), regroup(cotangent), regroup(block_perm), regroup(block_mask)))
    return (outputs.reshape(inputs.shape), pen_total.reshape(1), grad_rows.reshape(inputs.shape), grads[0], grads[1], grads[2], grads[3], grads[4], grads[5], grads[6], grads[7], grads[8])
```

```python
import functools

import jax
import jax.numpy as jnp
from jax import lax
from jax.experimental import pallas as pl
from jax.experimental.pallas import tpu as pltpu
from jax.sharding import PartitionSpec as P

HEADS = 8
HEAD_DIM = 64
BLOCK = 32
ITERS = 8
GROUP = 4
GROUP_WIDTH = GROUP * HEAD_DIM
GROUP_ROWS = GROUP * BLOCK
EPSILON = 1e-05
FACTOR = HEAD_DIM ** (-0.5)
HIGHEST = lax.Precision.HIGHEST
F32 = jnp.float32
BF16 = jnp.bfloat16
NT = (((1,), (1,)), ((), ()))
TN = (((0,), (0,)), ((), ()))
MIB = 1024 * 1024


def dot(left, right):
    return jnp.dot(left, right, preferred_element_type=F32)


def dot_nt(left, right):
    return lax.dot_general(left, right, NT, preferred_element_type=F32)


def dot_tn(left, right):
    return lax.dot_general(left, right, TN, preferred_element_type=F32)


def shape_of(dims, dtype):
    return jax.ShapeDtypeStruct(dims, dtype)


def whole(dims):
    return pl.BlockSpec(dims, lambda *_: (0,) * len(dims))


def rows_of(size, width):
    return pl.BlockSpec((size, width), lambda step, *_: (step, 0))


def params(mib):
    return pltpu.CompilerParams(vmem_limit_bytes=mib * MIB)


def normalize(values):
    center = values - jnp.mean(values, axis=-1, keepdims=True)
    inverse = lax.rsqrt(jnp.mean(center * center, axis=-1, keepdims=True) + EPSILON)
    return center * inverse, inverse


def norm_grad(grad_rows, unit_rows, inverse, gain):
    scaled_rows = grad_rows * gain
    return inverse * (
        scaled_rows
        - jnp.mean(scaled_rows, axis=-1, keepdims=True)
        - unit_rows * jnp.mean(scaled_rows * unit_rows, axis=-1, keepdims=True)
    )


def project_kernel(x_ref, gain_ref, wq_ref, wk_ref, wv_ref, act_ref, q_ref, k_ref, v_ref, sum_ref, w_ref):
    width = x_ref.shape[1]

    @pl.when(pl.program_id(0) == 0)
    def _():
        w_ref[:, :width] = wq_ref[...].astype(BF16)
        w_ref[:, width : 2 * width] = wk_ref[...].astype(BF16)
        w_ref[:, 2 * width :] = wv_ref[...].astype(BF16)

    unit, _ = normalize(x_ref[...])
    act = (unit * gain_ref[...]).astype(BF16)
    act_ref[...] = act
    q_ref[...] = dot(act, w_ref[:, :width]).astype(BF16)
    k_ref[...] = dot(act, w_ref[:, width : 2 * width]).astype(BF16)
    v_ref[...] = dot(act, w_ref[:, 2 * width :]).astype(BF16)
    rows = act.shape[0]
    sums = jnp.sum(act.astype(F32).reshape(rows // BLOCK, BLOCK, width), axis=1)
    sum_ref[...] = sums.astype(BF16).astype(F32)


def project(x, gain, wq, wk, wv, tile=512):
    rows, width = x.shape
    low = shape_of((rows, width), BF16)
    return pl.pallas_call(
        project_kernel,
        grid=(rows // tile,),
        in_specs=[rows_of(tile, width), whole((1, width))] + [whole((width, width))] * 3,
        out_specs=[rows_of(tile, width)] * 4 + [rows_of(tile // BLOCK, width)],
        out_shape=[low, low, low, low, shape_of((rows // BLOCK, width), F32)],
        scratch_shapes=[pltpu.VMEM((width, 3 * width), BF16)],
        compiler_params=params(48),
        cost_estimate=pl.CostEstimate(flops=6 * rows * width * width, bytes_accessed=15 * MIB, transcendentals=0),
        name="project",
    )(x, gain, wq, wk, wv)


def segment_sum(tile, first):
    left = jnp.sum(jnp.where(first, tile, 0.0), axis=1, keepdims=True)
    right = jnp.sum(jnp.where(first, 0.0, tile), axis=1, keepdims=True)
    return jnp.where(first, left, right)


def segment_max(tile, first):
    left = jnp.max(jnp.where(first, tile, -jnp.inf), axis=1, keepdims=True)
    right = jnp.max(jnp.where(first, -jnp.inf, tile), axis=1, keepdims=True)
    return jnp.where(first, left, right)


def lane_tiles(blocks):
    lane = lax.broadcasted_iota(jnp.int32, (blocks, 2 * blocks), 1)
    return lane < blocks, jnp.where(lane < blocks, lane, lane - blocks)


def balance_kernel(sum_ref, w_ref, perm_ref, mask_ref, share_ref, log_ref, chosen_ref, entropy_ref):
    blocks = sum_ref.shape[0]
    wide = 2 * blocks
    first, position = lane_tiles(blocks)
    hot = position == perm_ref[...]
    real = mask_ref[...] > 0.0
    logits = jnp.dot(sum_ref[...], w_ref[...], precision=HIGHEST, preferred_element_type=F32)
    for pair in range(logits.shape[1] // wide):
        span = slice(pair * wide, (pair + 1) * wide)
        tile = logits[:, span]
        for step in range(ITERS):
            top = segment_max(tile, first)
            powers = jnp.exp(tile - top)
            total = segment_sum(powers, first)
            tile = tile - (top + jnp.log(total))
            share_ref[2 * step, :, span] = powers * (1.0 / total)
            top = jnp.max(tile, axis=0, keepdims=True)
            powers = jnp.exp(tile - top)
            total = jnp.sum(powers, axis=0, keepdims=True)
            tile = tile - (top + jnp.log(total))
            if step < ITERS - 1:
                share_ref[2 * step + 1, :, span] = powers * (1.0 / total)
        plan = jnp.exp(tile)
        share_ref[2 * ITERS - 1, :, span] = plan
        log_ref[:, span] = tile
        chosen_ref[:, span] = blocks * segment_sum(jnp.where(hot, plan, 0.0), first)
        entropy_ref[:, span] = -jnp.sum(jnp.where(real, plan * tile, 0.0), axis=0, keepdims=True)


def balance(sums, w_sort, perm_column, mask_column):
    blocks, width = sums.shape
    cols = w_sort.shape[1]
    return pl.pallas_call(
        balance_kernel,
        out_shape=[
            shape_of((2 * ITERS, blocks, cols), F32),
            shape_of((blocks, cols), F32),
            shape_of((blocks, cols), F32),
            shape_of((1, cols), F32),
        ],
        compiler_params=params(32),
        name="balance",
    )(sums, w_sort, perm_column, mask_column)


def balance_back_kernel(
    coef_ref, gch_ref, share_ref, log_ref, sum_ref, w_ref, perm_ref, mask_ref, sort_ref, gsum_ref, glog_ref
):
    blocks = sum_ref.shape[0]
    wide = 2 * blocks
    first, position = lane_tiles(blocks)
    hot = position == perm_ref[...]
    weight = coef_ref[0] * mask_ref[...]
    for pair in range(log_ref.shape[1] // wide):
        span = slice(pair * wide, (pair + 1) * wide)
        plan = share_ref[2 * ITERS - 1, :, span]
        gch = segment_sum(gch_ref[:, span], first)
        grad = plan * (jnp.where(hot, blocks * gch, 0.0) - weight * (log_ref[:, span] + 1.0))
        for level in range(2 * ITERS - 1, -1, -1):
            if level % 2:
                total = jnp.sum(grad, axis=0, keepdims=True)
            else:
                total = segment_sum(grad, first)
            grad = grad - share_ref[level, :, span] * total
        glog_ref[:, span] = grad
    glog = glog_ref[...]
    sort_ref[...] = lax.dot_general(
        sum_ref[...], glog, TN, precision=HIGHEST, preferred_element_type=F32
    ).astype(sort_ref.dtype)
    gsum_ref[...] = lax.dot_general(glog, w_ref[...], NT, precision=HIGHEST, preferred_element_type=F32)


def balance_back(coef, gch, shares, plan_log, sums, w_sort, perm_column, mask_column):
    blocks, width = sums.shape
    cols = w_sort.shape[1]
    vmem = pl.BlockSpec(memory_space=pltpu.VMEM)
    return pl.pallas_call(
        balance_back_kernel,
        in_specs=[pl.BlockSpec(memory_space=pltpu.SMEM)] + [vmem] * 7,
        out_specs=[vmem, vmem],
        out_shape=[shape_of((width, cols), BF16), shape_of((blocks, width), F32)],
        scratch_shapes=[pltpu.VMEM((blocks, cols), F32)],
        compiler_params=params(32),
        name="balance_back",
    )(coef, gch, shares, plan_log, sums, w_sort, perm_column, mask_column)


def head_masks(rows):
    lane = lax.broadcasted_iota(jnp.int32, (rows, GROUP_WIDTH), 1)
    return [(lane >= h * HEAD_DIM) & (lane < (h + 1) * HEAD_DIM) for h in range(GROUP)]


def expand(rows, masks):
    zero = jnp.zeros_like(rows)
    return jnp.concatenate([jnp.where(mask, rows, zero) for mask in masks], axis=0)


def fold(rows, masks):
    parts = [rows[h * BLOCK : (h + 1) * BLOCK] for h in range(GROUP)]
    result = parts[GROUP - 1]
    for h in range(GROUP - 1):
        result = jnp.where(masks[h], parts[h], result)
    return result


def attend_kernel(
    perm_ref, mask_ref, q_ref, k_ref, v_ref, chosen_ref, wo_ref, x_ref, gain_ref,
    probs_ref, att_ref, second_ref, act_ref, wo_low_ref,
):
    tile_index = pl.program_id(0)
    rows, width = q_ref.shape
    blocks = rows // BLOCK

    @pl.when(tile_index == 0)
    def _():
        wo_low_ref[...] = wo_ref[...].astype(BF16)

    masks = head_masks(BLOCK)
    key_row = lax.broadcasted_iota(jnp.int32, (BLOCK, GROUP_ROWS), 0)
    query_row = lax.broadcasted_iota(jnp.int32, (BLOCK, GROUP_ROWS), 1) % BLOCK
    causal = key_row <= query_row
    for b in range(blocks):
        block = tile_index * blocks + b
        partner = perm_ref[block]
        usable = (partner < block) & (mask_ref[partner] > 0)
        far_bias = jnp.where(usable, 0.0, -1e30)
        own_at = pl.ds(pl.multiple_of(block * BLOCK, BLOCK), BLOCK)
        far_at = pl.ds(pl.multiple_of(partner * BLOCK, BLOCK), BLOCK)
        here = slice(b * BLOCK, (b + 1) * BLOCK)
        for g in range(width // GROUP_WIDTH):
            lanes = slice(g * GROUP_WIDTH, (g + 1) * GROUP_WIDTH)
            queries = expand(q_ref[here, lanes], masks)
            keys = jnp.concatenate([k_ref[own_at, lanes], k_ref[far_at, lanes]], axis=0)
            scores = dot_nt(keys, queries) * FACTOR
            own = jnp.where(causal, scores[:BLOCK], -1e30)
            far = jnp.where(usable, scores[BLOCK:], -1e30)
            top = jnp.maximum(jnp.max(own, axis=0, keepdims=True), jnp.max(far, axis=0, keepdims=True))
            powers = jnp.exp(jnp.concatenate([own, far], axis=0) - top)
            probs = (powers * (1.0 / jnp.sum(powers, axis=0, keepdims=True))).astype(BF16)
            probs_ref[b * 2 * BLOCK : (b + 1) * 2 * BLOCK, g * GROUP_ROWS : (g + 1) * GROUP_ROWS] = probs
            scaled = (v_ref[far_at, lanes].astype(F32) * chosen_ref[b : b + 1, lanes]).astype(BF16)
            values = jnp.concatenate([v_ref[own_at, lanes], scaled], axis=0)
            att_ref[here, lanes] = fold(dot_tn(probs, values), masks).astype(BF16)
    second = x_ref[...] + dot(att_ref[...], wo_low_ref[...])
    second_ref[...] = second
    unit, _ = normalize(second)
    act_ref[...] = (unit * gain_ref[...]).astype(BF16)


def attend(perm, mask, q, k, v, chosen, w_out, x, gain, tile=256):
    rows, width = q.shape
    blocks = rows // BLOCK
    grid_spec = pltpu.PrefetchScalarGridSpec(
        num_scalar_prefetch=2,
        grid=(rows // tile,),
        in_specs=[
            rows_of(tile, width),
            whole((rows, width)),
            whole((rows, width)),
            rows_of(tile // BLOCK, width),
            whole((width, width)),
            rows_of(tile, width),
            whole((1, width)),
        ],
        out_specs=[
            rows_of(2 * tile, HEADS * BLOCK),
            rows_of(tile, width),
            rows_of(tile, width),
            rows_of(tile, width),
        ],
        scratch_shapes=[pltpu.VMEM((width, width), BF16)],
    )
    return pl.pallas_call(
        attend_kernel,
        grid_spec=grid_spec,
        out_shape=[
            shape_of((2 * rows, HEADS * BLOCK), BF16),
            shape_of((rows, width), BF16),
            shape_of((rows, width), F32),
            shape_of((rows, width), BF16),
        ],
        compiler_params=params(48),
        name="attend",
    )(perm, mask, q, k, v, chosen, w_out, x, gain)


def attend_back_kernel(
    perm_ref, q_ref, gatt_ref, probs_ref, k_ref, v_ref, chosen_ref,
    gq_ref, gk_ref, gv_ref, gch_ref, own_k_ref, far_k_ref, own_v_ref, far_v_ref,
):
    tile_index = pl.program_id(0)
    rows, width = q_ref.shape
    blocks = rows // BLOCK
    masks = head_masks(BLOCK)
    for b in range(blocks):
        block = tile_index * blocks + b
        partner = perm_ref[block]
        own_at = pl.ds(pl.multiple_of(block * BLOCK, BLOCK), BLOCK)
        far_at = pl.ds(pl.multiple_of(partner * BLOCK, BLOCK), BLOCK)
        here = slice(b * BLOCK, (b + 1) * BLOCK)
        for g in range(width // GROUP_WIDTH):
            lanes = slice(g * GROUP_WIDTH, (g + 1) * GROUP_WIDTH)
            queries = expand(q_ref[here, lanes], masks)
            grads = expand(gatt_ref[here, lanes], masks)
            keys = jnp.concatenate([k_ref[own_at, lanes], k_ref[far_at, lanes]], axis=0)
            far_values = v_ref[far_at, lanes].astype(F32)
            chosen = chosen_ref[b : b + 1, lanes]
            values = jnp.concatenate([v_ref[own_at, lanes], (far_values * chosen).astype(BF16)], axis=0)
            probs_low = probs_ref[
                b * 2 * BLOCK : (b + 1) * 2 * BLOCK, g * GROUP_ROWS : (g + 1) * GROUP_ROWS
            ]
            probs = probs_low.astype(F32)
            grad_probs = dot_nt(values, grads)
            total = jnp.sum(probs * grad_probs, axis=0, keepdims=True)
            grad_scores = (probs * (grad_probs - total)).astype(BF16)
            grad_keys = dot(grad_scores, queries) * FACTOR
            grad_values = dot(probs_low, grads)
            gq_ref[here, lanes] = (fold(dot_tn(grad_scores, keys), masks) * FACTOR).astype(BF16)
            far_grad = grad_values[BLOCK:]
            gch_ref[b : b + 1, lanes] = jnp.sum(far_grad * far_values, axis=0, keepdims=True)
            own_k_ref[own_at, lanes] = grad_keys[:BLOCK]
            far_k_ref[far_at, lanes] = grad_keys[BLOCK:]
            own_v_ref[own_at, lanes] = grad_values[:BLOCK]
            far_v_ref[far_at, lanes] = far_grad * chosen

    @pl.when(tile_index == pl.num_programs(0) - 1)
    def _():
        gk_ref[...] = (own_k_ref[...] + far_k_ref[...]).astype(BF16)
        gv_ref[...] = (own_v_ref[...] + far_v_ref[...]).astype(BF16)


def attend_back(perm, q, gatt, probs, k, v, chosen, tile=256):
    rows, width = q.shape
    low = shape_of((rows, width), BF16)
    grid_spec = pltpu.PrefetchScalarGridSpec(
        num_scalar_prefetch=1,
        grid=(rows // tile,),
        in_specs=[
            rows_of(tile, width),
            rows_of(tile, width),
            rows_of(2 * tile, HEADS * BLOCK),
            whole((rows, width)),
            whole((rows, width)),
            rows_of(tile // BLOCK, width),
        ],
        out_specs=[
            rows_of(tile, width),
            whole((rows, width)),
            whole((rows, width)),
            rows_of(tile // BLOCK, width),
        ],
        scratch_shapes=[pltpu.VMEM((rows, width), F32)] * 4,
    )
    return pl.pallas_call(
        attend_back_kernel,
        grid_spec=grid_spec,
        out_shape=[low, low, low, shape_of((rows // BLOCK, width), F32)],
        compiler_params=params(56),
        name="attend_back",
    )(perm, q, gatt, probs, k, v, chosen)


def gelu_pair(up):
    square = up * up
    inner = 0.7978845608028654 * 0.044715
    half = 0.5 + 0.5 * jnp.tanh(up * (0.7978845608028654 + inner * square))
    value = up * half
    slope = half + (2.0 * value) * (1.0 - half) * (0.7978845608028654 + 3.0 * inner * square)
    return value, slope


def feed_kernel(
    act_ref, second_ref, cot_ref, att_ref, up_ref, down_ref, wo_ref, gain_ref,
    out_ref, gsec_ref, gatt_ref, gup_ref, gdown_ref, gout_ref, ggain_ref,
    wo_low_ref, up_acc, down_acc, out_acc, *, chunk
):
    tile_index = pl.program_id(0)

    @pl.when(tile_index == 0)
    def _():
        wo_low_ref[...] = wo_ref[...].astype(BF16)
        up_acc[...] = jnp.zeros_like(up_acc)
        down_acc[...] = jnp.zeros_like(down_acc)
        out_acc[...] = jnp.zeros_like(out_acc)
        ggain_ref[...] = jnp.zeros_like(ggain_ref)

    hidden_units = up_ref.shape[1]
    act = act_ref[...]
    cot = cot_ref[...]
    cot_low = cot.astype(BF16)
    act_turned = act.T
    cot_turned = cot_low.T
    second = second_ref[...]
    output = second
    grad_normed = jnp.zeros_like(second)
    for c in range(hidden_units // chunk):
        span = slice(c * chunk, (c + 1) * chunk)
        value, slope = gelu_pair(dot(act, up_ref[:, span]))
        hidden = value.astype(BF16)
        output = output + dot(hidden, down_ref[span, :])
        grad_up = (dot_nt(cot_low, down_ref[span, :]) * slope).astype(BF16)
        grad_normed = grad_normed + dot_nt(grad_up, up_ref[:, span])
        up_acc[:, span] += dot(act_turned, grad_up)
        down_acc[:, span] += dot(cot_turned, hidden)
    out_ref[...] = output
    unit, inverse = normalize(second)
    ggain_ref[...] += jnp.sum(grad_normed * unit, axis=0, keepdims=True)
    grad_second = cot + norm_grad(grad_normed, unit, inverse, gain_ref[...])
    gsec_ref[...] = grad_second
    second_low = grad_second.astype(BF16)
    gatt_ref[...] = dot_nt(second_low, wo_low_ref[...]).astype(BF16)
    out_acc[...] += dot_tn(att_ref[...], second_low)

    @pl.when(tile_index == pl.num_programs(0) - 1)
    def _():
        gup_ref[...] = up_acc[...].astype(BF16)
        gdown_ref[...] = down_acc[...].astype(BF16)
        gout_ref[...] = out_acc[...].astype(BF16)


def feed(act, second, cot, att, w_up, w_down, w_out, gain, tile=256, chunk=512):
    rows, width = act.shape
    units = w_up.shape[1]
    return pl.pallas_call(
        functools.partial(feed_kernel, chunk=chunk),
        grid=(rows // tile,),
        in_specs=[rows_of(tile, width)] * 4
        + [whole((width, units)), whole((units, width)), whole((width, width)), whole((1, width))],
        out_specs=[rows_of(tile, width)] * 3
        + [whole((width, units)), whole((width, units)), whole((width, width)), whole((1, width))],
        out_shape=[
            shape_of((rows, width), F32),
            shape_of((rows, width), F32),
            shape_of((rows, width), BF16),
            shape_of((width, units), BF16),
            shape_of((width, units), BF16),
            shape_of((width, width), BF16),
            shape_of((1, width), F32),
        ],
        scratch_shapes=[
            pltpu.VMEM((width, width), BF16),
            pltpu.VMEM((width, units), F32),
            pltpu.VMEM((width, units), F32),
            pltpu.VMEM((width, width), F32),
        ],
        compiler_params=params(60),
        cost_estimate=pl.CostEstimate(flops=12 * rows * width * units, bytes_accessed=30 * MIB, transcendentals=0),
        name="feed",
    )(act, second, cot, att, w_up, w_down, w_out, gain)


def weight_kernel(act_ref, gq_ref, gk_ref, gv_ref, out_ref, acc_ref):
    @pl.when(pl.program_id(0) == 0)
    def _():
        acc_ref[...] = jnp.zeros_like(acc_ref)

    turned = act_ref[...].T
    for which, ref in enumerate((gq_ref, gk_ref, gv_ref)):
        acc_ref[which] += dot(turned, ref[...])

    @pl.when(pl.program_id(0) == pl.num_programs(0) - 1)
    def _():
        out_ref[...] = acc_ref[...].astype(BF16)


def weight_grads(act, gq, gk, gv, tile=512):
    rows, width = act.shape
    cols = gq.shape[1]
    return pl.pallas_call(
        weight_kernel,
        grid=(rows // tile,),
        in_specs=[rows_of(tile, width)] + [rows_of(tile, cols)] * 3,
        out_specs=whole((3, width, cols)),
        out_shape=shape_of((3, width, cols), BF16),
        scratch_shapes=[pltpu.VMEM((3, width, cols), F32)],
        compiler_params=params(32),
        cost_estimate=pl.CostEstimate(flops=6 * rows * width * cols, bytes_accessed=10 * MIB, transcendentals=0),
        name="weight_grads",
    )(act, gq, gk, gv)


def input_kernel(
    gq_ref, gk_ref, gv_ref, gsum_ref, x_ref, gsec_ref, gain_ref, wq_ref, wk_ref, wv_ref, out_ref, w_ref
):
    @pl.when(pl.program_id(0) == 0)
    def _():
        for which, ref in enumerate((wq_ref, wk_ref, wv_ref)):
            w_ref[which] = ref[...].astype(BF16)

    rows, width = x_ref.shape
    grad = dot_nt(gq_ref[...], w_ref[0]) + dot_nt(gk_ref[...], w_ref[1]) + dot_nt(gv_ref[...], w_ref[2])
    grad = (grad.reshape(rows // BLOCK, BLOCK, width) + gsum_ref[...][:, None, :]).reshape(rows, width)
    unit, inverse = normalize(x_ref[...])
    out_ref[...] = gsec_ref[...] + norm_grad(grad, unit, inverse, gain_ref[...])


def input_grad(gq, gk, gv, gsum, x, gsec, gain, wq, wk, wv, tile=256):
    rows, width = x.shape
    return pl.pallas_call(
        input_kernel,
        grid=(rows // tile,),
        in_specs=[rows_of(tile, width)] * 3
        + [rows_of(tile // BLOCK, width)]
        + [rows_of(tile, width)] * 2
        + [whole((1, width))]
        + [whole((width, width))] * 3,
        out_specs=rows_of(tile, width),
        out_shape=shape_of((rows, width), F32),
        scratch_shapes=[pltpu.VMEM((3, width, width), BF16)],
        compiler_params=params(48),
        cost_estimate=pl.CostEstimate(flops=6 * rows * width * width, bytes_accessed=21 * MIB, transcendentals=0),
        name="input_grad",
    )(gq, gk, gv, gsum, x, gsec, gain, wq, wk, wv)


def local(
    inputs, cotangent, block_perm, block_mask, pen_weight, w_query, w_key, w_value, w_out, w_sort,
    gain_one, gain_two, w_up, w_down,
):
    both = ("batch", "mp")
    _, rows, width = inputs.shape
    x = inputs.reshape(rows, width)
    cot = cotangent.reshape(rows, width)
    perm = block_perm.reshape(-1)
    mask = block_mask.reshape(-1)
    perm_column = perm.reshape(-1, 1)
    mask_column = mask.reshape(-1, 1).astype(F32)
    gain_one_row = gain_one.reshape(1, width)
    gain_two_row = gain_two.reshape(1, width)
    block_total = lax.psum(jnp.sum(mask.astype(F32)), both)
    up_all = lax.all_gather(w_up.astype(BF16), "mp", axis=1, tiled=True)
    down_all = lax.all_gather(w_down.astype(BF16), "mp", axis=0, tiled=True)
    act_one, q, k, v, sums = project(x, gain_one_row, w_query, w_key, w_value)
    shares, plan_log, chosen, entropy = balance(sums, w_sort, perm_column, mask_column)
    probs, att, second, act_two = attend(perm, mask, q, k, v, chosen, w_out, x, gain_two_row)
    output, grad_second, grad_att, up_part, down_part, out_part, gain_two_part = feed(
        act_two, second, cot, att, up_all, down_all, w_out, gain_two_row
    )
    gq, gk, gv, gch = attend_back(perm, q, grad_att, probs, k, v, chosen)
    coef = (pen_weight[0] / (HEADS * block_total)).reshape(1)
    sort_part, grad_sums = balance_back(coef, gch, shares, plan_log, sums, w_sort, perm_column, mask_column)
    joined_part = weight_grads(act_one, gq, gk, gv)
    grad_input = input_grad(gq, gk, gv, grad_sums, x, grad_second, gain_one_row, w_query, w_key, w_value)
    up_sum = lax.psum(lax.psum_scatter(up_part, "mp", scatter_dimension=1, tiled=True), "batch")
    down_sum = lax.psum(lax.psum_scatter(down_part, "mp", scatter_dimension=1, tiled=True), "batch")
    joined, grad_out, grad_sort = lax.psum((joined_part, out_part, sort_part), both)
    grad_gain_two, entropy_all = lax.psum((gain_two_part, entropy), both)
    joined = joined.astype(F32)
    grad_sort = grad_sort.astype(F32)
    grad_gain_one = (
        jnp.sum(joined[0] * w_query, axis=1)
        + jnp.sum(joined[1] * w_key, axis=1)
        + jnp.sum(joined[2] * w_value, axis=1)
        + jnp.sum(grad_sort * w_sort, axis=1)
    ) / gain_one
    return (
        output.reshape(inputs.shape),
        (jnp.sum(entropy_all) / (HEADS * block_total)).reshape(1),
        grad_input.reshape(inputs.shape),
        joined[0],
        joined[1],
        joined[2],
        grad_out.astype(F32),
        grad_sort,
        grad_gain_one,
        grad_gain_two.reshape(width),
        up_sum.astype(F32),
        down_sum.T.astype(F32),
    )


def solution(mesh):
    tokens = P(("batch", "mp"), None, None)
    blocks = P(("batch", "mp"), None)
    return jax.shard_map(
        local,
        mesh=mesh,
        in_specs=(tokens, tokens, blocks, blocks) + (P(),) * 8 + (P(None, "mp"), P("mp", None)),
        out_specs=(tokens, P(), tokens) + (P(),) * 7 + (P(None, "mp"), P("mp", None)),
        check_vma=False,
    )
```

```python
import functools

import jax
import jax.numpy as jnp
from jax import lax
from jax.experimental import pallas as pl
from jax.experimental.pallas import tpu as pltpu
from jax.sharding import PartitionSpec as P

HEADS = 8
HEAD_DIM = 64
BLOCK = 32
ITERS = 8
GROUP = 4
GROUP_WIDTH = GROUP * HEAD_DIM
GROUP_ROWS = GROUP * BLOCK
EPSILON = 1e-05
FACTOR = HEAD_DIM ** (-0.5)
HIGHEST = lax.Precision.HIGHEST
F32 = jnp.float32
BF16 = jnp.bfloat16
NT = (((1,), (1,)), ((), ()))
TN = (((0,), (0,)), ((), ()))
MIB = 1024 * 1024
LANES = 128


def dot(left, right):
    return jnp.dot(left, right, preferred_element_type=F32)


def dot_nt(left, right):
    return lax.dot_general(left, right, NT, preferred_element_type=F32)


def dot_tn(left, right):
    return lax.dot_general(left, right, TN, preferred_element_type=F32)


def shape_of(dims, dtype):
    return jax.ShapeDtypeStruct(dims, dtype)


def whole(dims):
    return pl.BlockSpec(dims, lambda *_: (0,) * len(dims))


def once(dims):
    return pl.BlockSpec(dims, lambda *_: (0,) * len(dims), pipeline_mode=pl.Buffered(1))


def rows_of(size, width):
    return pl.BlockSpec((size, width), lambda step, *_: (step, 0))


def params(mib):
    return pltpu.CompilerParams(vmem_limit_bytes=mib * MIB)


def far(array):
    return pltpu.with_memory_space_constraint(array, pltpu.HBM)


def near(array):
    return pltpu.with_memory_space_constraint(array, pltpu.VMEM)


def near_shape(dims, dtype):
    return pltpu.VMEM(dims, dtype)


def far_shape(dims, dtype):
    return pltpu.HBM(dims, dtype)


def cost(wide):
    return pl.CostEstimate(flops=100000000000 if wide else 1000000, bytes_accessed=0, transcendentals=0)


def normalize(values):
    center = values - jnp.mean(values, axis=-1, keepdims=True)
    inverse = lax.rsqrt(jnp.mean(center * center, axis=-1, keepdims=True) + EPSILON)
    return center * inverse, inverse


def norm_grad(grad_rows, unit_rows, inverse, gain):
    scaled_rows = grad_rows * gain
    return inverse * (
        scaled_rows
        - jnp.mean(scaled_rows, axis=-1, keepdims=True)
        - unit_rows * jnp.mean(scaled_rows * unit_rows, axis=-1, keepdims=True)
    )


def segment_sum(tile, first):
    left = jnp.sum(jnp.where(first, tile, 0.0), axis=1, keepdims=True)
    right = jnp.sum(jnp.where(first, 0.0, tile), axis=1, keepdims=True)
    return jnp.where(first, left, right)


def segment_max(tile, first):
    left = jnp.max(jnp.where(first, tile, -jnp.inf), axis=1, keepdims=True)
    right = jnp.max(jnp.where(first, -jnp.inf, tile), axis=1, keepdims=True)
    return jnp.where(first, left, right)


def head_masks(rows):
    lane = lax.broadcasted_iota(jnp.int32, (rows, GROUP_WIDTH), 1)
    return [(lane >= h * HEAD_DIM) & (lane < (h + 1) * HEAD_DIM) for h in range(GROUP)]


def expand(rows, masks):
    zero = jnp.zeros_like(rows)
    return jnp.concatenate([jnp.where(mask, rows, zero) for mask in masks], axis=0)


def fold(rows, masks):
    parts = [rows[h * BLOCK : (h + 1) * BLOCK] for h in range(GROUP)]
    result = parts[GROUP - 1]
    for h in range(GROUP - 1):
        result = jnp.where(masks[h], parts[h], result)
    return result


def lane_tiles(blocks):
    lane = lax.broadcasted_iota(jnp.int32, (blocks, 2 * blocks), 1)
    return lane < blocks, jnp.where(lane < blocks, lane, lane - blocks).astype(F32)


def down_rows(row, wide):
    return jnp.broadcast_to(row.astype(F32), (wide, row.shape[1])).T


def balance_plans(logits, perm_row, mask_row, share_ref, log_ref, chosen_ref, entropy_ref):
    blocks = logits.shape[0]
    wide = 2 * blocks
    first, position = lane_tiles(blocks)
    hot = position == down_rows(perm_row, wide)
    real = down_rows(mask_row, wide) > 0.0
    for pair in range(logits.shape[1] // wide):
        span = slice(pair * wide, (pair + 1) * wide)
        tile = logits[:, span]
        for step in range(ITERS):
            top = segment_max(tile, first)
            powers = jnp.exp(tile - top)
            total = segment_sum(powers, first)
            tile = tile - (top + jnp.log(total))
            share_ref[2 * step, :, span] = powers * (1.0 / total)
            top = jnp.max(tile, axis=0, keepdims=True)
            powers = jnp.exp(tile - top)
            total = jnp.sum(powers, axis=0, keepdims=True)
            tile = tile - (top + jnp.log(total))
            if step < ITERS - 1:
                share_ref[2 * step + 1, :, span] = powers * (1.0 / total)
        plan = jnp.exp(tile)
        share_ref[2 * ITERS - 1, :, span] = plan
        log_ref[:, span] = tile
        chosen_ref[:, span] = blocks * segment_sum(jnp.where(hot, plan, 0.0), first)
        entropy_ref[:, span] = -jnp.sum(jnp.where(real, plan * tile, 0.0), axis=0, keepdims=True)


def forward_kernel(
    perm_ref, mask_ref, perm_row_ref, mask_row_ref, gain_one_ref, gain_two_ref,
    x_far, wq_far, wk_far, wv_far, ws_far, wo_far,
    act_far, q_far, k_far, v_far, probs_far, att_far, second_far, share_far,
    act_two_ref, sum_ref, log_ref, chosen_ref, entropy_ref,
    x_ref, w_ref, w_low_ref, wo_low_ref, act_ref, q_ref, k_ref, v_ref, probs_ref, att_ref, second_ref, share_ref,
    in_sem, out_sem, share_sem, *, tile,
):
    rows, width = x_ref.shape
    tiles = rows // tile

    def x_copy(i):
        at = pl.ds(pl.multiple_of(i * tile, tile), tile)
        return pltpu.make_async_copy(x_far.at[at, :], x_ref.at[at, :], in_sem.at[i])

    def w_copy(n):
        far_ref = (wq_far, wk_far, wv_far, ws_far, wo_far)[n]
        return pltpu.make_async_copy(far_ref, w_ref.at[n], in_sem.at[tiles + n])

    outs = (
        (act_ref, act_far), (q_ref, q_far), (k_ref, k_far), (v_ref, v_far),
        (probs_ref, probs_far), (att_ref, att_far), (second_ref, second_far),
    )

    def out_copy(n, i):
        near_ref, far_ref = outs[n]
        size = near_ref.shape[0] // tiles
        at = pl.ds(pl.multiple_of(i * size, size), size)
        return pltpu.make_async_copy(near_ref.at[at, :], far_ref.at[at, :], out_sem.at[n, i])

    x_copy(0).start()
    for n in range(3):
        w_copy(n).start()
    for i in range(1, tiles):
        x_copy(i).start()
    w_copy(3).start()
    w_copy(4).start()
    for n in range(3):
        w_copy(n).wait()
        w_low_ref[:, n * width : (n + 1) * width] = w_ref[n].astype(BF16)

    def project(i, _):
        x_copy(i).wait()
        at = pl.ds(pl.multiple_of(i * tile, tile), tile)
        unit, _ = normalize(x_ref[at, :])
        act = (unit * gain_one_ref[...]).astype(BF16)
        act_ref[at, :] = act
        for n, ref in enumerate((q_ref, k_ref, v_ref)):
            ref[at, :] = dot(act, w_low_ref[:, n * width : (n + 1) * width]).astype(BF16)
        sums = jnp.sum(act.astype(F32).reshape(tile // BLOCK, BLOCK, width), axis=1)
        some = tile // BLOCK
        sum_ref[pl.ds(pl.multiple_of(i * some, some), some), :] = sums.astype(BF16).astype(F32)
        for n in range(4):
            out_copy(n, i).start()
        return 0

    lax.fori_loop(0, tiles, project, 0)
    w_copy(3).wait()
    w_copy(4).wait()
    wo_low_ref[...] = w_ref[4].astype(BF16)
    logits = jnp.dot(sum_ref[...], w_ref[3], precision=HIGHEST, preferred_element_type=F32)
    balance_plans(
        logits, perm_row_ref[...], mask_row_ref[...], share_ref, log_ref, chosen_ref, entropy_ref
    )
    pltpu.make_async_copy(share_ref, share_far, share_sem).start()

    masks = head_masks(BLOCK)
    key_row = lax.broadcasted_iota(jnp.int32, (BLOCK, GROUP_ROWS), 0)
    query_row = lax.broadcasted_iota(jnp.int32, (BLOCK, GROUP_ROWS), 1) % BLOCK
    causal = key_row <= query_row
    part = 8

    def attend(j, _):
        for b in range(part):
            block = j * part + b
            partner = perm_ref[block]
            usable = (partner < block) & (mask_ref[partner] > 0)
            own_at = pl.ds(pl.multiple_of(block * BLOCK, BLOCK), BLOCK)
            far_at = pl.ds(pl.multiple_of(partner * BLOCK, BLOCK), BLOCK)
            probs_at = pl.ds(pl.multiple_of(block * 2 * BLOCK, 2 * BLOCK), 2 * BLOCK)
            chosen_row = chosen_ref[pl.ds(block, 1), :]
            for g in range(width // GROUP_WIDTH):
                lanes = slice(g * GROUP_WIDTH, (g + 1) * GROUP_WIDTH)
                queries = expand(q_ref[own_at, lanes], masks)
                keys = jnp.concatenate([k_ref[own_at, lanes], k_ref[far_at, lanes]], axis=0)
                scores = dot_nt(keys, queries) * FACTOR
                own = jnp.where(causal, scores[:BLOCK], -1e30)
                far = jnp.where(usable, scores[BLOCK:], -1e30)
                top = jnp.maximum(jnp.max(own, axis=0, keepdims=True), jnp.max(far, axis=0, keepdims=True))
                powers = jnp.exp(jnp.concatenate([own, far], axis=0) - top)
                probs = (powers * (1.0 / jnp.sum(powers, axis=0, keepdims=True))).astype(BF16)
                probs_ref[probs_at, g * GROUP_ROWS : (g + 1) * GROUP_ROWS] = probs
                scaled = (v_ref[far_at, lanes].astype(F32) * chosen_row[:, lanes]).astype(BF16)
                values = jnp.concatenate([v_ref[own_at, lanes], scaled], axis=0)
                att_ref[own_at, lanes] = fold(dot_tn(probs, values), masks).astype(BF16)
        return 0

    def finish_tile(i, _):
        per = tile // BLOCK // part
        lax.fori_loop(i * per, (i + 1) * per, attend, 0)
        at = pl.ds(pl.multiple_of(i * tile, tile), tile)
        second = x_ref[at, :] + dot(att_ref[at, :], wo_low_ref[...])
        second_ref[at, :] = second
        unit, _ = normalize(second)
        act_two_ref[at, :] = (unit * gain_two_ref[...]).astype(BF16)
        for n in range(4, 7):
            out_copy(n, i).start()
        return 0

    lax.fori_loop(0, tiles, finish_tile, 0)
    for n in range(7):
        for i in range(tiles):
            out_copy(n, i).wait()
    pltpu.make_async_copy(share_ref, share_far, share_sem).wait()


def forward(perm, mask, perm_row, mask_row, gain_one, gain_two, x, wq, wk, wv, ws, wo, tile=512):
    rows, width = x.shape
    blocks = rows // BLOCK
    tiles = rows // tile
    smem = pl.BlockSpec(memory_space=pltpu.SMEM)
    vmem = pl.BlockSpec(memory_space=pltpu.VMEM)
    hbm = pl.BlockSpec(memory_space=pltpu.HBM)
    low = ((rows, width), BF16)
    probs = ((2 * rows, HEADS * BLOCK), BF16)
    full = ((rows, width), F32)
    share = ((2 * ITERS, blocks, width), F32)
    plan = ((blocks, width), F32)
    return pl.pallas_call(
        functools.partial(forward_kernel, tile=tile),
        in_specs=[smem] * 2 + [vmem] * 4 + [hbm] * 6,
        out_specs=[hbm] * 8 + [vmem] * 5,
        out_shape=[far_shape(*s) for s in (low, low, low, low, probs, low, full, share)]
        + [near_shape(*s) for s in (low, plan, plan, plan, ((1, width), F32))],
        scratch_shapes=[pltpu.VMEM(*full), pltpu.VMEM((5, width, width), F32), pltpu.VMEM((width, 3 * width), BF16)]
        + [pltpu.VMEM((width, width), BF16)]
        + [pltpu.VMEM(*s) for s in (low, low, low, low, probs, low, full, share)]
        + [
            pltpu.SemaphoreType.DMA((tiles + 5,)),
            pltpu.SemaphoreType.DMA((7, tiles)),
            pltpu.SemaphoreType.DMA,
        ],
        compiler_params=params(44),
        cost_estimate=cost(True),
        name="forward",
    )(perm, mask, perm_row, mask_row, gain_one, gain_two, far(x), far(wq), far(wk), far(wv), far(ws), far(wo))


def attend_back_kernel(
    perm_ref, q_ref, gatt_ref, probs_ref, k_ref, v_ref, chosen_ref,
    gq_ref, gk_ref, gv_ref, gch_ref, own_k_ref, far_k_ref, own_v_ref, far_v_ref,
):
    tile_index = pl.program_id(0)
    rows = q_ref.shape[0]
    blocks = rows // BLOCK
    masks = head_masks(BLOCK)
    for b in range(blocks):
        block = tile_index * blocks + b
        partner = perm_ref[block]
        own_at = pl.ds(pl.multiple_of(block * BLOCK, BLOCK), BLOCK)
        far_at = pl.ds(pl.multiple_of(partner * BLOCK, BLOCK), BLOCK)
        here = slice(b * BLOCK, (b + 1) * BLOCK)
        queries = expand(q_ref[here, :], masks)
        grads = expand(gatt_ref[here, :], masks)
        keys = jnp.concatenate([k_ref[own_at, :], k_ref[far_at, :]], axis=0)
        far_values = v_ref[far_at, :].astype(F32)
        chosen = chosen_ref[b : b + 1, :]
        values = jnp.concatenate([v_ref[own_at, :], (far_values * chosen).astype(BF16)], axis=0)
        probs_low = probs_ref[b * 2 * BLOCK : (b + 1) * 2 * BLOCK, :]
        probs = probs_low.astype(F32)
        grad_probs = dot_nt(values, grads)
        total = jnp.sum(probs * grad_probs, axis=0, keepdims=True)
        grad_scores = (probs * (grad_probs - total)).astype(BF16)
        grad_keys = dot(grad_scores, queries) * FACTOR
        grad_values = dot(probs_low, grads)
        gq_ref[here, :] = (fold(dot_tn(grad_scores, keys), masks) * FACTOR).astype(BF16)
        far_grad = grad_values[BLOCK:]
        gch_ref[b : b + 1, :] = jnp.sum(far_grad * far_values, axis=0, keepdims=True)
        own_k_ref[own_at, :] = grad_keys[:BLOCK]
        far_k_ref[far_at, :] = grad_keys[BLOCK:]
        own_v_ref[own_at, :] = grad_values[:BLOCK]
        far_v_ref[far_at, :] = far_grad * chosen

    @pl.when(tile_index == pl.num_programs(0) - 1)
    def _():
        gk_ref[...] = (own_k_ref[...] + far_k_ref[...]).astype(BF16)
        gv_ref[...] = (own_v_ref[...] + far_v_ref[...]).astype(BF16)


def attend_back(perm, q, gatt, probs, k, v, chosen, group, tile=256):
    rows, width = q.shape
    low = near_shape((rows, GROUP_WIDTH), BF16)

    def lanes(size, cols):
        return pl.BlockSpec((size, cols), lambda step, *_: (step, group))

    full = pl.BlockSpec((rows, GROUP_WIDTH), lambda step, *_: (0, group), pipeline_mode=pl.Buffered(1))
    grid_spec = pltpu.PrefetchScalarGridSpec(
        num_scalar_prefetch=1,
        grid=(rows // tile,),
        in_specs=[
            lanes(tile, GROUP_WIDTH),
            lanes(tile, GROUP_WIDTH),
            lanes(2 * tile, GROUP_ROWS),
            full,
            full,
            lanes(tile // BLOCK, GROUP_WIDTH),
        ],
        out_specs=[
            rows_of(tile, GROUP_WIDTH),
            whole((rows, GROUP_WIDTH)),
            whole((rows, GROUP_WIDTH)),
            rows_of(tile // BLOCK, GROUP_WIDTH),
        ],
        scratch_shapes=[pltpu.VMEM((rows, GROUP_WIDTH), F32)] * 4,
    )
    return pl.pallas_call(
        attend_back_kernel,
        grid_spec=grid_spec,
        out_shape=[low, low, low, shape_of((rows // BLOCK, GROUP_WIDTH), F32)],
        compiler_params=params(20),
        cost_estimate=cost(group > 0),
        name="attend_back",
    )(perm, near(q), near(gatt), near(probs), near(k), near(v), near(chosen))


def gelu_pair(up):
    square = up * up
    inner = 0.7978845608028654 * 0.044715
    half = 0.5 + 0.5 * jnp.tanh(up * (0.7978845608028654 + inner * square))
    value = up * half
    slope = half + (2.0 * value) * (1.0 - half) * (0.7978845608028654 + 3.0 * inner * square)
    return value, slope


def spread(out_ref, acc_ref, where, lanes):
    chunks, size = out_ref.shape[0], out_ref.shape[-2]
    for r in range(chunks):
        at = pl.multiple_of((r ^ where) * size, size)
        out_ref[r, :, lanes] = acc_ref[pl.ds(at, size), :].astype(out_ref.dtype)


def quarter_math(act, cot_low, weights_ref, hidden_ref, up_acc, down_acc):
    value, slope = gelu_pair(dot(act, weights_ref[0]))
    hidden = value.astype(BF16)
    hidden_ref[...] = hidden
    grad_up = (dot_nt(cot_low, weights_ref[1]) * slope).astype(BF16)
    up_acc[...] += dot_tn(act, grad_up)
    down_acc[...] += dot_tn(cot_low, hidden)
    return dot_nt(grad_up, weights_ref[0])


def first_quarter_kernel(
    where_ref, act_ref, cot_ref, weights_ref,
    low_ref, grad_ref, hidden_ref, piece_ref, up_acc, down_acc,
):
    @pl.when(pl.program_id(0) == 0)
    def _():
        up_acc[...] = jnp.zeros_like(up_acc)
        down_acc[...] = jnp.zeros_like(down_acc)

    cot_low = cot_ref[...].astype(BF16)
    low_ref[...] = cot_low
    grad_ref[...] = quarter_math(act_ref[...], cot_low, weights_ref, hidden_ref, up_acc, down_acc)

    @pl.when(pl.program_id(0) == pl.num_programs(0) - 1)
    def _():
        spread(piece_ref.at[:, 0], up_acc, where_ref[0], slice(None))
        spread(piece_ref.at[:, 1], down_acc, where_ref[0], slice(None))


def quarter_kernel(
    where_ref, act_ref, cot_ref, weights_ref, sofar_ref,
    grad_ref, hidden_ref, piece_ref, up_acc, down_acc,
):
    @pl.when(pl.program_id(0) == 0)
    def _():
        up_acc[...] = jnp.zeros_like(up_acc)
        down_acc[...] = jnp.zeros_like(down_acc)

    grad_ref[...] = sofar_ref[...] + quarter_math(
        act_ref[...], cot_ref[...], weights_ref, hidden_ref, up_acc, down_acc
    )

    @pl.when(pl.program_id(0) == pl.num_programs(0) - 1)
    def _():
        spread(piece_ref.at[:, 0], up_acc, where_ref[0], slice(None))
        spread(piece_ref.at[:, 1], down_acc, where_ref[0], slice(None))


def settle_kernel(
    where_ref, grad_ref, cot_ref, second_ref, att_ref, wo_ref, gain_ref, entropy_ref,
    gsec_ref, gatt_ref, gout_ref, out_acc, gain_acc, column_ref, wo_low_ref,
):
    width = grad_ref.shape[1]

    @pl.when(pl.program_id(0) == 0)
    def _():
        out_acc[...] = jnp.zeros_like(out_acc)
        gain_acc[...] = jnp.zeros_like(gain_acc)
        wo_low_ref[...] = wo_ref[...].astype(BF16)

    grad_normed = grad_ref[...]
    unit, inverse = normalize(second_ref[...])
    gain_acc[...] += jnp.sum(grad_normed * unit, axis=0, keepdims=True)
    grad_second = cot_ref[...] + norm_grad(grad_normed, unit, inverse, gain_ref[...])
    gsec_ref[...] = grad_second
    second_low = grad_second.astype(BF16)
    gatt_ref[...] = dot_nt(second_low, wo_low_ref[...]).astype(BF16)
    out_acc[...] += dot_tn(att_ref[...], second_low)

    @pl.when(pl.program_id(0) == pl.num_programs(0) - 1)
    def _():
        spread(gout_ref, out_acc, where_ref[2], slice(0, width))
        half = (LANES // 2, width)
        column_ref[...] = jnp.concatenate(
            [jnp.broadcast_to(gain_acc[...], half), jnp.broadcast_to(entropy_ref[...], half)], axis=0
        ).T
        spread(gout_ref, column_ref, where_ref[2], slice(width, width + LANES))


def settle(where, grad, cot, second, att, w_out, gain, entropy, out_chunks, tile=512):
    rows, width = grad.shape
    out_piece = (out_chunks, width // out_chunks, width + LANES)
    return pl.pallas_call(
        settle_kernel,
        grid_spec=pltpu.PrefetchScalarGridSpec(
            num_scalar_prefetch=1,
            grid=(rows // tile,),
            in_specs=[rows_of(tile, width)] * 4
            + [pl.BlockSpec((width, width), lambda *_: (0, 0), pipeline_mode=pl.Buffered(1))]
            + [whole((1, width))] * 2,
            out_specs=[rows_of(tile, width)] * 2 + [whole(out_piece)],
            scratch_shapes=[
                pltpu.VMEM((width, width), F32),
                pltpu.VMEM((1, width), F32),
                pltpu.VMEM((width, LANES), F32),
                pltpu.VMEM((width, width), BF16),
            ],
        ),
        out_shape=[far_shape((rows, width), F32), near_shape((rows, width), BF16), near_shape(out_piece, BF16)],
        compiler_params=params(20),
        cost_estimate=cost(False),
        name="settle",
    )(where, near(grad), near(cot), near(second), near(att), far(w_out), gain, entropy)


def feed_quarter(where, act, cot, weights, sofar, row_chunks, tile=512):
    rows, width = act.shape
    units = weights.shape[2]
    resident = pl.BlockSpec(weights.shape, lambda *_: (0, 0, 0), pipeline_mode=pl.Buffered(1))
    piece = (row_chunks, 2, width // row_chunks, units)
    in_specs = [rows_of(tile, width), rows_of(tile, width), resident]
    out_shape = [near_shape((rows, width), F32), far_shape((rows, units), BF16)] + [near_shape(piece, BF16)]
    out_specs = [rows_of(tile, width), rows_of(tile, units), whole(piece)]
    aliases = {}
    if sofar is None:
        kernel, operands = first_quarter_kernel, (near(act), near(cot), near(weights))
        out_shape = [near_shape((rows, width), BF16)] + out_shape
        out_specs = [rows_of(tile, width)] + out_specs
    else:
        kernel, operands = quarter_kernel, (near(act), near(cot), near(weights), near(sofar))
        in_specs = in_specs + [rows_of(tile, width)]
    return pl.pallas_call(
        kernel,
        grid_spec=pltpu.PrefetchScalarGridSpec(
            num_scalar_prefetch=1,
            grid=(rows // tile,),
            in_specs=in_specs,
            out_specs=out_specs,
            scratch_shapes=[pltpu.VMEM((width, units), F32)] * 2,
        ),
        out_shape=out_shape,
        input_output_aliases=aliases,
        compiler_params=params(18),
        cost_estimate=cost(True),
        name="feed_quarter",
    )(where, *operands)


def output_kernel(second_ref, *refs):
    out_ref = refs[-1]
    count = (len(refs) - 1) // 2
    total = second_ref[...]
    for hidden_ref, weights_ref in zip(refs[:count], refs[count : 2 * count]):
        total = total + dot(hidden_ref[...], weights_ref[0])
    out_ref[...] = total


def layer_output(second, hidden, weights, tile=512):
    rows, width = second.shape
    units = hidden[0].shape[1]
    down = pl.BlockSpec((1, units, width), lambda *_: (1, 0, 0), pipeline_mode=pl.Buffered(1))
    return pl.pallas_call(
        output_kernel,
        grid=(rows // tile,),
        in_specs=[rows_of(tile, width)] + [rows_of(tile, units)] * len(hidden) + [down] * len(hidden),
        out_specs=rows_of(tile, width),
        out_shape=far_shape((rows, width), F32),
        compiler_params=params(16),
        cost_estimate=cost(True),
        name="layer_output",
    )(near(second), *[far(array) for array in hidden], *[near(array) for array in weights])


def group_kernel(
    where_ref, coef_ref, act_ref, gq_ref, gk_ref, gv_ref,
    gch_ref, share_ref, log_ref, sum_ref, w_ref, perm_ref, mask_ref, extra_ref,
    piece_ref, gsum_ref, glog_ref, acc_ref, *, leading,
):
    blocks = sum_ref.shape[0]
    cols = gq_ref.shape[1]
    wide = 2 * blocks
    first, position = lane_tiles(blocks)
    hot = position == down_rows(perm_ref[...], wide)
    weight = coef_ref[0] * down_rows(mask_ref[...], wide)
    for pair in range(cols // wide):
        span = slice(pair * wide, (pair + 1) * wide)
        plan = share_ref[2 * ITERS - 1, :, span]
        gch = segment_sum(gch_ref[:, span], first)
        grad = plan * (jnp.where(hot, blocks * gch, 0.0) - weight * (log_ref[:, span] + 1.0))
        for level in range(2 * ITERS - 1, -1, -1):
            if level % 2:
                total = jnp.sum(grad, axis=0, keepdims=True)
            else:
                total = segment_sum(grad, first)
            grad = grad - share_ref[level, :, span] * total
        glog_ref[:, span] = grad
    act = act_ref[...]
    for index, ref in enumerate((gq_ref, gk_ref, gv_ref)):
        acc_ref[...] = dot_tn(act, ref[...])
        spread(piece_ref, acc_ref, where_ref[2], slice(index * cols, (index + 1) * cols))
    glog = glog_ref[...]
    acc_ref[...] = lax.dot_general(sum_ref[...], glog, TN, precision=HIGHEST, preferred_element_type=F32)
    spread(piece_ref, acc_ref, where_ref[2], slice(3 * cols, 4 * cols))
    gsum = lax.dot_general(glog, w_ref[...], NT, precision=HIGHEST, preferred_element_type=F32)
    if leading:
        piece_ref[:, :, 4 * cols :] = extra_ref[...]
    else:
        gsum = gsum + extra_ref[...]
    gsum_ref[...] = gsum


def group_grads(
    where, coef, act, gq, gk, gv, gch, shares, plan_log, sums, w_sort, perm_row, mask_row, extra, group, chunks
):
    rows, width = act.shape
    blocks = sums.shape[0]
    cols = gq.shape[1]
    smem = pl.BlockSpec(memory_space=pltpu.SMEM)
    one = pl.Buffered(1)

    def full(array):
        return pl.BlockSpec(array.shape, lambda *_: (0,) * array.ndim, pipeline_mode=one)

    def lanes(array):
        return pl.BlockSpec(
            array.shape[:-1] + (cols,), lambda *_: (0,) * (array.ndim - 1) + (group,), pipeline_mode=one
        )

    leading = group == 0
    piece = (chunks, width // chunks, 4 * cols + (extra.shape[2] if leading else 0))
    return pl.pallas_call(
        functools.partial(group_kernel, leading=leading),
        grid=(1,),
        in_specs=[smem, smem, full(act), full(gq), full(gk), full(gv), full(gch), lanes(shares), lanes(plan_log)]
        + [full(sums), lanes(w_sort), full(perm_row), full(mask_row), full(extra)],
        out_specs=[whole(piece), whole((blocks, width))],
        out_shape=[near_shape(piece, BF16), near_shape((blocks, width), F32)],
        scratch_shapes=[pltpu.VMEM((blocks, cols), F32), pltpu.VMEM((width, cols), F32)],
        compiler_params=params(16),
        cost_estimate=cost(group > 0),
        name="group_grads",
    )(
        where, coef, near(act), near(gq), near(gk), near(gv), gch, near(shares), near(plan_log), sums, far(w_sort),
        perm_row, mask_row, extra,
    )


def input_kernel(*refs):
    count = (len(refs) - 9) // 3
    groups = [refs[3 * g : 3 * g + 3] for g in range(count)]
    gsum_ref, x_ref, gsec_ref, gain_ref, wq_ref, wk_ref, wv_ref, out_ref, w_ref = refs[3 * count :]

    @pl.when(pl.program_id(0) == 0)
    def _():
        for which, ref in enumerate((wq_ref, wk_ref, wv_ref)):
            w_ref[which] = ref[...].astype(BF16)

    rows, width = x_ref.shape
    grad = jnp.zeros((rows, width), F32)
    for g, group in enumerate(groups):
        for which, ref in enumerate(group):
            cols = ref.shape[1]
            grad = grad + dot_nt(ref[...], w_ref[which, :, g * cols : (g + 1) * cols])
    grad = (grad.reshape(rows // BLOCK, BLOCK, width) + gsum_ref[...][:, None, :]).reshape(rows, width)
    unit, inverse = normalize(x_ref[...])
    out_ref[...] = gsec_ref[...] + norm_grad(grad, unit, inverse, gain_ref[...])


def input_grad(groups, gsum, x, gsec, gain, wq, wk, wv, tile=512):
    rows, width = x.shape
    weight = pl.BlockSpec((width, width), lambda *_: (0, 0), pipeline_mode=pl.Buffered(1))
    flat = [array for group in groups for array in group]
    return pl.pallas_call(
        input_kernel,
        grid=(rows // tile,),
        in_specs=[rows_of(tile, array.shape[1]) for array in flat]
        + [rows_of(tile // BLOCK, width)]
        + [rows_of(tile, width)] * 2
        + [whole((1, width))]
        + [weight] * 3,
        out_specs=rows_of(tile, width),
        out_shape=far_shape((rows, width), F32),
        scratch_shapes=[pltpu.VMEM((3, width, width), BF16)],
        compiler_params=params(20),
        cost_estimate=cost(True),
        name="input_grad",
    )(*[near(array) for array in flat], gsum, far(x), far(gsec), gain, far(wq), far(wk), far(wv))


def pack_kernel(where_ref, up_a_ref, down_a_ref, up_b_ref, down_b_ref, mine_ref, other_ref):
    mine_ref[0] = up_a_ref[...].astype(BF16)
    mine_ref[1] = down_a_ref[...].astype(BF16)
    other_ref[0] = up_b_ref[...].astype(BF16)
    other_ref[1] = down_b_ref[...].astype(BF16)


def pack_weights(core, w_up, w_down):
    width, units = w_up.shape
    half = units // 2

    def up(flip):
        return pl.BlockSpec((width, half), lambda step, core: (0, core[0] ^ flip))

    def down(flip):
        return pl.BlockSpec((half, width), lambda step, core: (core[0] ^ flip, 0))

    shape = (2, width, half)
    return pl.pallas_call(
        pack_kernel,
        grid_spec=pltpu.PrefetchScalarGridSpec(
            num_scalar_prefetch=1,
            grid=(1,),
            in_specs=[up(0), down(0), up(1), down(1)],
            out_specs=[whole(shape), whole(shape)],
        ),
        out_shape=[near_shape(shape, BF16)] * 2,
        compiler_params=params(16),
        cost_estimate=cost(True),
        name="pack_weights",
    )(core, far(w_up), far(w_down), far(w_up), far(w_down))


def finish_feed_kernel(where_ref, mine_ref, other_ref, up_ref, down_ref, turn_ref):
    chunks, _, size, units = mine_ref.shape
    for flip, ref in enumerate((mine_ref, other_ref)):
        column = pl.multiple_of((where_ref[1] ^ flip) * units, units)
        for r in range(chunks):
            at = pl.multiple_of((r ^ where_ref[0]) * size, size)
            up_ref[pl.ds(at, size), pl.ds(column, units)] = ref[r, 0].astype(F32)
            turn_ref[pl.ds(at, size), :] = ref[r, 1].astype(F32)
        down_ref[pl.ds(column, units), :] = turn_ref[...].T


def finish_feed(where, mine, other):
    chunks, _, size, units = mine.shape
    width = chunks * size
    vmem = pl.BlockSpec(memory_space=pltpu.VMEM)
    return pl.pallas_call(
        finish_feed_kernel,
        in_specs=[pl.BlockSpec(memory_space=pltpu.SMEM)] + [vmem] * 2,
        out_specs=[vmem, vmem],
        out_shape=[far_shape((width, 2 * units), F32), far_shape((2 * units, width), F32)],
        scratch_shapes=[pltpu.VMEM((width, units), F32)],
        compiler_params=params(16),
        cost_estimate=cost(True),
        name="finish_feed",
    )(where, mine, other)


def finish_kernel(
    where_ref, piece_a_ref, piece_b_ref, wq_ref, wk_ref, wv_ref, ws_ref, gain_ref,
    gq_ref, gk_ref, gv_ref, gs_ref, go_ref, gain_one_ref, gain_two_ref, entropy_ref, one_ref, two_ref,
):
    width = wq_ref.shape[0]
    chunks, size = piece_a_ref.shape[:2]
    cols = piece_b_ref.shape[2] // 4
    for r in range(chunks):
        rows = pl.ds(pl.multiple_of((r ^ where_ref[2]) * size, size), size)
        go_ref[rows, :] = piece_a_ref[r, :, 4 * cols : 4 * cols + width].astype(F32)
        two_ref[rows, :] = piece_a_ref[r, :, 4 * cols + width :].astype(F32)
        for g, piece in enumerate((piece_a_ref, piece_b_ref)):
            span = slice(g * cols, (g + 1) * cols)
            for index, ref in enumerate((gq_ref, gk_ref, gv_ref, gs_ref)):
                ref[rows, span] = piece[r, :, index * cols : (index + 1) * cols].astype(F32)
    total = jnp.zeros((width, LANES), F32)
    for at in range(0, width, LANES):
        span = slice(at, at + LANES)
        for grad, weight in ((gq_ref, wq_ref), (gk_ref, wk_ref), (gv_ref, wv_ref)):
            total = total + grad[:, span] * weight[:, span].astype(BF16).astype(F32)
        total = total + gs_ref[:, span] * ws_ref[:, span]
    one_ref[...] = total
    gain_one_ref[...] = jnp.sum(one_ref[...].T, axis=0, keepdims=True) / gain_ref[...]
    turned = two_ref[...].T
    gain_two_ref[...] = turned[:1, :]
    entropy_ref[...] = turned[LANES // 2 : LANES // 2 + 1, :]


def finish(where, pieces, wq, wk, wv, ws, gain):
    width = wq.shape[0]
    vmem = pl.BlockSpec(memory_space=pltpu.VMEM)
    square = far_shape((width, width), F32)
    row = shape_of((1, width), F32)
    return pl.pallas_call(
        finish_kernel,
        in_specs=[pl.BlockSpec(memory_space=pltpu.SMEM)] + [vmem] * 7,
        out_specs=[vmem] * 8,
        out_shape=[square] * 5 + [row] * 3,
        scratch_shapes=[pltpu.VMEM((width, LANES), F32)] * 2,
        compiler_params=params(16),
        cost_estimate=cost(True),
        name="finish",
    )(where, *pieces, far(wq), far(wk), far(wv), far(ws), gain)


MP, CORE, X, Z_LOW, Z_HIGH = 1, 2, 4, 8, 16
CORE_STEP = ((CORE,), (CORE,))
FEED_STEPS = ((X,), (Z_LOW, Z_HIGH, Z_LOW + Z_HIGH))
HEAD_STEPS = ((CORE,), (MP, X, MP + X), (Z_LOW, Z_HIGH, Z_LOW + Z_HIGH))


def swap(array, flip):
    count = lax.axis_size("batch") * lax.axis_size("mp")
    return lax.ppermute(array, ("batch", "mp"), [(i, i ^ flip) for i in range(count)])


def place(steps, index):
    result = jnp.int32(0)
    for step in steps:
        for bit in reversed(step[: (len(step) + 1).bit_length() - 1]):
            result = 2 * result + ((index & bit) > 0).astype(jnp.int32)
    return result


def add_low(left, right):
    return (left.astype(F32) + right.astype(F32)).astype(BF16)


class Walk:
    def __init__(self, piece, steps):
        self.value = piece
        self.down = list(steps)
        self.up = list(reversed(steps))
        self.reducing = False
        self.arrived = []

    def combine(self, plan):
        arrived = self.arrived if plan is None else [plan.after(array) for array in self.arrived]
        if arrived and self.reducing:
            self.value = self.value.astype(F32)
            for array in arrived:
                self.value = self.value + array.astype(F32)
            if not self.down:
                self.value = self.value.astype(BF16)
        elif arrived:
            self.value = jnp.concatenate([self.value] + arrived, axis=0)

    def step(self, plan=None):
        self.combine(plan)
        send = (lambda array: array) if plan is None else plan.after
        self.reducing = bool(self.down)
        if self.reducing:
            flips = self.down.pop(0)
            size = self.value.shape[0] // (len(flips) + 1)
            self.arrived = [
                swap(send(self.value[(n + 1) * size : (n + 2) * size].astype(BF16)), flip)
                for n, flip in enumerate(flips)
            ]
            self.value = self.value[:size]
        else:
            mine = send(self.value)
            self.arrived = [swap(mine, flip) for flip in self.up.pop(0)]
        return self.arrived

    def rest(self):
        while self.down or self.up:
            self.step()
        self.combine(None)
        return self.value


class Schedule:
    def __init__(self):
        self.pending, self.launched, self.done = [], [], None

    def after(self, array):
        return lax.optimization_barrier((array, self.done))[0]

    def enter(self, small):
        tied = lax.optimization_barrier((small, *self.pending))[0]
        self.pending, self.launched = self.launched, []
        return tied

    def leave(self, *arrays):
        self.pending.extend(arrays)
        self.done = arrays[0]

    def launch(self, *arrays):
        for array in arrays:
            self.launched.extend(array if isinstance(array, list) else [array])


def local_small(
    inputs, cotangent, block_perm, block_mask, pen_weight, w_query, w_key, w_value, w_out, w_sort,
    gain_one, gain_two, w_up, w_down,
):
    _, rows, width = inputs.shape
    x = inputs.reshape(rows, width)
    cot = cotangent.reshape(rows, width)
    perm = block_perm.reshape(-1)
    mask = block_mask.reshape(-1)
    perm_row = block_perm.reshape(1, -1)
    mask_row = block_mask.reshape(1, -1)
    gain_one_row = gain_one.reshape(1, width)
    gain_two_row = gain_two.reshape(1, width)
    batch, mp = lax.axis_index("batch"), lax.axis_index("mp")
    core = batch & 1
    index = batch * 2 + mp
    where = jnp.stack([place(FEED_STEPS, index), core, place(HEAD_STEPS, index)])
    row_chunks, out_chunks = 8, 32
    plan = Schedule()

    count = jnp.broadcast_to(jnp.sum(mask.astype(F32)), (8, LANES))
    flips = [CORE, MP, X, Z_LOW, Z_HIGH]

    def count_step(count):
        arrived = swap(plan.after(count), flips.pop(0))
        plan.launch(arrived)
        return count + arrived

    own_a, own_b = pack_weights(core.reshape(1), w_up, w_down)
    far_a = swap(own_a, MP)
    plan.leave(own_b)
    count = count_step(count)
    act_one, q, k, v, probs, att, second, shares, act_two, sums, plan_log, chosen, entropy = forward(
        perm, mask, perm_row, mask_row, plan.enter(gain_one_row), gain_two_row, x, w_query, w_key, w_value,
        w_sort, w_out,
    )
    plan.leave(act_two)
    count = count_step(count)
    cot_low, sofar, hid_a, piece = feed_quarter(plan.enter(where), act_two, cot, own_b, None, row_chunks)
    plan.leave(piece)
    plan.pending.append(far_a)

    far_b = swap(plan.after(far_a), CORE)
    near = swap(plan.after(piece), CORE)
    plan.launch(far_b, near)
    count = count_step(count)
    sofar, hid_b, piece = feed_quarter(plan.enter(where), act_two, cot_low, own_a, sofar, row_chunks)
    plan.leave(piece)

    own = piece.astype(F32) + plan.after(near).astype(F32)
    count = count_step(count)
    sofar, hid_c, piece = feed_quarter(plan.enter(where), act_two, cot_low, far_b, sofar, row_chunks)
    plan.leave(piece)

    near = swap(plan.after(piece), CORE)
    plan.launch(near)
    count = count_step(count)
    sofar, hid_d, piece = feed_quarter(plan.enter(where), act_two, cot_low, far_a, sofar, row_chunks)
    plan.leave(piece)

    arrived = swap(add_low(piece, plan.after(near)), MP)
    grad_second, grad_att, out_piece = settle(
        plan.enter(where), sofar, cot, second, att, w_out, gain_two_row, entropy, out_chunks
    )
    plan.leave(grad_att)

    gq, gk, gv, gch = attend_back(plan.enter(perm), q, grad_att, probs, k, v, chosen, 0)
    plan.leave(gch)
    groups = [(gq, gk, gv)]

    block_total = count[0, 0]
    coef = (pen_weight[0] / (HEADS * block_total)).reshape(1)
    piece, gsum = group_grads(
        plan.enter(where), coef, act_one, gq, gk, gv, gch, shares, plan_log, sums, w_sort,
        perm_row, mask_row, out_piece, 0, out_chunks,
    )
    plan.leave(gsum)

    first = Walk(piece, HEAD_STEPS)
    feed_sum = Walk(own + plan.after(arrived).astype(F32), FEED_STEPS)
    plan.launch(first.step(plan), feed_sum.step(plan))
    gq, gk, gv, gch = attend_back(plan.enter(perm), q, grad_att, probs, k, v, chosen, 1)
    plan.leave(gch)
    groups.append((gq, gk, gv))

    plan.launch(first.step(plan), feed_sum.step(plan))
    piece, gsum = group_grads(
        plan.enter(where), coef, act_one, gq, gk, gv, gch, shares, plan_log, sums, w_sort,
        perm_row, mask_row, gsum, 1, out_chunks,
    )
    plan.leave(gsum)

    final = Walk(piece, HEAD_STEPS)
    final.step(plan)
    plan.launch(final.step(plan), first.step(plan), feed_sum.step(plan))
    grad_input = input_grad(
        groups, gsum, x, grad_second, plan.enter(gain_one_row), w_query, w_key, w_value
    )
    plan.leave(grad_input)

    final.step(plan)
    first.step(plan)
    feed_sum.step(plan)
    final.step(plan)
    plan.launch(final.step(plan), first.step(plan))
    quarters = (own_b, own_a, far_b, far_a)
    output = layer_output(plan.enter(second), (hid_a, hid_b, hid_c, hid_d), quarters)
    plan.leave(output)
    final.step(plan)
    pieces = [first.rest(), final.rest()]
    total = feed_sum.rest()
    grad_up, grad_down = finish_feed(where, total, swap(total, CORE))
    grad_query, grad_key, grad_value, grad_sort, grad_out, grad_gain_one, grad_gain_two, entropies = finish(
        where, pieces, w_query, w_key, w_value, w_sort, gain_one_row
    )
    return (
        output.reshape(inputs.shape),
        (jnp.sum(entropies) / (HEADS * block_total)).reshape(1),
        grad_input.reshape(inputs.shape),
        grad_query,
        grad_key,
        grad_value,
        grad_out,
        grad_sort,
        grad_gain_one.reshape(width),
        grad_gain_two.reshape(width),
        grad_up,
        grad_down,
    )


def local_any(
    inputs, cotangent, block_perm, block_mask, pen_weight, w_query, w_key, w_value, w_out, w_sort,
    gain_one, gain_two, w_up, w_down,
):
    both = ("batch", "mp")
    _, rows, width = inputs.shape
    x = inputs.reshape(rows, width)
    cot = cotangent.reshape(rows, width)
    perm = block_perm.reshape(-1)
    mask = block_mask.reshape(-1)
    perm_row = block_perm.reshape(1, -1)
    mask_row = block_mask.reshape(1, -1)
    gain_one_row = gain_one.reshape(1, width)
    gain_two_row = gain_two.reshape(1, width)
    where = jnp.zeros((3,), jnp.int32)
    up_all = lax.all_gather(w_up.astype(BF16), "mp", axis=1, tiled=True)
    down_all = lax.all_gather(w_down.astype(BF16), "mp", axis=0, tiled=True)
    quarters = [
        jnp.stack([up_all[:, at : at + width], down_all[at : at + width]])
        for at in range(0, up_all.shape[1], width)
    ]
    act_one, q, k, v, probs, att, second, shares, act_two, sums, plan_log, chosen, entropy = forward(
        perm, mask, perm_row, mask_row, gain_one_row, gain_two_row, x, w_query, w_key, w_value, w_sort, w_out
    )
    block_total = lax.psum(jnp.sum(mask_row).astype(F32), both)
    hidden, parts = [], []
    sofar = None
    cot_low = cot
    for weights in quarters:
        results = feed_quarter(where, act_two, cot_low, weights, sofar, 1)
        if sofar is None:
            cot_low = results[0]
        sofar, hid, piece = results[-3:]
        hidden.append(hid)
        parts.append(piece[0])
    grad_second, grad_att, extra = settle(where, sofar, cot, second, att, w_out, gain_two_row, entropy, 1)
    coef = (pen_weight[0] / (HEADS * block_total)).reshape(1)
    groups, pieces = [], []
    for group in range(width // GROUP_WIDTH):
        gq, gk, gv, gch = attend_back(perm, q, grad_att, probs, k, v, chosen, group)
        piece, extra = group_grads(
            where, coef, act_one, gq, gk, gv, gch, shares, plan_log, sums, w_sort, perm_row, mask_row,
            extra, group, 1,
        )
        groups.append((gq, gk, gv))
        pieces.append(piece)
    grad_input = input_grad(groups, extra, x, grad_second, gain_one_row, w_query, w_key, w_value)
    output = layer_output(second, hidden, quarters)

    parts = jnp.concatenate(parts, axis=2)
    parts = lax.psum(lax.psum_scatter(parts, "mp", scatter_dimension=2, tiled=True), "batch").astype(F32)
    grad_up, grad_down = parts[0], parts[1].T
    pieces = lax.psum(pieces, both)
    grad_query, grad_key, grad_value, grad_sort, grad_out, grad_gain_one, grad_gain_two, entropies = finish(
        where, pieces, w_query, w_key, w_value, w_sort, gain_one_row
    )
    return (
        output.reshape(inputs.shape),
        (jnp.sum(entropies) / (HEADS * block_total)).reshape(1),
        grad_input.reshape(inputs.shape),
        grad_query,
        grad_key,
        grad_value,
        grad_out,
        grad_sort,
        grad_gain_one.reshape(width),
        grad_gain_two.reshape(width),
        grad_up,
        grad_down,
    )


def solution(mesh):
    tokens = P(("batch", "mp"), None, None)
    blocks = P(("batch", "mp"), None)
    small = mesh.shape["batch"] == 16 and mesh.shape["mp"] == 2
    return jax.shard_map(
        local_small if small else local_any,
        mesh=mesh,
        in_specs=(tokens, tokens, blocks, blocks) + (P(),) * 8 + (P(None, "mp"), P("mp", None)),
        out_specs=(tokens, P(), tokens) + (P(),) * 7 + (P(None, "mp"), P("mp", None)),
        check_vma=False,
    )
```

```python
import functools

import jax
import jax.numpy as jnp
from jax import lax
from jax.experimental import pallas as pl
from jax.experimental.pallas import tpu as pltpu
from jax.sharding import PartitionSpec as P

HEADS = 8
HEAD_DIM = 64
BLOCK = 32
ITERS = 8
GROUP = 4
GROUP_WIDTH = GROUP * HEAD_DIM
GROUP_ROWS = GROUP * BLOCK
EPSILON = 1e-05
FACTOR = HEAD_DIM ** (-0.5)
HIGHEST = lax.Precision.HIGHEST
F32 = jnp.float32
BF16 = jnp.bfloat16
NT = (((1,), (1,)), ((), ()))
TN = (((0,), (0,)), ((), ()))
MIB = 1024 * 1024
LANES = 128
TALLY_ROWS = 16


def dot(left, right):
    return jnp.dot(left, right, preferred_element_type=F32)


def dot_nt(left, right):
    return lax.dot_general(left, right, NT, preferred_element_type=F32)


def dot_tn(left, right):
    return lax.dot_general(left, right, TN, preferred_element_type=F32)


def shape_of(dims, dtype):
    return jax.ShapeDtypeStruct(dims, dtype)


def whole(dims):
    return pl.BlockSpec(dims, lambda *_: (0,) * len(dims))


def once(dims):
    return pl.BlockSpec(dims, lambda *_: (0,) * len(dims), pipeline_mode=pl.Buffered(1))


def rows_of(size, width):
    return pl.BlockSpec((size, width), lambda step, *_: (step, 0))


def params(mib):
    return pltpu.CompilerParams(vmem_limit_bytes=mib * MIB)


def far(array):
    return pltpu.with_memory_space_constraint(array, pltpu.HBM)


def near(array):
    return pltpu.with_memory_space_constraint(array, pltpu.VMEM)


def near_shape(dims, dtype):
    return pltpu.VMEM(dims, dtype)


def far_shape(dims, dtype):
    return pltpu.HBM(dims, dtype)


def cost(micros):
    return pl.CostEstimate(flops=int(micros * 1150000000), bytes_accessed=0, transcendentals=0)


def normalize(values):
    center = values - jnp.mean(values, axis=-1, keepdims=True)
    inverse = lax.rsqrt(jnp.mean(center * center, axis=-1, keepdims=True) + EPSILON)
    return center * inverse, inverse


def norm_grad(grad_rows, unit_rows, inverse, gain):
    scaled_rows = grad_rows * gain
    return inverse * (
        scaled_rows
        - jnp.mean(scaled_rows, axis=-1, keepdims=True)
        - unit_rows * jnp.mean(scaled_rows * unit_rows, axis=-1, keepdims=True)
    )


def segment_sum(tile, first):
    left = jnp.sum(jnp.where(first, tile, 0.0), axis=1, keepdims=True)
    right = jnp.sum(jnp.where(first, 0.0, tile), axis=1, keepdims=True)
    return jnp.where(first, left, right)


def segment_max(tile, first):
    left = jnp.max(jnp.where(first, tile, -jnp.inf), axis=1, keepdims=True)
    right = jnp.max(jnp.where(first, -jnp.inf, tile), axis=1, keepdims=True)
    return jnp.where(first, left, right)


def head_masks(rows):
    lane = lax.broadcasted_iota(jnp.int32, (rows, GROUP_WIDTH), 1)
    return [(lane >= h * HEAD_DIM) & (lane < (h + 1) * HEAD_DIM) for h in range(GROUP)]


def expand(rows, masks):
    zero = jnp.zeros_like(rows)
    return jnp.concatenate([jnp.where(mask, rows, zero) for mask in masks], axis=0)


def fold(rows, masks):
    parts = [rows[h * BLOCK : (h + 1) * BLOCK] for h in range(GROUP)]
    result = parts[GROUP - 1]
    for h in range(GROUP - 1):
        result = jnp.where(masks[h], parts[h], result)
    return result


def lane_tiles(blocks):
    lane = lax.broadcasted_iota(jnp.int32, (blocks, 2 * blocks), 1)
    return lane < blocks, jnp.where(lane < blocks, lane, lane - blocks).astype(F32)


def down_rows(row, wide):
    return jnp.broadcast_to(row.astype(F32), (wide, row.shape[1])).T


def balance_plans(logits, perm_row, mask_row, share_ref, log_ref, chosen_ref, entropy_ref):
    blocks = logits.shape[0]
    wide = 2 * blocks
    first, position = lane_tiles(blocks)
    hot = position == down_rows(perm_row, wide)
    real = down_rows(mask_row, wide) > 0.0
    for pair in range(logits.shape[1] // wide):
        span = slice(pair * wide, (pair + 1) * wide)
        tile = logits[:, span]
        for step in range(ITERS):
            top = segment_max(tile, first)
            powers = jnp.exp(tile - top)
            total = segment_sum(powers, first)
            tile = tile - (top + jnp.log(total))
            share_ref[2 * step, :, span] = powers * (1.0 / total)
            top = jnp.max(tile, axis=0, keepdims=True)
            powers = jnp.exp(tile - top)
            total = jnp.sum(powers, axis=0, keepdims=True)
            tile = tile - (top + jnp.log(total))
            if step < ITERS - 1:
                share_ref[2 * step + 1, :, span] = powers * (1.0 / total)
        plan = jnp.exp(tile)
        share_ref[2 * ITERS - 1, :, span] = plan
        log_ref[:, span] = tile
        chosen_ref[:, span] = blocks * segment_sum(jnp.where(hot, plan, 0.0), first)
        entropy_ref[:, span] = -jnp.sum(jnp.where(real, plan * tile, 0.0), axis=0, keepdims=True)


def forward_kernel(
    perm_ref, mask_ref, other_ref, perm_row_ref, mask_row_ref, gain_one_ref, gain_two_ref,
    x_far, wq_far, wk_far, wv_far, ws_far, wo_far, up_far, down_far,
    act_far, q_far, k_far, v_far, probs_far, att_far, second_far, act_two_far, share_far,
    sum_ref, log_ref, chosen_ref, entropy_ref, packed_ref,
    x_ref, w_ref, w_low_ref, wo_low_ref, act_ref, q_ref, k_ref, v_ref, probs_ref, att_ref, second_ref, act_two_ref, share_ref,
    feed_ref, in_sem, out_sem, share_sem, feed_sem, *, tile,
):
    rows, width = x_ref.shape
    tiles = rows // tile

    def x_copy(i):
        at = pl.ds(pl.multiple_of(i * tile, tile), tile)
        return pltpu.make_async_copy(x_far.at[at, :], x_ref.at[at, :], in_sem.at[i])

    def w_copy(n):
        far_ref = (wq_far, wk_far, wv_far, ws_far, wo_far)[n]
        return pltpu.make_async_copy(far_ref, w_ref.at[n], in_sem.at[tiles + n])

    outs = (
        (act_ref, act_far), (q_ref, q_far), (k_ref, k_far), (v_ref, v_far),
        (probs_ref, probs_far), (att_ref, att_far), (second_ref, second_far), (act_two_ref, act_two_far),
    )
    part = 8
    some = part * BLOCK
    parts = rows // some

    def out_copy(n, i):
        near_ref, far_ref = outs[n]
        size = near_ref.shape[0] // (tiles if n < 4 else parts)
        at = pl.ds(pl.multiple_of(i * size, size), size)
        return pltpu.make_async_copy(near_ref.at[at, :], far_ref.at[at, :], out_sem.at[n, i])

    x_copy(0).start()
    for n in range(3):
        w_copy(n).start()
    for i in range(1, tiles):
        x_copy(i).start()
    w_copy(3).start()
    w_copy(4).start()
    units = packed_ref.shape[2]
    at = pl.ds(pl.multiple_of(other_ref[0] * units, units), units)
    feed_copies = [
        pltpu.make_async_copy(up_far.at[:, at], feed_ref.at[0], feed_sem.at[0]),
        pltpu.make_async_copy(down_far.at[at, :], feed_ref.at[1], feed_sem.at[1]),
    ]
    for copy in feed_copies:
        copy.start()
    for n in range(3):
        w_copy(n).wait()
        w_low_ref[:, n * width : (n + 1) * width] = w_ref[n].astype(BF16)

    def prepare(i):
        at = pl.ds(pl.multiple_of(i * tile, tile), tile)
        unit, _ = normalize(x_ref[at, :])
        act = (unit * gain_one_ref[...]).astype(BF16)
        act_ref[at, :] = act
        sums = jnp.sum(act.astype(F32).reshape(tile // BLOCK, BLOCK, width), axis=1)
        some = tile // BLOCK
        sum_ref[pl.ds(pl.multiple_of(i * some, some), some), :] = sums.astype(BF16).astype(F32)

    def project(i):
        at = pl.ds(pl.multiple_of(i * tile, tile), tile)
        act = act_ref[at, :]
        for n, ref in enumerate((q_ref, k_ref, v_ref)):
            ref[at, :] = dot(act, w_low_ref[:, n * width : (n + 1) * width]).astype(BF16)

    def project_out(i):
        for n in range(4):
            out_copy(n, i).start()

    def both(i, _):
        x_copy(i + 1).wait()
        project(i)
        prepare(i + 1)
        project_out(i)
        return 0

    x_copy(0).wait()
    prepare(0)
    lax.fori_loop(0, tiles - 2, both, 0)
    x_copy(tiles - 1).wait()
    prepare(tiles - 1)
    w_copy(3).wait()
    w_copy(4).wait()
    wo_low_ref[...] = w_ref[4].astype(BF16)
    for n, copy in enumerate(feed_copies):
        copy.wait()
        packed_ref[n] = feed_ref[n].astype(BF16)
    logits = jnp.dot(sum_ref[...], w_ref[3], precision=HIGHEST, preferred_element_type=F32)
    balance_plans(
        logits, perm_row_ref[...], mask_row_ref[...], share_ref, log_ref, chosen_ref, entropy_ref
    )
    for i in (tiles - 2, tiles - 1):
        project(i)
    for i in (tiles - 2, tiles - 1):
        project_out(i)
    pltpu.make_async_copy(share_ref, share_far, share_sem).start()

    masks = head_masks(BLOCK)
    key_row = lax.broadcasted_iota(jnp.int32, (BLOCK, GROUP_ROWS), 0)
    query_row = lax.broadcasted_iota(jnp.int32, (BLOCK, GROUP_ROWS), 1) % BLOCK
    causal = key_row <= query_row

    def attend(j):
        for b in range(part):
            block = j * part + b
            partner = perm_ref[block]
            usable = (partner < block) & (mask_ref[partner] > 0)
            own_at = pl.ds(pl.multiple_of(block * BLOCK, BLOCK), BLOCK)
            far_at = pl.ds(pl.multiple_of(partner * BLOCK, BLOCK), BLOCK)
            probs_at = pl.ds(pl.multiple_of(block * 2 * BLOCK, 2 * BLOCK), 2 * BLOCK)
            chosen_row = chosen_ref[pl.ds(block, 1), :]
            for g in range(width // GROUP_WIDTH):
                lanes = slice(g * GROUP_WIDTH, (g + 1) * GROUP_WIDTH)
                queries = expand(q_ref[own_at, lanes], masks)
                keys = jnp.concatenate([k_ref[own_at, lanes], k_ref[far_at, lanes]], axis=0)
                scores = dot_nt(keys, queries) * FACTOR
                own = jnp.where(causal, scores[:BLOCK], -1e30)
                far = jnp.where(usable, scores[BLOCK:], -1e30)
                top = jnp.maximum(jnp.max(own, axis=0, keepdims=True), jnp.max(far, axis=0, keepdims=True))
                powers = jnp.exp(jnp.concatenate([own, far], axis=0) - top)
                probs = (powers * (1.0 / jnp.sum(powers, axis=0, keepdims=True))).astype(BF16)
                probs_ref[probs_at, g * GROUP_ROWS : (g + 1) * GROUP_ROWS] = probs
                scaled = (v_ref[far_at, lanes].astype(F32) * chosen_row[:, lanes]).astype(BF16)
                values = jnp.concatenate([v_ref[own_at, lanes], scaled], axis=0)
                att_ref[own_at, lanes] = fold(dot_tn(probs, values), masks).astype(BF16)

    def settle(j):
        at = pl.ds(pl.multiple_of(j * some, some), some)
        second = x_ref[at, :] + dot(att_ref[at, :], wo_low_ref[...])
        second_ref[at, :] = second
        unit, _ = normalize(second)
        act_two_ref[at, :] = (unit * gain_two_ref[...]).astype(BF16)

    def settle_out(j):
        for n in range(4, 8):
            out_copy(n, j).start()

    def step(j, _):
        settle(j - 1)
        attend(j)
        settle_out(j - 1)
        return 0

    attend(0)
    lax.fori_loop(1, parts, step, 0)
    settle(parts - 1)
    settle_out(parts - 1)
    for n in range(8):
        for i in range(tiles if n < 4 else parts):
            out_copy(n, i).wait()
    pltpu.make_async_copy(share_ref, share_far, share_sem).wait()


def forward(perm, mask, other, perm_row, mask_row, gain_one, gain_two, x, wq, wk, wv, ws, wo, w_up, w_down, tile=512):
    rows, width = x.shape
    blocks = rows // BLOCK
    tiles = rows // tile
    smem = pl.BlockSpec(memory_space=pltpu.SMEM)
    vmem = pl.BlockSpec(memory_space=pltpu.VMEM)
    hbm = pl.BlockSpec(memory_space=pltpu.HBM)
    low = ((rows, width), BF16)
    probs = ((2 * rows, HEADS * BLOCK), BF16)
    full = ((rows, width), F32)
    share = ((2 * ITERS, blocks, width), F32)
    plan = ((blocks, width), F32)
    packed = ((2, width, width), BF16)
    return pl.pallas_call(
        functools.partial(forward_kernel, tile=tile),
        in_specs=[smem] * 3 + [vmem] * 4 + [hbm] * 8,
        out_specs=[hbm] * 9 + [vmem] * 5,
        out_shape=[far_shape(*s) for s in (low, low, low, low, probs, low, full, low, share)]
        + [near_shape(*s) for s in (plan, plan, plan, ((1, width), F32), packed)],
        scratch_shapes=[pltpu.VMEM(*full), pltpu.VMEM((5, width, width), F32), pltpu.VMEM((width, 3 * width), BF16)]
        + [pltpu.VMEM((width, width), BF16)]
        + [pltpu.VMEM(*s) for s in (low, low, low, low, probs, low, full, low, share)]
        + [
            pltpu.VMEM((2, width, width), F32),
            pltpu.SemaphoreType.DMA((tiles + 5,)),
            pltpu.SemaphoreType.DMA((8, rows // (8 * BLOCK))),
            pltpu.SemaphoreType.DMA,
            pltpu.SemaphoreType.DMA((2,)),
        ],
        compiler_params=params(40),
        cost_estimate=cost(25),
        name="forward",
    )(
        perm, mask, other, perm_row, mask_row, gain_one, gain_two, far(x), far(wq), far(wk), far(wv), far(ws), far(wo),
        far(w_up), far(w_down),
    )


def attend_back_kernel(
    perm_ref, chosen_ref, gatt_ref, q_far, probs_far, k_far, v_far,
    gq_ref, gk_ref, gv_ref, gch_ref,
    q_ref, probs_ref, k_ref, v_ref, own_k_ref, far_k_ref, own_v_ref, far_v_ref, sems, *, group, part,
):
    rows, width = q_ref.shape
    parts = rows // (part * BLOCK)
    masks = head_masks(BLOCK)

    def copies():
        for n, (far_ref, near_ref) in enumerate(((k_far, k_ref), (v_far, v_ref), (q_far, q_ref), (probs_far, probs_ref))):
            cols = near_ref.shape[1]
            lanes = pl.ds(group * cols, cols)
            yield pltpu.make_async_copy(far_ref.at[:, lanes], near_ref, sems.at[n])

    for copy in copies():
        copy.start()
    for copy in copies():
        copy.wait()

    def body(j, _):
        for b in range(part):
            block = j * part + b
            partner = perm_ref[block]
            own_at = pl.ds(pl.multiple_of(block * BLOCK, BLOCK), BLOCK)
            far_at = pl.ds(pl.multiple_of(partner * BLOCK, BLOCK), BLOCK)
            probs_at = pl.ds(pl.multiple_of(block * 2 * BLOCK, 2 * BLOCK), 2 * BLOCK)
            queries = expand(q_ref[own_at, :], masks)
            grads = expand(gatt_ref[own_at, group * width : (group + 1) * width], masks)
            keys = jnp.concatenate([k_ref[own_at, :], k_ref[far_at, :]], axis=0)
            far_values = v_ref[far_at, :].astype(F32)
            chosen = chosen_ref[pl.ds(block, 1), group * width : (group + 1) * width]
            values = jnp.concatenate([v_ref[own_at, :], (far_values * chosen).astype(BF16)], axis=0)
            probs_low = probs_ref[probs_at, :]
            probs = probs_low.astype(F32)
            grad_probs = dot_nt(values, grads)
            total = jnp.sum(probs * grad_probs, axis=0, keepdims=True)
            grad_scores = (probs * (grad_probs - total)).astype(BF16)
            grad_keys = dot(grad_scores, queries) * FACTOR
            grad_values = dot(probs_low, grads)
            gq_ref[own_at, :] = (fold(dot_tn(grad_scores, keys), masks) * FACTOR).astype(BF16)
            far_grad = grad_values[BLOCK:]
            gch_ref[pl.ds(block, 1), :] = jnp.sum(far_grad * far_values, axis=0, keepdims=True)
            own_k_ref[own_at, :] = grad_keys[:BLOCK]
            far_k_ref[far_at, :] = grad_keys[BLOCK:]
            own_v_ref[own_at, :] = grad_values[:BLOCK]
            far_v_ref[far_at, :] = far_grad * chosen
        return 0

    lax.fori_loop(0, parts, body, 0)
    gk_ref[...] = (own_k_ref[...] + far_k_ref[...]).astype(BF16)
    gv_ref[...] = (own_v_ref[...] + far_v_ref[...]).astype(BF16)


def attend_back(perm, q, gatt, probs, k, v, chosen, group, part=8):
    rows = q.shape[0]
    smem = pl.BlockSpec(memory_space=pltpu.SMEM)
    vmem = pl.BlockSpec(memory_space=pltpu.VMEM)
    hbm = pl.BlockSpec(memory_space=pltpu.HBM)
    low = ((rows, GROUP_WIDTH), BF16)
    full = ((rows, GROUP_WIDTH), F32)
    return pl.pallas_call(
        functools.partial(attend_back_kernel, group=group, part=part),
        in_specs=[smem, vmem, vmem] + [hbm] * 4,
        out_specs=[vmem] * 4,
        out_shape=[near_shape(*s) for s in (low, low, low, ((rows // BLOCK, GROUP_WIDTH), F32))],
        scratch_shapes=[pltpu.VMEM(*s) for s in (low, ((2 * rows, GROUP_ROWS), BF16), low, low, full, full, full, full)]
        + [pltpu.SemaphoreType.DMA((4,))],
        compiler_params=params(18),
        cost_estimate=cost(10),
        name="attend_back",
    )(perm, near(chosen), near(gatt), far(q), far(probs), far(k), far(v))


def gelu_pair(up):
    square = up * up
    inner = 0.7978845608028654 * 0.044715
    half = 0.5 + 0.5 * jnp.tanh(up * (0.7978845608028654 + inner * square))
    value = up * half
    slope = half + (2.0 * value) * (1.0 - half) * (0.7978845608028654 + 3.0 * inner * square)
    return value, slope


def spread(out_ref, acc_ref, where, lanes):
    chunks, size = out_ref.shape[0], out_ref.shape[-2]
    for r in range(chunks):
        at = pl.multiple_of((r ^ where) * size, size)
        out_ref[r, :, lanes] = acc_ref[pl.ds(at, size), :].astype(out_ref.dtype)


class Copies:
    def __init__(self, source, target, sems, tile):
        self.source, self.target, self.sems, self.tile = source, target, sems, tile

    def copy(self, i):
        at = pl.ds(pl.multiple_of(i * self.tile, self.tile), self.tile)
        return pltpu.make_async_copy(self.source.at[at, :], self.target.at[at, :], self.sems.at[i])

    def start(self, i):
        self.copy(i).start()

    def wait(self, i):
        self.copy(i).wait()


def quarter_math(act, cot_low, weights_ref, up_acc, down_acc):
    value, slope = gelu_pair(dot(act, weights_ref[0]))
    hidden = value.astype(BF16)
    grad_up = (dot_nt(cot_low, weights_ref[1]) * slope).astype(BF16)
    up_acc[...] += dot_tn(act, grad_up)
    down_acc[...] += dot_tn(cot_low, hidden)
    return hidden, dot_nt(grad_up, weights_ref[0])


def quarter_kernel(*refs, kind, tile, tally):
    if tally:
        mask_ref, refs = refs[0], refs[1:]
    where_ref, act_ref, weights_ref = refs[:3]
    if kind == "first":
        cot_far, hidden_far, grad_ref, piece_ref, low_ref, act_ref = refs[3:9]
        hidden_ref, up_acc, down_acc, hidden_sems, cot_ref, cot_sems, act_sems = refs[9:]
    elif kind == "middle":
        low_ref, sofar_ref, hidden_far, grad_ref, piece_ref = refs[3:8]
        hidden_ref, up_acc, down_acc, hidden_sems = refs[8:]
    else:
        low_ref, sofar_ref, gain_ref, entropy_ref, cot_far, second_far, att_far, wo_far = refs[3:11]
        hidden_far, gsec_far, piece_ref, gatt_ref, gout_ref = refs[11:16]
        hidden_ref, up_acc, down_acc, hidden_sems, cot_ref, cot_sems = refs[16:22]
        second_ref, second_sems, att_ref, att_sems, gsec_ref, gsec_sems = refs[22:28]
        wo_ref, wo_low_ref, wo_sem, out_acc, gain_acc, column_ref, sum_ref = refs[28:]
    rows, width = act_ref.shape
    tiles = rows // tile
    hidden_out = Copies(hidden_ref, hidden_far, hidden_sems, tile)
    ins = []
    if kind == "first":
        ins = [Copies(cot_far, cot_ref, cot_sems, tile), Copies(refs[1], act_ref, act_sems, tile)]
    if kind == "last":
        ins = [
            Copies(second_far, second_ref, second_sems, tile),
            Copies(cot_far, cot_ref, cot_sems, tile),
            Copies(att_far, att_ref, att_sems, tile),
        ]
        gsec_out = Copies(gsec_ref, gsec_far, gsec_sems, tile)
    for i in range(tiles):
        for copies in ins:
            copies.start(i)
        if kind == "last" and i == 0:
            wo_copy = pltpu.make_async_copy(wo_far, wo_ref, wo_sem)
            wo_copy.start()
    up_acc[...] = jnp.zeros_like(up_acc)
    down_acc[...] = jnp.zeros_like(down_acc)
    if kind == "last":
        out_acc[...] = jnp.zeros_like(out_acc)
        gain_acc[...] = jnp.zeros_like(gain_acc)
        wo_copy.wait()
        wo_low_ref[...] = wo_ref[...].astype(BF16)

    def multiply(i):
        at = pl.ds(pl.multiple_of(i * tile, tile), tile)
        if kind == "first":
            low_ref[at, :] = cot_ref[at, :].astype(BF16)
        hidden, grad = quarter_math(act_ref[at, :], low_ref[at, :], weights_ref, up_acc, down_acc)
        hidden_ref[at, :] = hidden
        if kind == "first":
            grad_ref[at, :] = grad
        elif kind == "middle":
            grad_ref[at, :] = sofar_ref[at, :] + grad
        else:
            sum_ref[i % 2] = sofar_ref[at, :] + grad

    def settle(i):
        at = pl.ds(pl.multiple_of(i * tile, tile), tile)
        grad = sum_ref[i % 2]
        unit, inverse = normalize(second_ref[at, :])
        gain_acc[...] += jnp.sum(grad * unit, axis=0, keepdims=True)
        grad_second = cot_ref[at, :] + norm_grad(grad, unit, inverse, gain_ref[...])
        gsec_ref[at, :] = grad_second
        second_low = grad_second.astype(BF16)
        gatt_ref[at, :] = dot_nt(second_low, wo_low_ref[...]).astype(BF16)
        out_acc[...] += dot_tn(att_ref[at, :], second_low)

    def body(i, _):
        for copies in ins:
            copies.wait(i - 1 if kind == "last" else i)
        if kind == "last":
            settle(i - 1)
        multiply(i)
        if kind == "last":
            gsec_out.start(i - 1)
        hidden_out.start(i)
        return 0

    if kind == "last":
        multiply(0)
        hidden_out.start(0)
        lax.fori_loop(1, tiles, body, 0)
        for copies in ins:
            copies.wait(tiles - 1)
        settle(tiles - 1)
        gsec_out.start(tiles - 1)
    else:
        lax.fori_loop(0, tiles, body, 0)
    size = width // piece_ref.shape[0]
    spread(piece_ref.at[:, :size], up_acc, where_ref[0], slice(None))
    spread(piece_ref.at[:, size : 2 * size], down_acc, where_ref[0], slice(None))
    if tally:
        shape = (TALLY_ROWS, weights_ref.shape[2])
        mine = lax.broadcasted_iota(jnp.int32, shape, 1) == where_ref[3]
        count = jnp.sum(mask_ref[...].astype(F32), axis=1, keepdims=True)
        row = jnp.where(mine, jnp.broadcast_to(count, shape), 0.0).astype(BF16)
        for r in range(piece_ref.shape[0]):
            piece_ref[r, 2 * size :, :] = row
    if kind == "last":
        spread(gout_ref, out_acc, where_ref[2], slice(0, width))
        half = (LANES // 2, width)
        column_ref[...] = jnp.concatenate(
            [jnp.broadcast_to(gain_acc[...], half), jnp.broadcast_to(entropy_ref[...], half)], axis=0
        ).T
        spread(gout_ref, column_ref, where_ref[2], slice(width, width + LANES))
    for i in range(tiles):
        hidden_out.wait(i)
        if kind == "last":
            gsec_out.wait(i)


def feed_quarter(
    kind, where, act, weights, cot, sofar=None, extra=None, mask_row=None, row_chunks=1, out_chunks=1, tile=512
):
    rows, width = act.shape
    units = weights.shape[2]
    tiles = rows // tile
    smem = pl.BlockSpec(memory_space=pltpu.SMEM)
    vmem = pl.BlockSpec(memory_space=pltpu.VMEM)
    hbm = pl.BlockSpec(memory_space=pltpu.HBM)
    tally = mask_row is not None
    size = 2 * (width // row_chunks) + (TALLY_ROWS if tally else 0)
    piece = near_shape((row_chunks, size, units), BF16)
    low = near_shape((rows, width), BF16)
    full = near_shape((rows, width), F32)
    hidden = far_shape((rows, units), BF16)
    sems = pltpu.SemaphoreType.DMA((tiles,))
    low_buffer, full_buffer = pltpu.VMEM((rows, width), BF16), pltpu.VMEM((rows, width), F32)
    square = pltpu.VMEM((width, width), F32)
    scratch = [pltpu.VMEM((rows, units), BF16), square, square, sems]
    if kind == "first":
        operands = (far(cot),)
        in_specs = [hbm]
        out_shape, out_specs = [hidden, full, piece, low, low], [hbm] + [vmem] * 4
        scratch = scratch + [full_buffer, sems, sems]
        limit = 24
    elif kind == "middle":
        operands = (near(cot), near(sofar))
        in_specs = [vmem] * 2
        out_shape, out_specs = [hidden, full, piece], [hbm] + [vmem] * 2
        limit = 18
    else:
        full_cot, second, att, w_out, gain, entropy = extra
        operands = (near(cot), near(sofar), gain, entropy, far(full_cot), far(second), far(att), far(w_out))
        in_specs = [vmem] * 4 + [hbm] * 4
        out_piece = near_shape((out_chunks, width // out_chunks, width + LANES), BF16)
        out_shape = [hidden, far_shape((rows, width), F32), piece, low, out_piece]
        out_specs = [hbm] * 2 + [vmem] * 3
        scratch = scratch + [full_buffer, sems, full_buffer, sems, low_buffer, sems, full_buffer, sems]
        scratch = scratch + [square, pltpu.VMEM((width, width), BF16), pltpu.SemaphoreType.DMA]
        scratch = scratch + [square, pltpu.VMEM((1, width), F32), pltpu.VMEM((width, LANES), F32)]
        scratch = scratch + [pltpu.VMEM((2, tile, width), F32)]
        limit = 32
    return pl.pallas_call(
        functools.partial(quarter_kernel, kind=kind, tile=tile, tally=tally),
        in_specs=([vmem] if tally else []) + [smem, hbm if kind == "first" else vmem, vmem] + in_specs,
        out_specs=out_specs,
        out_shape=out_shape,
        scratch_shapes=scratch,
        compiler_params=params(limit),
        cost_estimate=cost(9),
        name="feed_" + kind,
    )(
        *([mask_row] if tally else []), where, far(act) if kind == "first" else near(act), near(weights), *operands
    )


def output_kernel(second_ref, *refs):
    out_ref = refs[-1]
    count = (len(refs) - 1) // 2
    total = second_ref[...]
    for hidden_ref, weights_ref in zip(refs[:count], refs[count : 2 * count]):
        total = total + dot(hidden_ref[...], weights_ref[0])
    out_ref[...] = total


def layer_output(second, hidden, weights, tile=512):
    rows, width = second.shape
    units = hidden[0].shape[1]
    down = pl.BlockSpec((1, units, width), lambda *_: (1, 0, 0), pipeline_mode=pl.Buffered(1))
    return pl.pallas_call(
        output_kernel,
        grid=(rows // tile,),
        in_specs=[rows_of(tile, width)] + [rows_of(tile, units)] * len(hidden) + [down] * len(hidden),
        out_specs=rows_of(tile, width),
        out_shape=far_shape((rows, width), F32),
        compiler_params=params(16),
        cost_estimate=cost(8),
        name="layer_output",
    )(near(second), *[far(array) for array in hidden], *[near(array) for array in weights])


def head_kernel(*refs, count):
    where_ref, pen_ref, act_ref = refs[:3]
    groups = [refs[3 + 4 * g : 7 + 4 * g] for g in range(count)]
    share_ref, log_ref, sum_ref, w_ref, perm_ref, mask_ref, out_ref, tally_ref = refs[3 + 4 * count : 11 + 4 * count]
    piece_ref, gsum_ref, total_ref, glog_ref, acc_ref = refs[11 + 4 * count :]
    block_total = jnp.sum(tally_ref[...].astype(F32), axis=1, keepdims=True)
    block_total = jnp.sum(block_total, axis=0, keepdims=True)
    total_ref[...] = jnp.broadcast_to(block_total, total_ref.shape)
    coef = pen_ref[0] / (HEADS * block_total)
    blocks, width = sum_ref.shape
    cols = acc_ref.shape[1]
    wide = 2 * blocks
    first, position = lane_tiles(blocks)
    hot = position == down_rows(perm_ref[...], wide)
    weight = coef * down_rows(mask_ref[...], wide)
    act = act_ref[...]
    for g, group in enumerate(groups):
        for index in range(3):
            acc_ref[...] = dot_tn(act, group[index][...])
            at = index * width + g * cols
            spread(piece_ref, acc_ref, where_ref[2], slice(at, at + cols))
        for pair in range(cols // wide):
            at = g * cols + pair * wide
            span = slice(at, at + wide)
            plan = share_ref[2 * ITERS - 1, :, span]
            gch = segment_sum(group[3][:, pair * wide : (pair + 1) * wide], first)
            grad = plan * (jnp.where(hot, blocks * gch, 0.0) - weight * (log_ref[:, span] + 1.0))
            for level in range(2 * ITERS - 1, -1, -1):
                if level % 2:
                    total = jnp.sum(grad, axis=0, keepdims=True)
                else:
                    total = segment_sum(grad, first)
                grad = grad - share_ref[level, :, span] * total
            glog_ref[:, span] = grad
    for g in range(count):
        at = slice(g * cols, (g + 1) * cols)
        acc_ref[...] = lax.dot_general(
            sum_ref[...], glog_ref[:, at], TN, precision=HIGHEST, preferred_element_type=F32
        )
        spread(piece_ref, acc_ref, where_ref[2], slice(3 * width + g * cols, 3 * width + (g + 1) * cols))
    gsum_ref[...] = lax.dot_general(glog_ref[...], w_ref[...], NT, precision=HIGHEST, preferred_element_type=F32)
    piece_ref[:, :, 4 * width :] = out_ref[...]


def head_grads(
    where, pen_weight, act, groups, shares, plan_log, sums, w_sort, perm_row, mask_row, out_piece, tallies, chunks
):
    rows, width = act.shape
    blocks = sums.shape[0]
    cols = groups[0][0].shape[1]
    smem = pl.BlockSpec(memory_space=pltpu.SMEM)
    vmem = pl.BlockSpec(memory_space=pltpu.VMEM)
    flat = [near(array) for group in groups for array in group]
    piece = (chunks, width // chunks, 4 * width + out_piece.shape[2])
    return pl.pallas_call(
        functools.partial(head_kernel, count=len(groups)),
        in_specs=[smem] * 2 + [vmem] * (9 + len(flat)),
        out_specs=[vmem] * 3,
        out_shape=[near_shape(piece, BF16), near_shape((blocks, width), F32), near_shape((1, LANES), F32)],
        scratch_shapes=[pltpu.VMEM((blocks, width), F32), pltpu.VMEM((width, cols), F32)],
        compiler_params=params(14),
        cost_estimate=cost(6),
        name="head_grads",
    )(
        where, pen_weight, near(act), *flat, near(shares), near(plan_log), near(sums), near(w_sort), perm_row, mask_row,
        near(out_piece), tallies,
    )


def input_kernel(*refs):
    count = (len(refs) - 9) // 3
    groups = [refs[3 * g : 3 * g + 3] for g in range(count)]
    gsum_ref, x_ref, gsec_ref, gain_ref, wq_ref, wk_ref, wv_ref, out_ref, w_ref = refs[3 * count :]

    @pl.when(pl.program_id(0) == 0)
    def _():
        for which, ref in enumerate((wq_ref, wk_ref, wv_ref)):
            w_ref[which] = ref[...].astype(BF16)

    rows, width = x_ref.shape
    grad = jnp.zeros((rows, width), F32)
    for g, group in enumerate(groups):
        for which, ref in enumerate(group):
            cols = ref.shape[1]
            grad = grad + dot_nt(ref[...], w_ref[which, :, g * cols : (g + 1) * cols])
    grad = (grad.reshape(rows // BLOCK, BLOCK, width) + gsum_ref[...][:, None, :]).reshape(rows, width)
    unit, inverse = normalize(x_ref[...])
    out_ref[...] = gsec_ref[...] + norm_grad(grad, unit, inverse, gain_ref[...])


def input_grad(groups, gsum, x, gsec, gain, wq, wk, wv, tile=512):
    rows, width = x.shape
    weight = pl.BlockSpec((width, width), lambda *_: (0, 0), pipeline_mode=pl.Buffered(1))
    flat = [array for group in groups for array in group]
    return pl.pallas_call(
        input_kernel,
        grid=(rows // tile,),
        in_specs=[rows_of(tile, array.shape[1]) for array in flat]
        + [rows_of(tile // BLOCK, width)]
        + [rows_of(tile, width)] * 2
        + [whole((1, width))]
        + [weight] * 3,
        out_specs=rows_of(tile, width),
        out_shape=far_shape((rows, width), F32),
        scratch_shapes=[pltpu.VMEM((3, width, width), BF16)],
        compiler_params=params(20),
        cost_estimate=cost(10),
        name="input_grad",
    )(*[near(array) for array in flat], gsum, far(x), far(gsec), gain, far(wq), far(wk), far(wv))


def pack_kernel(core_ref, up_ref, down_ref, mine_ref):
    mine_ref[0] = up_ref[...].astype(BF16)
    mine_ref[1] = down_ref[...].astype(BF16)


def pack_weights(core, w_up, w_down):
    width, units = w_up.shape
    half = units // 2
    shape = (2, width, half)
    return pl.pallas_call(
        pack_kernel,
        grid_spec=pltpu.PrefetchScalarGridSpec(
            num_scalar_prefetch=1,
            grid=(1,),
            in_specs=[
                pl.BlockSpec((width, half), lambda step, core: (0, core[0])),
                pl.BlockSpec((half, width), lambda step, core: (core[0], 0)),
            ],
            out_specs=whole(shape),
        ),
        out_shape=near_shape(shape, BF16),
        compiler_params=params(12),
        cost_estimate=cost(2),
        name="pack_weights",
    )(core, far(w_up), far(w_down))


def finish_feed_kernel(*refs):
    where_ref, parts = refs[0], refs[1:-3]
    up_ref, down_ref, turn_ref = refs[-3:]
    some, size, units = parts[0].shape
    size = size // 2
    half = len(parts) // 2
    for flip in range(2):
        column = pl.multiple_of((where_ref[1] ^ flip) * units, units)
        for n, ref in enumerate(parts[flip * half : (flip + 1) * half]):
            for r in range(some):
                at = pl.multiple_of(((n * some + r) ^ where_ref[0]) * size, size)
                up_ref[pl.ds(at, size), pl.ds(column, units)] = ref[r, :size].astype(F32)
                turn_ref[pl.ds(at, size), :] = ref[r, size:].astype(F32)
        down_ref[pl.ds(column, units), :] = turn_ref[...].T


def finish_feed(where, parts):
    some, size, units = parts[0].shape
    width = len(parts) // 2 * some * size // 2
    vmem = pl.BlockSpec(memory_space=pltpu.VMEM)
    return pl.pallas_call(
        finish_feed_kernel,
        in_specs=[pl.BlockSpec(memory_space=pltpu.SMEM)] + [vmem] * len(parts),
        out_specs=[vmem, vmem],
        out_shape=[far_shape((width, 2 * units), F32), far_shape((2 * units, width), F32)],
        scratch_shapes=[pltpu.VMEM((width, units), F32)],
        compiler_params=params(16),
        cost_estimate=cost(3),
        name="finish_feed",
    )(where, *parts)


def finish_kernel(*refs):
    where_ref, parts = refs[0], refs[1:-22]
    weights = refs[-22:-18]
    gain_ref, total_ref = refs[-18:-16]
    fars = refs[-16:-11]
    gain_one_ref, gain_two_ref, penalty_ref = refs[-11:-8]
    nears = refs[-8:-3]
    one_ref, two_ref, sems = refs[-3:]
    width = gain_ref.shape[1]
    some, size = parts[0].shape[:2]
    total = jnp.zeros((width, LANES), F32)
    copies = []
    for index, near_ref in enumerate(nears):
        for n, part_ref in enumerate(parts):
            for r in range(some):
                rows = pl.ds(pl.multiple_of(((n * some + r) ^ where_ref[2]) * size, size), size)
                near_ref[rows, :] = part_ref[r, :, index * width : (index + 1) * width].astype(F32)
                if index == 0:
                    two_ref[rows, :] = part_ref[r, :, 5 * width :].astype(F32)
        copies.append(pltpu.make_async_copy(near_ref, fars[index], sems.at[index]))
        copies[-1].start()
    for at in range(0, width, LANES):
        span = slice(at, at + LANES)
        for grad, weight in zip(nears[:3], weights[:3]):
            total = total + grad[:, span] * weight[:, span].astype(BF16).astype(F32)
        total = total + nears[3][:, span] * weights[3][:, span]
    one_ref[...] = total
    gain_one_ref[...] = jnp.sum(one_ref[...].T, axis=0, keepdims=True) / gain_ref[...]
    turned = two_ref[...].T
    gain_two_ref[...] = turned[:1, :]
    entropy = jnp.sum(turned[LANES // 2 : LANES // 2 + 1, :], axis=1, keepdims=True)
    penalty_ref[...] = entropy / (HEADS * total_ref[:, :1])
    for copy in copies:
        copy.wait()


def finish(where, parts, wq, wk, wv, ws, gain, total):
    width = wq.shape[0]
    vmem = pl.BlockSpec(memory_space=pltpu.VMEM)
    hbm = pl.BlockSpec(memory_space=pltpu.HBM)
    square = far_shape((width, width), F32)
    row = shape_of((1, width), F32)
    return pl.pallas_call(
        finish_kernel,
        in_specs=[pl.BlockSpec(memory_space=pltpu.SMEM)] + [vmem] * (6 + len(parts)),
        out_specs=[hbm] * 5 + [vmem] * 3,
        out_shape=[square] * 5 + [row] * 2 + [shape_of((1, 1), F32)],
        scratch_shapes=[pltpu.VMEM((width, width), F32)] * 5
        + [pltpu.VMEM((width, LANES), F32)] * 2
        + [pltpu.SemaphoreType.DMA((5,))],
        compiler_params=params(16),
        cost_estimate=cost(5),
        name="finish",
    )(where, *parts, near(wq), near(wk), near(wv), near(ws), gain, total)


MP, CORE, X, Z_LOW, Z_HIGH = 1, 2, 4, 8, 16
CORE_STEP = ((CORE,), (CORE,))
FEED_STEPS = ((X,), (Z_LOW, Z_HIGH, Z_LOW + Z_HIGH))
HEAD_STEPS = ((CORE,), (MP, X, MP + X), (Z_LOW, Z_HIGH, Z_LOW + Z_HIGH))


def swap(array, flip):
    count = lax.axis_size("batch") * lax.axis_size("mp")
    return lax.ppermute(array, ("batch", "mp"), [(i, i ^ flip) for i in range(count)])


def place(steps, index):
    result = jnp.int32(0)
    for step in steps:
        for bit in reversed(step[: (len(step) + 1).bit_length() - 1]):
            result = 2 * result + ((index & bit) > 0).astype(jnp.int32)
    return result


def add_low(first, *others):
    total = first.astype(F32)
    for array in others:
        total = total + array.astype(F32)
    return total.astype(BF16)


class Walk:
    def __init__(self, pieces, steps):
        self.pieces = pieces
        self.down = list(steps)
        self.up = list(reversed(steps))
        self.parts, self.arrived = None, []

    def added(self, plan, count):
        pieces = self.pieces + [plan.after(array) for array in self.arrived]
        self.arrived = []
        size = pieces[0].shape[0] // count
        if len(pieces) == 1 and count == 1:
            return pieces
        return [
            add_low(*[piece[n * size : (n + 1) * size] for piece in pieces]) if len(pieces) > 1
            else pieces[0][n * size : (n + 1) * size]
            for n in range(count)
        ]

    def reduce(self, plan):
        flips = self.down.pop(0)
        parts = self.added(plan, len(flips) + 1)
        self.arrived = [swap(plan.after(part), flip) for part, flip in zip(parts[1:], flips)]
        self.pieces = parts[:1]
        return self.arrived

    def reduced(self, plan):
        return self.added(plan, 1)[0]

    def gather(self, plan, value):
        flips = self.up.pop(0)
        self.parts = [value]
        mine = plan.after(value)
        self.arrived = [swap(mine, flip) for flip in flips]
        return self.arrived

    def gathered(self, plan):
        parts = self.parts + [plan.after(array) for array in self.arrived]
        self.arrived = []
        return parts


class Schedule:
    def __init__(self):
        self.pending, self.launched, self.done = [], [], None

    def after(self, array):
        return lax.optimization_barrier((array, self.done))[0]

    def enter(self, small):
        tied = lax.optimization_barrier((small, *self.pending))[0]
        self.pending, self.launched = self.launched, []
        return tied

    def leave(self, *arrays):
        self.pending.extend(arrays)
        self.done = arrays[0]

    def launch(self, *arrays):
        for array in arrays:
            self.launched.extend(array if isinstance(array, list) else [array])


def local_small(
    inputs, cotangent, block_perm, block_mask, pen_weight, w_query, w_key, w_value, w_out, w_sort,
    gain_one, gain_two, w_up, w_down,
):
    _, rows, width = inputs.shape
    x = inputs.reshape(rows, width)
    cot = cotangent.reshape(rows, width)
    perm = block_perm.reshape(-1)
    mask = block_mask.reshape(-1)
    perm_row = block_perm.reshape(1, -1)
    mask_row = block_mask.reshape(1, -1)
    gain_one_row = gain_one.reshape(1, width)
    gain_two_row = gain_two.reshape(1, width)
    batch, mp = lax.axis_index("batch"), lax.axis_index("mp")
    core = batch & 1
    index = batch * 2 + mp
    where = jnp.stack([place(FEED_STEPS, index), core, place(HEAD_STEPS, index), index])
    row_chunks, out_chunks = 8, 32
    plan = Schedule()

    count = jnp.broadcast_to(jnp.sum(mask.astype(F32)), (8, LANES))
    own_a = pack_weights(core.reshape(1), w_up, w_down)
    far_a = swap(own_a, MP)
    plan.leave(own_a)
    act_one, q, k, v, probs, att, second, act_two_far, shares, sums, plan_log, chosen, entropy, own_b = forward(
        perm, mask, (1 - core).reshape(1), perm_row, mask_row, plan.enter(gain_one_row), gain_two_row, x,
        w_query, w_key, w_value, w_sort, w_out, w_up, w_down,
    )
    plan.leave(entropy)
    plan.pending.append(far_a)

    far_b = swap(plan.after(far_a), CORE)
    plan.launch(far_b)
    hid_a, sofar, other_piece, cot_low, act_two = feed_quarter(
        "first", plan.enter(where), act_two_far, far_a, cot, mask_row=mask_row, row_chunks=row_chunks
    )
    plan.leave(other_piece)

    hid_b, sofar, piece = feed_quarter(
        "middle", plan.enter(where), act_two, far_b, cot_low, sofar, mask_row=mask_row, row_chunks=row_chunks
    )
    plan.leave(piece)

    arrived = swap(plan.after(piece), CORE)
    plan.launch(arrived)
    hid_c, sofar, piece = feed_quarter(
        "middle", plan.enter(where), act_two, own_b, cot_low, sofar, row_chunks=row_chunks
    )
    plan.leave(piece)

    other = Walk([other_piece, plan.after(arrived)], FEED_STEPS)
    arrived = swap(plan.after(piece), CORE)
    plan.launch(arrived, other.reduce(plan))
    extra = (cot, second, att, w_out, gain_two_row, entropy)
    hid_d, grad_second, piece, grad_att, out_piece = feed_quarter(
        "last", plan.enter(where), act_two, own_a, cot_low, sofar, extra, None, row_chunks, out_chunks
    )
    plan.leave(grad_att)

    own = Walk([piece, plan.after(arrived)], FEED_STEPS)
    plan.launch(own.reduce(plan), other.reduce(plan))
    groups = [attend_back(plan.enter(perm), q, grad_att, probs, k, v, chosen, 0)]
    plan.leave(groups[0][3])

    other_sum = other.reduced(plan)
    crossed = swap(plan.after(other_sum), MP)
    plan.launch(crossed, own.reduce(plan))
    plan.pending.extend(own.pieces)
    groups.append(attend_back(plan.enter(perm), q, grad_att, probs, k, v, chosen, 1))
    plan.leave(groups[1][3])

    crossed = plan.after(crossed)
    rows_fed = own.pieces[0].shape[1]
    tallies = jnp.concatenate([other_sum[0, rows_fed:], crossed[0, rows_fed:]], axis=0)
    tallies = tallies.reshape(2, TALLY_ROWS, -1)[:, 0]
    own.pieces.append(crossed[:, :rows_fed])
    value = own.reduced(plan)
    plan.launch(own.gather(plan, value))
    plan.pending.append(value)
    piece, gsum, block_total = head_grads(
        plan.enter(where), pen_weight, act_one, groups, shares, plan_log, sums, w_sort, perm_row, mask_row, out_piece,
        tallies, out_chunks,
    )
    plan.leave(gsum)

    head = Walk([piece], HEAD_STEPS)
    plan.pending.extend(head.reduce(plan))
    plan.launch(head.reduce(plan))
    plan.pending.extend(head.pieces)
    grad_input = input_grad(
        [group[:3] for group in groups], gsum, x, grad_second, plan.enter(gain_one_row), w_query, w_key, w_value
    )
    plan.leave(grad_input)

    head.reduce(plan)
    own.gather(plan, jnp.concatenate(own.gathered(plan), axis=0))
    head.gather(plan, head.reduced(plan))
    value = jnp.concatenate(head.gathered(plan), axis=0)
    plan.pending.append(value)
    head.gather(plan, value)
    quarters = (far_a, far_b, own_b, own_a)
    output = layer_output(plan.enter(second), (hid_a, hid_b, hid_c, hid_d), quarters)
    plan.leave(output)

    parts = own.parts + own.arrived
    grad_up, grad_down = finish_feed(plan.enter(where), parts + [swap(part, CORE) for part in parts])
    plan.leave(grad_up)
    parts = head.gathered(plan)
    parts = parts + [swap(part, CORE) for part in parts]
    grad_query, grad_key, grad_value, grad_sort, grad_out, grad_gain_one, grad_gain_two, penalty = finish(
        where, parts, w_query, w_key, w_value, w_sort, gain_one_row, block_total
    )
    return (
        output.reshape(inputs.shape),
        penalty.reshape(1),
        grad_input.reshape(inputs.shape),
        grad_query,
        grad_key,
        grad_value,
        grad_out,
        grad_sort,
        grad_gain_one.reshape(width),
        grad_gain_two.reshape(width),
        grad_up,
        grad_down,
    )


def local_any(
    inputs, cotangent, block_perm, block_mask, pen_weight, w_query, w_key, w_value, w_out, w_sort,
    gain_one, gain_two, w_up, w_down,
):
    both = ("batch", "mp")
    _, rows, width = inputs.shape
    x = inputs.reshape(rows, width)
    cot = cotangent.reshape(rows, width)
    perm = block_perm.reshape(-1)
    mask = block_mask.reshape(-1)
    perm_row = block_perm.reshape(1, -1)
    mask_row = block_mask.reshape(1, -1)
    gain_one_row = gain_one.reshape(1, width)
    gain_two_row = gain_two.reshape(1, width)
    where = jnp.zeros((4,), jnp.int32)
    up_all = lax.all_gather(w_up.astype(BF16), "mp", axis=1, tiled=True)
    down_all = lax.all_gather(w_down.astype(BF16), "mp", axis=0, tiled=True)
    quarters = [
        jnp.stack([up_all[:, at : at + width], down_all[at : at + width]])
        for at in range(0, up_all.shape[1], width)
    ]
    act_one, q, k, v, probs, att, second, act_two_far, shares, sums, plan_log, chosen, entropy = forward(
        perm, mask, jnp.zeros((1,), jnp.int32), perm_row, mask_row, gain_one_row, gain_two_row, x,
        w_query, w_key, w_value, w_sort, w_out, w_query, w_query,
    )[:-1]
    tallies = jnp.broadcast_to(lax.psum(jnp.sum(mask_row).astype(F32), both) / width, (1, width))
    hidden, parts = [], []
    low, sofar = cot, None
    for index, weights in enumerate(quarters):
        if index == 0:
            hid, sofar, piece, low, act_two = feed_quarter("first", where, act_two_far, weights, low)
        elif index < len(quarters) - 1:
            hid, sofar, piece = feed_quarter("middle", where, act_two, weights, low, sofar)
        else:
            extra = (cot, second, att, w_out, gain_two_row, entropy)
            hid, grad_second, piece, grad_att, extra = feed_quarter(
                "last", where, act_two, weights, low, sofar, extra
            )
        hidden.append(hid)
        parts.append(piece[0])
    groups = [
        attend_back(perm, q, grad_att, probs, k, v, chosen, group) for group in range(width // GROUP_WIDTH)
    ]
    piece, gsum, block_total = head_grads(
        where, pen_weight, act_one, groups, shares, plan_log, sums, w_sort, perm_row, mask_row, extra, tallies, 1
    )
    grad_input = input_grad(
        [group[:3] for group in groups], gsum, x, grad_second, gain_one_row, w_query, w_key, w_value
    )
    output = layer_output(second, hidden, quarters)

    parts = jnp.concatenate(parts, axis=1).reshape(2, width, -1)
    parts = lax.psum(lax.psum_scatter(parts, "mp", scatter_dimension=2, tiled=True), "batch").astype(F32)
    grad_up, grad_down = parts[0], parts[1].T
    piece = lax.psum(piece, both)
    grad_query, grad_key, grad_value, grad_sort, grad_out, grad_gain_one, grad_gain_two, penalty = finish(
        where, [piece], w_query, w_key, w_value, w_sort, gain_one_row, block_total
    )
    return (
        output.reshape(inputs.shape),
        penalty.reshape(1),
        grad_input.reshape(inputs.shape),
        grad_query,
        grad_key,
        grad_value,
        grad_out,
        grad_sort,
        grad_gain_one.reshape(width),
        grad_gain_two.reshape(width),
        grad_up,
        grad_down,
    )


def solution(mesh):
    tokens = P(("batch", "mp"), None, None)
    blocks = P(("batch", "mp"), None)
    small = mesh.shape["batch"] == 16 and mesh.shape["mp"] == 2
    return jax.shard_map(
        local_small if small else local_any,
        mesh=mesh,
        in_specs=(tokens, tokens, blocks, blocks) + (P(),) * 8 + (P(None, "mp"), P("mp", None)),
        out_specs=(tokens, P(), tokens) + (P(),) * 7 + (P(None, "mp"), P("mp", None)),
        check_vma=False,
    )
```

```python
import functools

import jax
import jax.numpy as jnp
from jax import lax
from jax.experimental import pallas as pl
from jax.experimental.pallas import tpu as pltpu
from jax.sharding import PartitionSpec as P

HEADS = 8
HEAD_DIM = 64
BLOCK = 32
ITERS = 8
GROUP = 4
GROUP_WIDTH = GROUP * HEAD_DIM
GROUP_ROWS = GROUP * BLOCK
EPSILON = 1e-05
FACTOR = HEAD_DIM ** (-0.5)
HIGHEST = lax.Precision.HIGHEST
F32 = jnp.float32
BF16 = jnp.bfloat16
NT = (((1,), (1,)), ((), ()))
TN = (((0,), (0,)), ((), ()))
MIB = 1024 * 1024
LANES = 128
TALLY_ROWS = 16


def dot(left, right):
    return jnp.dot(left, right, preferred_element_type=F32)


def dot_nt(left, right):
    return lax.dot_general(left, right, NT, preferred_element_type=F32)


def dot_tn(left, right):
    return lax.dot_general(left, right, TN, preferred_element_type=F32)


def shape_of(dims, dtype):
    return jax.ShapeDtypeStruct(dims, dtype)


def whole(dims):
    return pl.BlockSpec(dims, lambda *_: (0,) * len(dims))


def once(dims):
    return pl.BlockSpec(dims, lambda *_: (0,) * len(dims), pipeline_mode=pl.Buffered(1))


def rows_of(size, width):
    return pl.BlockSpec((size, width), lambda step, *_: (step, 0))


def params(mib):
    return pltpu.CompilerParams(vmem_limit_bytes=mib * MIB)


def far(array):
    return pltpu.with_memory_space_constraint(array, pltpu.HBM)


def near(array):
    return pltpu.with_memory_space_constraint(array, pltpu.VMEM)


def near_shape(dims, dtype):
    return pltpu.VMEM(dims, dtype)


def far_shape(dims, dtype):
    return pltpu.HBM(dims, dtype)


def cost(micros):
    return pl.CostEstimate(flops=int(micros * 1150000000), bytes_accessed=0, transcendentals=0)


def normalize(values):
    center = values - jnp.mean(values, axis=-1, keepdims=True)
    inverse = lax.rsqrt(jnp.mean(center * center, axis=-1, keepdims=True) + EPSILON)
    return center * inverse, inverse


def norm_grad(grad_rows, unit_rows, inverse, gain):
    scaled_rows = grad_rows * gain
    return inverse * (
        scaled_rows
        - jnp.mean(scaled_rows, axis=-1, keepdims=True)
        - unit_rows * jnp.mean(scaled_rows * unit_rows, axis=-1, keepdims=True)
    )


def segment_sum(tile, first):
    left = jnp.sum(jnp.where(first, tile, 0.0), axis=1, keepdims=True)
    right = jnp.sum(jnp.where(first, 0.0, tile), axis=1, keepdims=True)
    return jnp.where(first, left, right)


def segment_max(tile, first):
    left = jnp.max(jnp.where(first, tile, -jnp.inf), axis=1, keepdims=True)
    right = jnp.max(jnp.where(first, -jnp.inf, tile), axis=1, keepdims=True)
    return jnp.where(first, left, right)


def head_masks(rows):
    lane = lax.broadcasted_iota(jnp.int32, (rows, GROUP_WIDTH), 1)
    return [(lane >= h * HEAD_DIM) & (lane < (h + 1) * HEAD_DIM) for h in range(GROUP)]


def expand(rows, masks):
    zero = jnp.zeros_like(rows)
    return jnp.concatenate([jnp.where(mask, rows, zero) for mask in masks], axis=0)


def fold(rows, masks):
    parts = [rows[h * BLOCK : (h + 1) * BLOCK] for h in range(GROUP)]
    result = parts[GROUP - 1]
    for h in range(GROUP - 1):
        result = jnp.where(masks[h], parts[h], result)
    return result


def lane_tiles(blocks):
    lane = lax.broadcasted_iota(jnp.int32, (blocks, 2 * blocks), 1)
    return lane < blocks, jnp.where(lane < blocks, lane, lane - blocks).astype(F32)


def down_rows(row, wide):
    return jnp.broadcast_to(row.astype(F32), (wide, row.shape[1])).T


def balance_plans(logits, perm_row, mask_row, share_ref, log_ref, chosen_ref, entropy_ref):
    blocks = logits.shape[0]
    wide = 2 * blocks
    first, position = lane_tiles(blocks)
    hot = position == down_rows(perm_row, wide)
    real = down_rows(mask_row, wide) > 0.0
    for pair in range(logits.shape[1] // wide):
        span = slice(pair * wide, (pair + 1) * wide)
        tile = logits[:, span]
        for step in range(ITERS):
            top = segment_max(tile, first)
            powers = jnp.exp(tile - top)
            total = segment_sum(powers, first)
            tile = tile - (top + jnp.log(total))
            share_ref[2 * step, :, span] = powers * (1.0 / total)
            top = jnp.max(tile, axis=0, keepdims=True)
            powers = jnp.exp(tile - top)
            total = jnp.sum(powers, axis=0, keepdims=True)
            tile = tile - (top + jnp.log(total))
            if step < ITERS - 1:
                share_ref[2 * step + 1, :, span] = powers * (1.0 / total)
        plan = jnp.exp(tile)
        share_ref[2 * ITERS - 1, :, span] = plan
        log_ref[:, span] = tile
        chosen_ref[:, span] = blocks * segment_sum(jnp.where(hot, plan, 0.0), first)
        entropy_ref[:, span] = -jnp.sum(jnp.where(real, plan * tile, 0.0), axis=0, keepdims=True)


def forward_kernel(
    perm_ref, mask_ref, other_ref, perm_row_ref, mask_row_ref, gain_one_ref, gain_two_ref,
    x_far, wq_far, wk_far, wv_far, ws_far, wo_far, up_far, down_far,
    act_far, q_far, k_far, v_far, probs_far, att_far, second_far, act_two_far, share_far,
    sum_ref, log_ref, chosen_ref, entropy_ref, packed_ref,
    x_ref, w_ref, w_low_ref, wo_low_ref, act_ref, q_ref, k_ref, v_ref, probs_ref, att_ref, second_ref, act_two_ref, share_ref,
    feed_ref, in_sem, out_sem, share_sem, feed_sem, *, tile,
):
    rows, width = x_ref.shape
    tiles = rows // tile

    def x_copy(i):
        at = pl.ds(pl.multiple_of(i * tile, tile), tile)
        return pltpu.make_async_copy(x_far.at[at, :], x_ref.at[at, :], in_sem.at[i])

    def w_copy(n):
        far_ref = (wq_far, wk_far, wv_far, ws_far, wo_far)[n]
        return pltpu.make_async_copy(far_ref, w_ref.at[n], in_sem.at[tiles + n])

    outs = (
        (act_ref, act_far), (q_ref, q_far), (k_ref, k_far), (v_ref, v_far),
        (probs_ref, probs_far), (att_ref, att_far), (second_ref, second_far), (act_two_ref, act_two_far),
    )
    part = 8
    some = part * BLOCK
    parts = rows // some

    def out_copy(n, i):
        near_ref, far_ref = outs[n]
        size = near_ref.shape[0] // (tiles if n < 4 else parts)
        at = pl.ds(pl.multiple_of(i * size, size), size)
        return pltpu.make_async_copy(near_ref.at[at, :], far_ref.at[at, :], out_sem.at[n, i])

    x_copy(0).start()
    for n in range(3):
        w_copy(n).start()
    for i in range(1, tiles):
        x_copy(i).start()
    w_copy(3).start()
    w_copy(4).start()
    units = packed_ref.shape[2]
    at = pl.ds(pl.multiple_of(other_ref[0] * units, units), units)
    feed_copies = [
        pltpu.make_async_copy(up_far.at[:, at], feed_ref.at[0], feed_sem.at[0]),
        pltpu.make_async_copy(down_far.at[at, :], feed_ref.at[1], feed_sem.at[1]),
    ]
    for copy in feed_copies:
        copy.start()
    for n in range(3):
        w_copy(n).wait()
        w_low_ref[:, n * width : (n + 1) * width] = w_ref[n].astype(BF16)

    def prepare(i):
        at = pl.ds(pl.multiple_of(i * tile, tile), tile)
        unit, _ = normalize(x_ref[at, :])
        act = (unit * gain_one_ref[...]).astype(BF16)
        act_ref[at, :] = act
        sums = jnp.sum(act.astype(F32).reshape(tile // BLOCK, BLOCK, width), axis=1)
        some = tile // BLOCK
        sum_ref[pl.ds(pl.multiple_of(i * some, some), some), :] = sums.astype(BF16).astype(F32)

    def project(i):
        at = pl.ds(pl.multiple_of(i * tile, tile), tile)
        act = act_ref[at, :]
        for n, ref in enumerate((q_ref, k_ref, v_ref)):
            ref[at, :] = dot(act, w_low_ref[:, n * width : (n + 1) * width]).astype(BF16)

    def project_out(i):
        for n in range(4):
            out_copy(n, i).start()

    def both(i, _):
        x_copy(i + 1).wait()
        project(i)
        prepare(i + 1)
        project_out(i)
        return 0

    x_copy(0).wait()
    prepare(0)
    lax.fori_loop(0, tiles - 2, both, 0)
    x_copy(tiles - 1).wait()
    prepare(tiles - 1)
    w_copy(3).wait()
    w_copy(4).wait()
    wo_low_ref[...] = w_ref[4].astype(BF16)
    for n, copy in enumerate(feed_copies):
        copy.wait()
        packed_ref[n] = feed_ref[n].astype(BF16)
    logits = jnp.dot(sum_ref[...], w_ref[3], precision=HIGHEST, preferred_element_type=F32)
    balance_plans(
        logits, perm_row_ref[...], mask_row_ref[...], share_ref, log_ref, chosen_ref, entropy_ref
    )
    for i in (tiles - 2, tiles - 1):
        project(i)
    for i in (tiles - 2, tiles - 1):
        project_out(i)
    pltpu.make_async_copy(share_ref, share_far, share_sem).start()

    masks = head_masks(BLOCK)
    key_row = lax.broadcasted_iota(jnp.int32, (BLOCK, GROUP_ROWS), 0)
    query_row = lax.broadcasted_iota(jnp.int32, (BLOCK, GROUP_ROWS), 1) % BLOCK
    causal = key_row <= query_row

    def attend(j):
        for b in range(part):
            block = j * part + b
            partner = perm_ref[block]
            usable = (partner < block) & (mask_ref[partner] > 0)
            own_at = pl.ds(pl.multiple_of(block * BLOCK, BLOCK), BLOCK)
            far_at = pl.ds(pl.multiple_of(partner * BLOCK, BLOCK), BLOCK)
            probs_at = pl.ds(pl.multiple_of(block * 2 * BLOCK, 2 * BLOCK), 2 * BLOCK)
            chosen_row = chosen_ref[pl.ds(block, 1), :]
            for g in range(width // GROUP_WIDTH):
                lanes = slice(g * GROUP_WIDTH, (g + 1) * GROUP_WIDTH)
                queries = expand(q_ref[own_at, lanes], masks)
                keys = jnp.concatenate([k_ref[own_at, lanes], k_ref[far_at, lanes]], axis=0)
                scores = dot_nt(keys, queries) * FACTOR
                own = jnp.where(causal, scores[:BLOCK], -1e30)
                far = jnp.where(usable, scores[BLOCK:], -1e30)
                top = jnp.maximum(jnp.max(own, axis=0, keepdims=True), jnp.max(far, axis=0, keepdims=True))
                powers = jnp.exp(jnp.concatenate([own, far], axis=0) - top)
                probs = (powers * (1.0 / jnp.sum(powers, axis=0, keepdims=True))).astype(BF16)
                probs_ref[probs_at, g * GROUP_ROWS : (g + 1) * GROUP_ROWS] = probs
                scaled = (v_ref[far_at, lanes].astype(F32) * chosen_row[:, lanes]).astype(BF16)
                values = jnp.concatenate([v_ref[own_at, lanes], scaled], axis=0)
                att_ref[own_at, lanes] = fold(dot_tn(probs, values), masks).astype(BF16)

    def settle(j):
        at = pl.ds(pl.multiple_of(j * some, some), some)
        second = x_ref[at, :] + dot(att_ref[at, :], wo_low_ref[...])
        second_ref[at, :] = second
        unit, _ = normalize(second)
        act_two_ref[at, :] = (unit * gain_two_ref[...]).astype(BF16)

    def settle_out(j):
        for n in range(4, 8):
            out_copy(n, j).start()

    def step(j, _):
        settle(j - 1)
        attend(j)
        settle_out(j - 1)
        return 0

    attend(0)
    lax.fori_loop(1, parts, step, 0)
    settle(parts - 1)
    settle_out(parts - 1)
    for n in range(8):
        for i in range(tiles if n < 4 else parts):
            out_copy(n, i).wait()
    pltpu.make_async_copy(share_ref, share_far, share_sem).wait()


def forward(perm, mask, other, perm_row, mask_row, gain_one, gain_two, x, wq, wk, wv, ws, wo, w_up, w_down, tile=512):
    rows, width = x.shape
    blocks = rows // BLOCK
    tiles = rows // tile
    smem = pl.BlockSpec(memory_space=pltpu.SMEM)
    vmem = pl.BlockSpec(memory_space=pltpu.VMEM)
    hbm = pl.BlockSpec(memory_space=pltpu.HBM)
    low = ((rows, width), BF16)
    probs = ((2 * rows, HEADS * BLOCK), BF16)
    full = ((rows, width), F32)
    share = ((2 * ITERS, blocks, width), F32)
    plan = ((blocks, width), F32)
    packed = ((2, width, width), BF16)
    return pl.pallas_call(
        functools.partial(forward_kernel, tile=tile),
        in_specs=[smem] * 3 + [vmem] * 4 + [hbm] * 8,
        out_specs=[hbm] * 9 + [vmem] * 5,
        out_shape=[far_shape(*s) for s in (low, low, low, low, probs, low, full, low, share)]
        + [near_shape(*s) for s in (plan, plan, plan)]
        + [far_shape((1, width), F32), near_shape(*packed)],
        scratch_shapes=[pltpu.VMEM(*full), pltpu.VMEM((5, width, width), F32), pltpu.VMEM((width, 3 * width), BF16)]
        + [pltpu.VMEM((width, width), BF16)]
        + [pltpu.VMEM(*s) for s in (low, low, low, low, probs, low, full, low, share)]
        + [
            pltpu.VMEM((2, width, width), F32),
            pltpu.SemaphoreType.DMA((tiles + 5,)),
            pltpu.SemaphoreType.DMA((8, rows // (8 * BLOCK))),
            pltpu.SemaphoreType.DMA,
            pltpu.SemaphoreType.DMA((2,)),
        ],
        compiler_params=params(40),
        cost_estimate=cost(25),
        name="forward",
    )(
        perm, mask, other, perm_row, mask_row, gain_one, gain_two, far(x), far(wq), far(wk), far(wv), far(ws), far(wo),
        far(w_up), far(w_down),
    )


def attend_back_kernel(
    perm_ref, chosen_ref, gatt_ref, q_ref, probs_ref, k_ref, v_ref,
    gq_ref, gk_ref, gv_ref, gch_ref,
    own_k_ref, far_k_ref, own_v_ref, far_v_ref, *, group, part,
):
    rows, width = gq_ref.shape
    parts = rows // (part * BLOCK)
    masks = head_masks(BLOCK)
    lanes = slice(group * width, (group + 1) * width)

    def body(j, _):
        for b in range(part):
            block = j * part + b
            partner = perm_ref[block]
            own_at = pl.ds(pl.multiple_of(block * BLOCK, BLOCK), BLOCK)
            far_at = pl.ds(pl.multiple_of(partner * BLOCK, BLOCK), BLOCK)
            probs_at = pl.ds(pl.multiple_of(block * 2 * BLOCK, 2 * BLOCK), 2 * BLOCK)
            queries = expand(q_ref[own_at, lanes], masks)
            grads = expand(gatt_ref[own_at, lanes], masks)
            keys = jnp.concatenate([k_ref[own_at, lanes], k_ref[far_at, lanes]], axis=0)
            far_values = v_ref[far_at, lanes].astype(F32)
            chosen = chosen_ref[pl.ds(block, 1), lanes]
            values = jnp.concatenate([v_ref[own_at, lanes], (far_values * chosen).astype(BF16)], axis=0)
            probs_low = probs_ref[probs_at, group * GROUP_ROWS : (group + 1) * GROUP_ROWS]
            probs = probs_low.astype(F32)
            grad_probs = dot_nt(values, grads)
            total = jnp.sum(probs * grad_probs, axis=0, keepdims=True)
            grad_scores = (probs * (grad_probs - total)).astype(BF16)
            grad_keys = dot(grad_scores, queries) * FACTOR
            grad_values = dot(probs_low, grads)
            gq_ref[own_at, :] = (fold(dot_tn(grad_scores, keys), masks) * FACTOR).astype(BF16)
            far_grad = grad_values[BLOCK:]
            gch_ref[pl.ds(block, 1), :] = jnp.sum(far_grad * far_values, axis=0, keepdims=True)
            own_k_ref[own_at, :] = grad_keys[:BLOCK]
            far_k_ref[far_at, :] = grad_keys[BLOCK:]
            own_v_ref[own_at, :] = grad_values[:BLOCK]
            far_v_ref[far_at, :] = far_grad * chosen
        return 0

    lax.fori_loop(0, parts, body, 0)
    gk_ref[...] = (own_k_ref[...] + far_k_ref[...]).astype(BF16)
    gv_ref[...] = (own_v_ref[...] + far_v_ref[...]).astype(BF16)


def attend_back(perm, q, gatt, probs, k, v, chosen, group, part=8):
    rows = q.shape[0]
    smem = pl.BlockSpec(memory_space=pltpu.SMEM)
    vmem = pl.BlockSpec(memory_space=pltpu.VMEM)
    low = ((rows, GROUP_WIDTH), BF16)
    full = ((rows, GROUP_WIDTH), F32)
    return pl.pallas_call(
        functools.partial(attend_back_kernel, group=group, part=part),
        in_specs=[smem] + [vmem] * 6,
        out_specs=[vmem] * 4,
        out_shape=[near_shape(*s) for s in (low, low, low, ((rows // BLOCK, GROUP_WIDTH), F32))],
        scratch_shapes=[pltpu.VMEM(*full)] * 4,
        compiler_params=params(12),
        cost_estimate=cost(10),
        name="attend_back",
    )(perm, near(chosen), near(gatt), near(q), near(probs), near(k), near(v))


def gelu_pair(up):
    square = up * up
    inner = 0.7978845608028654 * 0.044715
    half = 0.5 + 0.5 * jnp.tanh(up * (0.7978845608028654 + inner * square))
    value = up * half
    slope = half + (2.0 * value) * (1.0 - half) * (0.7978845608028654 + 3.0 * inner * square)
    return value, slope


def spread(out_ref, acc_ref, where, lanes):
    chunks, size = out_ref.shape[0], out_ref.shape[-2]
    for r in range(chunks):
        at = pl.multiple_of((r ^ where) * size, size)
        out_ref[r, :, lanes] = acc_ref[pl.ds(at, size), :].astype(out_ref.dtype)


class Copies:
    def __init__(self, source, target, sems, tile):
        self.source, self.target, self.sems, self.tile = source, target, sems, tile

    def copy(self, i):
        at = pl.ds(pl.multiple_of(i * self.tile, self.tile), self.tile)
        return pltpu.make_async_copy(self.source.at[at, :], self.target.at[at, :], self.sems.at[i])

    def start(self, i):
        self.copy(i).start()

    def wait(self, i):
        self.copy(i).wait()


def quarter_math(act, cot_low, weights_ref, up_acc, down_acc):
    value, slope = gelu_pair(dot(act, weights_ref[0]))
    hidden = value.astype(BF16)
    grad_up = (dot_nt(cot_low, weights_ref[1]) * slope).astype(BF16)
    up_acc[...] += dot_tn(act, grad_up)
    down_acc[...] += dot_tn(cot_low, hidden)
    return hidden, dot_nt(grad_up, weights_ref[0])


def quarter_kernel(*refs, kind, tile, tally):
    if tally:
        mask_ref, refs = refs[0], refs[1:]
    where_ref, act_ref, weights_ref = refs[:3]
    if kind == "first":
        cot_far, hidden_far, grad_ref, piece_ref, low_ref, act_ref = refs[3:9]
        hidden_ref, up_acc, down_acc, hidden_sems, cot_ref, cot_sems, act_sems = refs[9:]
    elif kind == "middle":
        low_ref, sofar_ref, hidden_far, grad_ref, piece_ref = refs[3:8]
        hidden_ref, up_acc, down_acc, hidden_sems = refs[8:]
    else:
        low_ref, sofar_ref, gain_ref, entropy_ref, cot_far, second_far, att_far, wo_far = refs[3:11]
        hidden_far, gsec_far, piece_ref, gatt_ref, gout_ref = refs[11:16]
        hidden_ref, up_acc, down_acc, hidden_sems, cot_ref, cot_sems = refs[16:22]
        second_ref, second_sems, att_ref, att_sems, gsec_ref, gsec_sems = refs[22:28]
        wo_ref, wo_low_ref, wo_sem, out_acc, gain_acc, column_ref, sum_ref, second_low_ref = refs[28:]
    rows, width = act_ref.shape
    tiles = rows // tile
    hidden_out = Copies(hidden_ref, hidden_far, hidden_sems, tile)
    ins = []
    if kind == "first":
        ins = [Copies(cot_far, cot_ref, cot_sems, tile), Copies(refs[1], act_ref, act_sems, tile)]
    if kind == "last":
        ins = [
            Copies(second_far, second_ref, second_sems, tile),
            Copies(cot_far, cot_ref, cot_sems, tile),
            Copies(att_far, att_ref, att_sems, tile),
        ]
        gsec_out = Copies(gsec_ref, gsec_far, gsec_sems, tile)
    for i in range(tiles):
        for copies in ins:
            copies.start(i)
        if kind == "last" and i == 0:
            wo_copy = pltpu.make_async_copy(wo_far, wo_ref, wo_sem)
            wo_copy.start()
    up_acc[...] = jnp.zeros_like(up_acc)
    down_acc[...] = jnp.zeros_like(down_acc)
    if kind == "last":
        out_acc[...] = jnp.zeros_like(out_acc)
        gain_acc[...] = jnp.zeros_like(gain_acc)

    def multiply(i):
        at = pl.ds(pl.multiple_of(i * tile, tile), tile)
        if kind == "first":
            low_ref[at, :] = cot_ref[at, :].astype(BF16)
        hidden, grad = quarter_math(act_ref[at, :], low_ref[at, :], weights_ref, up_acc, down_acc)
        hidden_ref[at, :] = hidden
        if kind == "first":
            grad_ref[at, :] = grad
        elif kind == "middle":
            grad_ref[at, :] = sofar_ref[at, :] + grad
        else:
            sum_ref[i % 2] = sofar_ref[at, :] + grad

    def settle(i):
        at = pl.ds(pl.multiple_of(i * tile, tile), tile)
        grad = sum_ref[i % 2]
        unit, inverse = normalize(second_ref[at, :])
        gain_acc[...] += jnp.sum(grad * unit, axis=0, keepdims=True)
        grad_second = cot_ref[at, :] + norm_grad(grad, unit, inverse, gain_ref[...])
        gsec_ref[at, :] = grad_second
        second_low_ref[...] = grad_second.astype(BF16)

    def settle_back(i):
        at = pl.ds(pl.multiple_of(i * tile, tile), tile)
        second_low = second_low_ref[...]
        gatt_ref[at, :] = dot_nt(second_low, wo_low_ref[...]).astype(BF16)
        out_acc[...] += dot_tn(att_ref[at, :], second_low)

    def body(i, _):
        for copies in ins:
            copies.wait(i - 1 if kind == "last" else i)
        if kind == "last":
            settle(i - 1)
        multiply(i)
        if kind == "last":
            settle_back(i - 1)
            gsec_out.start(i - 1)
        hidden_out.start(i)
        return 0

    if kind == "last":
        multiply(0)
        hidden_out.start(0)
        wo_copy.wait()
        wo_low_ref[...] = wo_ref[...].astype(BF16)
        lax.fori_loop(1, tiles, body, 0)
        for copies in ins:
            copies.wait(tiles - 1)
        settle(tiles - 1)
        gsec_out.start(tiles - 1)
        settle_back(tiles - 1)
    else:
        lax.fori_loop(0, tiles, body, 0)
    size = width // piece_ref.shape[0]
    spread(piece_ref.at[:, :size], up_acc, where_ref[0], slice(None))
    spread(piece_ref.at[:, size : 2 * size], down_acc, where_ref[0], slice(None))
    if tally:
        shape = (TALLY_ROWS, weights_ref.shape[2])
        mine = lax.broadcasted_iota(jnp.int32, shape, 1) == where_ref[3]
        count = jnp.sum(mask_ref[...].astype(F32), axis=1, keepdims=True)
        row = jnp.where(mine, jnp.broadcast_to(count, shape), 0.0).astype(BF16)
        for r in range(piece_ref.shape[0]):
            piece_ref[r, 2 * size :, :] = row
    if kind == "last":
        spread(gout_ref, out_acc, where_ref[2], slice(0, width))
        half = (LANES // 2, width)
        column_ref[...] = jnp.concatenate(
            [jnp.broadcast_to(gain_acc[...], half), jnp.broadcast_to(entropy_ref[...], half)], axis=0
        ).T
        spread(gout_ref, column_ref, where_ref[2], slice(width, width + LANES))
    for i in range(tiles):
        hidden_out.wait(i)
        if kind == "last":
            gsec_out.wait(i)


def feed_quarter(
    kind, where, act, weights, cot, sofar=None, extra=None, mask_row=None, row_chunks=1, out_chunks=1, tile=512
):
    rows, width = act.shape
    units = weights.shape[2]
    tiles = rows // tile
    smem = pl.BlockSpec(memory_space=pltpu.SMEM)
    vmem = pl.BlockSpec(memory_space=pltpu.VMEM)
    hbm = pl.BlockSpec(memory_space=pltpu.HBM)
    tally = mask_row is not None
    size = 2 * (width // row_chunks) + (TALLY_ROWS if tally else 0)
    piece = near_shape((row_chunks, size, units), BF16)
    low = near_shape((rows, width), BF16)
    full = near_shape((rows, width), F32)
    hidden = far_shape((rows, units), BF16)
    sems = pltpu.SemaphoreType.DMA((tiles,))
    low_buffer, full_buffer = pltpu.VMEM((rows, width), BF16), pltpu.VMEM((rows, width), F32)
    square = pltpu.VMEM((width, width), F32)
    scratch = [pltpu.VMEM((rows, units), BF16), square, square, sems]
    if kind == "first":
        operands = (far(cot),)
        in_specs = [hbm]
        out_shape, out_specs = [hidden, full, piece, low, low], [hbm] + [vmem] * 4
        scratch = scratch + [full_buffer, sems, sems]
        limit = 24
    elif kind == "middle":
        operands = (near(cot), near(sofar))
        in_specs = [vmem] * 2
        out_shape, out_specs = [hidden, full, piece], [hbm] + [vmem] * 2
        limit = 18
    else:
        full_cot, second, att, w_out, gain, entropy = extra
        operands = (near(cot), near(sofar), gain, entropy, far(full_cot), far(second), far(att), far(w_out))
        in_specs = [vmem] * 4 + [hbm] * 4
        out_piece = near_shape((out_chunks, width // out_chunks, width + LANES), BF16)
        out_shape = [hidden, far_shape((rows, width), F32), piece, low, out_piece]
        out_specs = [hbm] * 2 + [vmem] * 3
        scratch = scratch + [full_buffer, sems, full_buffer, sems, low_buffer, sems, full_buffer, sems]
        scratch = scratch + [square, pltpu.VMEM((width, width), BF16), pltpu.SemaphoreType.DMA]
        scratch = scratch + [square, pltpu.VMEM((1, width), F32), pltpu.VMEM((width, LANES), F32)]
        scratch = scratch + [pltpu.VMEM((2, tile, width), F32), pltpu.VMEM((tile, width), BF16)]
        limit = 32
    return pl.pallas_call(
        functools.partial(quarter_kernel, kind=kind, tile=tile, tally=tally),
        in_specs=([vmem] if tally else []) + [smem, hbm if kind == "first" else vmem, vmem] + in_specs,
        out_specs=out_specs,
        out_shape=out_shape,
        scratch_shapes=scratch,
        compiler_params=params(limit),
        cost_estimate=cost(9),
        name="feed_" + kind,
    )(
        *([mask_row] if tally else []), where, far(act) if kind == "first" else near(act), near(weights), *operands
    )


def output_kernel(second_ref, *refs):
    out_ref = refs[-1]
    count = (len(refs) - 1) // 2
    total = second_ref[...]
    for hidden_ref, weights_ref in zip(refs[:count], refs[count : 2 * count]):
        total = total + dot(hidden_ref[...], weights_ref[0])
    out_ref[...] = total


def layer_output(second, hidden, weights, tile=512):
    rows, width = second.shape
    units = hidden[0].shape[1]
    down = pl.BlockSpec((1, units, width), lambda *_: (1, 0, 0), pipeline_mode=pl.Buffered(1))
    return pl.pallas_call(
        output_kernel,
        grid=(rows // tile,),
        in_specs=[rows_of(tile, width)] + [rows_of(tile, units)] * len(hidden) + [down] * len(hidden),
        out_specs=rows_of(tile, width),
        out_shape=far_shape((rows, width), F32),
        compiler_params=params(16),
        cost_estimate=cost(8),
        name="layer_output",
    )(near(second), *[far(array) for array in hidden], *[near(array) for array in weights])


def head_kernel(*refs, count):
    where_ref, pen_ref, act_ref = refs[:3]
    groups = [refs[3 + 4 * g : 7 + 4 * g] for g in range(count)]
    share_ref, log_ref, sum_ref, w_ref, perm_ref, mask_ref, out_ref, tally_ref = refs[3 + 4 * count : 11 + 4 * count]
    piece_ref, gsum_ref, total_ref, glog_ref, acc_ref = refs[11 + 4 * count :]
    block_total = jnp.sum(tally_ref[...].astype(F32), axis=1, keepdims=True)
    block_total = jnp.sum(block_total, axis=0, keepdims=True)
    total_ref[...] = jnp.broadcast_to(block_total, total_ref.shape)
    coef = pen_ref[0] / (HEADS * block_total)
    blocks, width = sum_ref.shape
    cols = acc_ref.shape[1]
    wide = 2 * blocks
    first, position = lane_tiles(blocks)
    hot = position == down_rows(perm_ref[...], wide)
    weight = coef * down_rows(mask_ref[...], wide)
    act = act_ref[...]
    for g, group in enumerate(groups):
        for index in range(3):
            acc_ref[...] = dot_tn(act, group[index][...])
            at = index * width + g * cols
            spread(piece_ref, acc_ref, where_ref[2], slice(at, at + cols))
        for pair in range(cols // wide):
            at = g * cols + pair * wide
            span = slice(at, at + wide)
            plan = share_ref[2 * ITERS - 1, :, span]
            gch = segment_sum(group[3][:, pair * wide : (pair + 1) * wide], first)
            grad = plan * (jnp.where(hot, blocks * gch, 0.0) - weight * (log_ref[:, span] + 1.0))
            for level in range(2 * ITERS - 1, -1, -1):
                if level % 2:
                    total = jnp.sum(grad, axis=0, keepdims=True)
                else:
                    total = segment_sum(grad, first)
                grad = grad - share_ref[level, :, span] * total
            glog_ref[:, span] = grad
    for g in range(count):
        at = slice(g * cols, (g + 1) * cols)
        acc_ref[...] = lax.dot_general(
            sum_ref[...], glog_ref[:, at], TN, precision=HIGHEST, preferred_element_type=F32
        )
        spread(piece_ref, acc_ref, where_ref[2], slice(3 * width + g * cols, 3 * width + (g + 1) * cols))
    gsum_ref[...] = lax.dot_general(glog_ref[...], w_ref[...], NT, precision=HIGHEST, preferred_element_type=F32)
    piece_ref[:, :, 4 * width :] = out_ref[...]


def head_grads(
    where, pen_weight, act, groups, shares, plan_log, sums, w_sort, perm_row, mask_row, out_piece, tallies, chunks
):
    rows, width = act.shape
    blocks = sums.shape[0]
    cols = groups[0][0].shape[1]
    smem = pl.BlockSpec(memory_space=pltpu.SMEM)
    vmem = pl.BlockSpec(memory_space=pltpu.VMEM)
    flat = [near(array) for group in groups for array in group]
    piece = (chunks, width // chunks, 4 * width + out_piece.shape[2])
    return pl.pallas_call(
        functools.partial(head_kernel, count=len(groups)),
        in_specs=[smem] * 2 + [vmem] * (9 + len(flat)),
        out_specs=[vmem] * 3,
        out_shape=[near_shape(piece, BF16), near_shape((blocks, width), F32), near_shape((1, LANES), F32)],
        scratch_shapes=[pltpu.VMEM((blocks, width), F32), pltpu.VMEM((width, cols), F32)],
        compiler_params=params(14),
        cost_estimate=cost(6),
        name="head_grads",
    )(
        where, pen_weight, near(act), *flat, near(shares), near(plan_log), near(sums), near(w_sort), perm_row, mask_row,
        near(out_piece), tallies,
    )


def input_kernel(*refs):
    count = (len(refs) - 9) // 3
    groups = [refs[3 * g : 3 * g + 3] for g in range(count)]
    gsum_ref, x_ref, gsec_ref, gain_ref, wq_ref, wk_ref, wv_ref, out_ref, w_ref = refs[3 * count :]

    @pl.when(pl.program_id(0) == 0)
    def _():
        for which, ref in enumerate((wq_ref, wk_ref, wv_ref)):
            w_ref[which] = ref[...].astype(BF16)

    rows, width = x_ref.shape
    grad = jnp.zeros((rows, width), F32)
    for g, group in enumerate(groups):
        for which, ref in enumerate(group):
            cols = ref.shape[1]
            grad = grad + dot_nt(ref[...], w_ref[which, :, g * cols : (g + 1) * cols])
    grad = (grad.reshape(rows // BLOCK, BLOCK, width) + gsum_ref[...][:, None, :]).reshape(rows, width)
    unit, inverse = normalize(x_ref[...])
    out_ref[...] = gsec_ref[...] + norm_grad(grad, unit, inverse, gain_ref[...])


def input_grad(groups, gsum, x, gsec, gain, wq, wk, wv, tile=512):
    rows, width = x.shape
    weight = pl.BlockSpec((width, width), lambda *_: (0, 0), pipeline_mode=pl.Buffered(1))
    flat = [array for group in groups for array in group]
    return pl.pallas_call(
        input_kernel,
        grid=(rows // tile,),
        in_specs=[rows_of(tile, array.shape[1]) for array in flat]
        + [rows_of(tile // BLOCK, width)]
        + [rows_of(tile, width)] * 2
        + [whole((1, width))]
        + [weight] * 3,
        out_specs=rows_of(tile, width),
        out_shape=far_shape((rows, width), F32),
        scratch_shapes=[pltpu.VMEM((3, width, width), BF16)],
        compiler_params=params(20),
        cost_estimate=cost(10),
        name="input_grad",
    )(*[near(array) for array in flat], gsum, far(x), far(gsec), gain, far(wq), far(wk), far(wv))


def pack_kernel(core_ref, up_ref, down_ref, mine_ref):
    mine_ref[0] = up_ref[...].astype(BF16)
    mine_ref[1] = down_ref[...].astype(BF16)


def pack_weights(core, w_up, w_down):
    width, units = w_up.shape
    half = units // 2
    shape = (2, width, half)
    return pl.pallas_call(
        pack_kernel,
        grid_spec=pltpu.PrefetchScalarGridSpec(
            num_scalar_prefetch=1,
            grid=(1,),
            in_specs=[
                pl.BlockSpec((width, half), lambda step, core: (0, core[0])),
                pl.BlockSpec((half, width), lambda step, core: (core[0], 0)),
            ],
            out_specs=whole(shape),
        ),
        out_shape=near_shape(shape, BF16),
        compiler_params=params(12),
        cost_estimate=cost(2),
        name="pack_weights",
    )(core, far(w_up), far(w_down))


def finish_feed_kernel(*refs):
    where_ref, parts = refs[0], refs[1:-3]
    up_ref, down_ref, turn_ref = refs[-3:]
    some, size, units = parts[0].shape
    size = size // 2
    half = len(parts) // 2
    for flip in range(2):
        column = pl.multiple_of((where_ref[1] ^ flip) * units, units)
        for n, ref in enumerate(parts[flip * half : (flip + 1) * half]):
            for r in range(some):
                at = pl.multiple_of(((n * some + r) ^ where_ref[0]) * size, size)
                up_ref[pl.ds(at, size), pl.ds(column, units)] = ref[r, :size].astype(F32)
                turn_ref[pl.ds(at, size), :] = ref[r, size:].astype(F32)
        down_ref[pl.ds(column, units), :] = turn_ref[...].T


def finish_feed(where, parts):
    some, size, units = parts[0].shape
    width = len(parts) // 2 * some * size // 2
    vmem = pl.BlockSpec(memory_space=pltpu.VMEM)
    return pl.pallas_call(
        finish_feed_kernel,
        in_specs=[pl.BlockSpec(memory_space=pltpu.SMEM)] + [vmem] * len(parts),
        out_specs=[vmem, vmem],
        out_shape=[far_shape((width, 2 * units), F32), far_shape((2 * units, width), F32)],
        scratch_shapes=[pltpu.VMEM((width, units), F32)],
        compiler_params=params(16),
        cost_estimate=cost(3),
        name="finish_feed",
    )(where, *parts)


def finish_kernel(*refs):
    where_ref, parts = refs[0], refs[1:-22]
    weights = refs[-22:-18]
    gain_ref, total_ref = refs[-18:-16]
    fars = refs[-16:-11]
    gain_one_ref, gain_two_ref, penalty_ref = refs[-11:-8]
    nears = refs[-8:-3]
    one_ref, two_ref, sems = refs[-3:]
    width = gain_ref.shape[1]
    some, size = parts[0].shape[:2]
    total = jnp.zeros((width, LANES), F32)
    copies = []
    for index, near_ref in enumerate(nears):
        for n, part_ref in enumerate(parts):
            for r in range(some):
                rows = pl.ds(pl.multiple_of(((n * some + r) ^ where_ref[2]) * size, size), size)
                near_ref[rows, :] = part_ref[r, :, index * width : (index + 1) * width].astype(F32)
                if index == 0:
                    two_ref[rows, :] = part_ref[r, :, 5 * width :].astype(F32)
        copies.append(pltpu.make_async_copy(near_ref, fars[index], sems.at[index]))
        copies[-1].start()
    for at in range(0, width, LANES):
        span = slice(at, at + LANES)
        for grad, weight in zip(nears[:3], weights[:3]):
            total = total + grad[:, span] * weight[:, span].astype(BF16).astype(F32)
        total = total + nears[3][:, span] * weights[3][:, span]
    one_ref[...] = total
    gain_one_ref[...] = jnp.sum(one_ref[...].T, axis=0, keepdims=True) / gain_ref[...]
    turned = two_ref[...].T
    gain_two_ref[...] = turned[:1, :]
    entropy = jnp.sum(turned[LANES // 2 : LANES // 2 + 1, :], axis=1, keepdims=True)
    penalty_ref[...] = entropy / (HEADS * total_ref[:, :1])
    for copy in copies:
        copy.wait()


def finish(where, parts, wq, wk, wv, ws, gain, total):
    width = wq.shape[0]
    vmem = pl.BlockSpec(memory_space=pltpu.VMEM)
    hbm = pl.BlockSpec(memory_space=pltpu.HBM)
    square = far_shape((width, width), F32)
    row = shape_of((1, width), F32)
    return pl.pallas_call(
        finish_kernel,
        in_specs=[pl.BlockSpec(memory_space=pltpu.SMEM)] + [vmem] * (6 + len(parts)),
        out_specs=[hbm] * 5 + [vmem] * 3,
        out_shape=[square] * 5 + [row] * 2 + [shape_of((1, 1), F32)],
        scratch_shapes=[pltpu.VMEM((width, width), F32)] * 5
        + [pltpu.VMEM((width, LANES), F32)] * 2
        + [pltpu.SemaphoreType.DMA((5,))],
        compiler_params=params(16),
        cost_estimate=cost(5),
        name="finish",
    )(where, *parts, near(wq), near(wk), near(wv), near(ws), gain, total)


MP, CORE, X, Z_LOW, Z_HIGH = 1, 2, 4, 8, 16
CORE_STEP = ((CORE,), (CORE,))
FEED_STEPS = ((X,), (Z_LOW, Z_HIGH, Z_LOW + Z_HIGH))
HEAD_STEPS = ((CORE,), (MP, X, MP + X), (Z_LOW, Z_HIGH, Z_LOW + Z_HIGH))


def swap(array, flip):
    count = lax.axis_size("batch") * lax.axis_size("mp")
    return lax.ppermute(array, ("batch", "mp"), [(i, i ^ flip) for i in range(count)])


def place(steps, index):
    result = jnp.int32(0)
    for step in steps:
        for bit in reversed(step[: (len(step) + 1).bit_length() - 1]):
            result = 2 * result + ((index & bit) > 0).astype(jnp.int32)
    return result


def add_low(first, *others):
    total = first.astype(F32)
    for array in others:
        total = total + array.astype(F32)
    return total.astype(BF16)


class Walk:
    def __init__(self, pieces, steps):
        self.pieces = pieces
        self.down = list(steps)
        self.up = list(reversed(steps))
        self.parts, self.arrived = None, []

    def added(self, plan, count):
        pieces = self.pieces + [plan.after(array) for array in self.arrived]
        self.arrived = []
        size = pieces[0].shape[0] // count
        if len(pieces) == 1 and count == 1:
            return pieces
        return [
            add_low(*[piece[n * size : (n + 1) * size] for piece in pieces]) if len(pieces) > 1
            else pieces[0][n * size : (n + 1) * size]
            for n in range(count)
        ]

    def reduce(self, plan):
        flips = self.down.pop(0)
        parts = self.added(plan, len(flips) + 1)
        self.arrived = [swap(plan.after(part), flip) for part, flip in zip(parts[1:], flips)]
        self.pieces = parts[:1]
        return self.arrived

    def reduced(self, plan):
        return self.added(plan, 1)[0]

    def gather(self, plan, value):
        flips = self.up.pop(0)
        self.parts = [value]
        mine = plan.after(value)
        self.arrived = [swap(mine, flip) for flip in flips]
        return self.arrived

    def gathered(self, plan):
        parts = self.parts + [plan.after(array) for array in self.arrived]
        self.arrived = []
        return parts


class Schedule:
    def __init__(self):
        self.pending, self.launched, self.done = [], [], None

    def after(self, array):
        return lax.optimization_barrier((array, self.done))[0]

    def enter(self, small):
        tied = lax.optimization_barrier((small, *self.pending))[0]
        self.pending, self.launched = self.launched, []
        return tied

    def leave(self, *arrays):
        self.pending.extend(arrays)
        self.done = arrays[0]

    def launch(self, *arrays):
        for array in arrays:
            self.launched.extend(array if isinstance(array, list) else [array])


def local_small(
    inputs, cotangent, block_perm, block_mask, pen_weight, w_query, w_key, w_value, w_out, w_sort,
    gain_one, gain_two, w_up, w_down,
):
    _, rows, width = inputs.shape
    x = inputs.reshape(rows, width)
    cot = cotangent.reshape(rows, width)
    perm = block_perm.reshape(-1)
    mask = block_mask.reshape(-1)
    perm_row = block_perm.reshape(1, -1)
    mask_row = block_mask.reshape(1, -1)
    gain_one_row = gain_one.reshape(1, width)
    gain_two_row = gain_two.reshape(1, width)
    batch, mp = lax.axis_index("batch"), lax.axis_index("mp")
    core = batch & 1
    index = batch * 2 + mp
    where = jnp.stack([place(FEED_STEPS, index), core, place(HEAD_STEPS, index), index])
    row_chunks, out_chunks = 8, 32
    plan = Schedule()

    count = jnp.broadcast_to(jnp.sum(mask.astype(F32)), (8, LANES))
    own_a = pack_weights(core.reshape(1), w_up, w_down)
    far_a = swap(own_a, MP)
    plan.leave(own_a)
    act_one, q, k, v, probs, att, second, act_two_far, shares, sums, plan_log, chosen, entropy, own_b = forward(
        perm, mask, (1 - core).reshape(1), perm_row, mask_row, plan.enter(gain_one_row), gain_two_row, x,
        w_query, w_key, w_value, w_sort, w_out, w_up, w_down,
    )
    plan.leave(entropy)
    plan.pending.append(far_a)

    far_b = swap(plan.after(far_a), CORE)
    plan.launch(far_b)
    hid_a, sofar, other_piece, cot_low, act_two = feed_quarter(
        "first", plan.enter(where), act_two_far, far_a, cot, mask_row=mask_row, row_chunks=row_chunks
    )
    plan.leave(other_piece)

    hid_b, sofar, piece = feed_quarter(
        "middle", plan.enter(where), act_two, far_b, cot_low, sofar, mask_row=mask_row, row_chunks=row_chunks
    )
    plan.leave(piece)

    arrived = swap(plan.after(piece), CORE)
    plan.launch(arrived)
    hid_c, sofar, piece = feed_quarter(
        "middle", plan.enter(where), act_two, own_b, cot_low, sofar, row_chunks=row_chunks
    )
    plan.leave(piece)

    other = Walk([other_piece, plan.after(arrived)], FEED_STEPS)
    arrived = swap(plan.after(piece), CORE)
    plan.launch(arrived, other.reduce(plan))
    extra = (cot, second, att, w_out, gain_two_row, entropy)
    hid_d, grad_second, piece, grad_att, out_piece = feed_quarter(
        "last", plan.enter(where), act_two, own_a, cot_low, sofar, extra, None, row_chunks, out_chunks
    )
    plan.leave(grad_att)

    own = Walk([piece, plan.after(arrived)], FEED_STEPS)
    plan.launch(own.reduce(plan), other.reduce(plan))
    groups = [attend_back(plan.enter(perm), q, grad_att, probs, k, v, chosen, 0)]
    plan.leave(groups[0][3])

    other_sum = other.reduced(plan)
    crossed = swap(plan.after(other_sum), MP)
    plan.launch(crossed, own.reduce(plan))
    plan.pending.extend(own.pieces)
    groups.append(attend_back(plan.enter(perm), q, grad_att, probs, k, v, chosen, 1))
    plan.leave(groups[1][3])

    crossed = plan.after(crossed)
    rows_fed = own.pieces[0].shape[1]
    tallies = jnp.concatenate([other_sum[0, rows_fed:], crossed[0, rows_fed:]], axis=0)
    tallies = tallies.reshape(2, TALLY_ROWS, -1)[:, 0]
    own.pieces.append(crossed[:, :rows_fed])
    value = own.reduced(plan)
    plan.pending.append(value)
    piece, gsum, block_total = head_grads(
        plan.enter(where), pen_weight, act_one, groups, shares, plan_log, sums, w_sort, perm_row, mask_row, out_piece,
        tallies, out_chunks,
    )
    plan.leave(gsum)

    head = Walk([piece], HEAD_STEPS)
    plan.pending.extend(head.reduce(plan))
    own.gather(plan, value)
    plan.launch(head.reduce(plan))
    plan.pending.extend(head.pieces)
    grad_input = input_grad(
        [group[:3] for group in groups], gsum, x, grad_second, plan.enter(gain_one_row), w_query, w_key, w_value
    )
    plan.leave(grad_input)

    head.reduce(plan)
    own.gather(plan, jnp.concatenate(own.gathered(plan), axis=0))
    head.gather(plan, head.reduced(plan))
    value = jnp.concatenate(head.gathered(plan), axis=0)
    plan.pending.append(value)
    head.gather(plan, value)
    quarters = (far_a, far_b, own_b, own_a)
    output = layer_output(plan.enter(second), (hid_a, hid_b, hid_c, hid_d), quarters)
    plan.leave(output)

    parts = own.parts + own.arrived
    grad_up, grad_down = finish_feed(plan.enter(where), parts + [swap(part, CORE) for part in parts])
    plan.leave(grad_up)
    parts = head.gathered(plan)
    parts = parts + [swap(part, CORE) for part in parts]
    grad_query, grad_key, grad_value, grad_sort, grad_out, grad_gain_one, grad_gain_two, penalty = finish(
        where, parts, w_query, w_key, w_value, w_sort, gain_one_row, block_total
    )
    return (
        output.reshape(inputs.shape),
        penalty.reshape(1),
        grad_input.reshape(inputs.shape),
        grad_query,
        grad_key,
        grad_value,
        grad_out,
        grad_sort,
        grad_gain_one.reshape(width),
        grad_gain_two.reshape(width),
        grad_up,
        grad_down,
    )


def local_any(
    inputs, cotangent, block_perm, block_mask, pen_weight, w_query, w_key, w_value, w_out, w_sort,
    gain_one, gain_two, w_up, w_down,
):
    both = ("batch", "mp")
    _, rows, width = inputs.shape
    x = inputs.reshape(rows, width)
    cot = cotangent.reshape(rows, width)
    perm = block_perm.reshape(-1)
    mask = block_mask.reshape(-1)
    perm_row = block_perm.reshape(1, -1)
    mask_row = block_mask.reshape(1, -1)
    gain_one_row = gain_one.reshape(1, width)
    gain_two_row = gain_two.reshape(1, width)
    where = jnp.zeros((4,), jnp.int32)
    up_all = lax.all_gather(w_up.astype(BF16), "mp", axis=1, tiled=True)
    down_all = lax.all_gather(w_down.astype(BF16), "mp", axis=0, tiled=True)
    quarters = [
        jnp.stack([up_all[:, at : at + width], down_all[at : at + width]])
        for at in range(0, up_all.shape[1], width)
    ]
    act_one, q, k, v, probs, att, second, act_two_far, shares, sums, plan_log, chosen, entropy = forward(
        perm, mask, jnp.zeros((1,), jnp.int32), perm_row, mask_row, gain_one_row, gain_two_row, x,
        w_query, w_key, w_value, w_sort, w_out, w_query, w_query,
    )[:-1]
    tallies = jnp.broadcast_to(lax.psum(jnp.sum(mask_row).astype(F32), both) / width, (1, width))
    hidden, parts = [], []
    low, sofar = cot, None
    for index, weights in enumerate(quarters):
        if index == 0:
            hid, sofar, piece, low, act_two = feed_quarter("first", where, act_two_far, weights, low)
        elif index < len(quarters) - 1:
            hid, sofar, piece = feed_quarter("middle", where, act_two, weights, low, sofar)
        else:
            extra = (cot, second, att, w_out, gain_two_row, entropy)
            hid, grad_second, piece, grad_att, extra = feed_quarter(
                "last", where, act_two, weights, low, sofar, extra
            )
        hidden.append(hid)
        parts.append(piece[0])
    groups = [
        attend_back(perm, q, grad_att, probs, k, v, chosen, group) for group in range(width // GROUP_WIDTH)
    ]
    piece, gsum, block_total = head_grads(
        where, pen_weight, act_one, groups, shares, plan_log, sums, w_sort, perm_row, mask_row, extra, tallies, 1
    )
    grad_input = input_grad(
        [group[:3] for group in groups], gsum, x, grad_second, gain_one_row, w_query, w_key, w_value
    )
    output = layer_output(second, hidden, quarters)

    parts = jnp.concatenate(parts, axis=1).reshape(2, width, -1)
    parts = lax.psum(lax.psum_scatter(parts, "mp", scatter_dimension=2, tiled=True), "batch").astype(F32)
    grad_up, grad_down = parts[0], parts[1].T
    piece = lax.psum(piece, both)
    grad_query, grad_key, grad_value, grad_sort, grad_out, grad_gain_one, grad_gain_two, penalty = finish(
        where, [piece], w_query, w_key, w_value, w_sort, gain_one_row, block_total
    )
    return (
        output.reshape(inputs.shape),
        penalty.reshape(1),
        grad_input.reshape(inputs.shape),
        grad_query,
        grad_key,
        grad_value,
        grad_out,
        grad_sort,
        grad_gain_one.reshape(width),
        grad_gain_two.reshape(width),
        grad_up,
        grad_down,
    )


def solution(mesh):
    tokens = P(("batch", "mp"), None, None)
    blocks = P(("batch", "mp"), None)
    small = mesh.shape["batch"] == 16 and mesh.shape["mp"] == 2
    return jax.shard_map(
        local_small if small else local_any,
        mesh=mesh,
        in_specs=(tokens, tokens, blocks, blocks) + (P(),) * 8 + (P(None, "mp"), P("mp", None)),
        out_specs=(tokens, P(), tokens) + (P(),) * 7 + (P(None, "mp"), P("mp", None)),
        check_vma=False,
    )
```

```python
import functools

import jax
import jax.numpy as jnp
from jax import lax
from jax.experimental import pallas as pl
from jax.experimental.pallas import tpu as pltpu
from jax.sharding import PartitionSpec as P

HEADS = 8
HEAD_DIM = 64
BLOCK = 32
ITERS = 8
GROUP = 4
GROUP_WIDTH = GROUP * HEAD_DIM
GROUP_ROWS = GROUP * BLOCK
EPSILON = 1e-05
FACTOR = HEAD_DIM ** (-0.5)
HIGHEST = lax.Precision.HIGHEST
F32 = jnp.float32
BF16 = jnp.bfloat16
NT = (((1,), (1,)), ((), ()))
TN = (((0,), (0,)), ((), ()))
MIB = 1024 * 1024
LANES = 128
TALLY_ROWS = 16
AHEAD = 3


def dot(left, right):
    return jnp.dot(left, right, preferred_element_type=F32)


def dot_nt(left, right):
    return lax.dot_general(left, right, NT, preferred_element_type=F32)


def dot_tn(left, right):
    return lax.dot_general(left, right, TN, preferred_element_type=F32)


def shape_of(dims, dtype):
    return jax.ShapeDtypeStruct(dims, dtype)


def whole(dims):
    return pl.BlockSpec(dims, lambda *_: (0,) * len(dims))


def once(dims):
    return pl.BlockSpec(dims, lambda *_: (0,) * len(dims), pipeline_mode=pl.Buffered(1))


def rows_of(size, width):
    return pl.BlockSpec((size, width), lambda step, *_: (step, 0))


def params(mib):
    return pltpu.CompilerParams(vmem_limit_bytes=mib * MIB)


def far(array):
    return pltpu.with_memory_space_constraint(array, pltpu.HBM)


def near(array):
    return pltpu.with_memory_space_constraint(array, pltpu.VMEM)


def near_shape(dims, dtype):
    return pltpu.VMEM(dims, dtype)


def far_shape(dims, dtype):
    return pltpu.HBM(dims, dtype)


def cost(micros):
    return pl.CostEstimate(flops=int(micros * 1150000000), bytes_accessed=0, transcendentals=0)


def normalize(values):
    center = values - jnp.mean(values, axis=-1, keepdims=True)
    inverse = lax.rsqrt(jnp.mean(center * center, axis=-1, keepdims=True) + EPSILON)
    return center * inverse, inverse


def norm_grad(grad_rows, unit_rows, inverse, gain):
    scaled_rows = grad_rows * gain
    return inverse * (
        scaled_rows
        - jnp.mean(scaled_rows, axis=-1, keepdims=True)
        - unit_rows * jnp.mean(scaled_rows * unit_rows, axis=-1, keepdims=True)
    )


def segment_sum(tile, first):
    left = jnp.sum(jnp.where(first, tile, 0.0), axis=1, keepdims=True)
    right = jnp.sum(jnp.where(first, 0.0, tile), axis=1, keepdims=True)
    return jnp.where(first, left, right)


def segment_max(tile, first):
    left = jnp.max(jnp.where(first, tile, -jnp.inf), axis=1, keepdims=True)
    right = jnp.max(jnp.where(first, -jnp.inf, tile), axis=1, keepdims=True)
    return jnp.where(first, left, right)


def head_masks(rows):
    lane = lax.broadcasted_iota(jnp.int32, (rows, GROUP_WIDTH), 1)
    return [(lane >= h * HEAD_DIM) & (lane < (h + 1) * HEAD_DIM) for h in range(GROUP)]


def expand(rows, masks):
    zero = jnp.zeros_like(rows)
    return jnp.concatenate([jnp.where(mask, rows, zero) for mask in masks], axis=0)


def fold(rows, masks):
    parts = [rows[h * BLOCK : (h + 1) * BLOCK] for h in range(GROUP)]
    result = parts[GROUP - 1]
    for h in range(GROUP - 1):
        result = jnp.where(masks[h], parts[h], result)
    return result


def lane_tiles(blocks):
    lane = lax.broadcasted_iota(jnp.int32, (blocks, 2 * blocks), 1)
    return lane < blocks, jnp.where(lane < blocks, lane, lane - blocks).astype(F32)


def down_rows(row, wide):
    return jnp.broadcast_to(row.astype(F32), (wide, row.shape[1])).T


def balance_plans(logits, perm_row, mask_row, share_ref, log_ref, chosen_ref, entropy_ref):
    blocks = logits.shape[0]
    wide = 2 * blocks
    first, position = lane_tiles(blocks)
    hot = position == down_rows(perm_row, wide)
    real = down_rows(mask_row, wide) > 0.0
    for pair in range(logits.shape[1] // wide):
        span = slice(pair * wide, (pair + 1) * wide)
        tile = logits[:, span]
        for step in range(ITERS):
            top = segment_max(tile, first)
            powers = jnp.exp(tile - top)
            total = segment_sum(powers, first)
            tile = tile - (top + jnp.log(total))
            share_ref[2 * step, :, span] = powers * (1.0 / total)
            top = jnp.max(tile, axis=0, keepdims=True)
            powers = jnp.exp(tile - top)
            total = jnp.sum(powers, axis=0, keepdims=True)
            tile = tile - (top + jnp.log(total))
            if step < ITERS - 1:
                share_ref[2 * step + 1, :, span] = powers * (1.0 / total)
        plan = jnp.exp(tile)
        share_ref[2 * ITERS - 1, :, span] = plan
        log_ref[:, span] = tile
        chosen_ref[:, span] = blocks * segment_sum(jnp.where(hot, plan, 0.0), first)
        entropy_ref[:, span] = -jnp.sum(jnp.where(real, plan * tile, 0.0), axis=0, keepdims=True)


def forward_kernel(
    perm_ref, mask_ref, other_ref, perm_row_ref, mask_row_ref, gain_one_ref, gain_two_ref,
    x_far, wq_far, wk_far, wv_far, ws_far, wo_far, up_far, down_far,
    act_far, q_far, k_far, v_far, probs_far, att_far, second_far, act_two_far, share_far,
    sum_ref, log_ref, chosen_ref, entropy_ref, packed_ref,
    x_ref, w_ref, w_low_ref, wo_low_ref, act_ref, q_ref, k_ref, v_ref, probs_ref, att_ref, second_ref, act_two_ref, share_ref,
    feed_ref, in_sem, out_sem, share_sem, feed_sem, *, tile,
):
    rows, width = x_ref.shape
    tiles = rows // tile

    def x_copy(i):
        at = pl.ds(pl.multiple_of(i * tile, tile), tile)
        return pltpu.make_async_copy(x_far.at[at, :], x_ref.at[at, :], in_sem.at[i])

    def w_copy(n):
        far_ref = (wq_far, wk_far, wv_far, ws_far, wo_far)[n]
        return pltpu.make_async_copy(far_ref, w_ref.at[n], in_sem.at[tiles + n])

    outs = (
        (act_ref, act_far), (q_ref, q_far), (k_ref, k_far), (v_ref, v_far),
        (probs_ref, probs_far), (att_ref, att_far), (second_ref, second_far), (act_two_ref, act_two_far),
    )
    part = 8
    some = part * BLOCK
    parts = rows // some

    def out_copy(n, i):
        near_ref, far_ref = outs[n]
        size = near_ref.shape[0] // (tiles if n < 4 else parts)
        at = pl.ds(pl.multiple_of(i * size, size), size)
        return pltpu.make_async_copy(near_ref.at[at, :], far_ref.at[at, :], out_sem.at[n, i])

    x_copy(0).start()
    for n in range(3):
        w_copy(n).start()
    for i in range(1, tiles):
        x_copy(i).start()
    w_copy(3).start()
    w_copy(4).start()
    units = packed_ref.shape[2]
    at = pl.ds(pl.multiple_of(other_ref[0] * units, units), units)
    feed_copies = [
        pltpu.make_async_copy(up_far.at[:, at], feed_ref.at[0], feed_sem.at[0]),
        pltpu.make_async_copy(down_far.at[at, :], feed_ref.at[1], feed_sem.at[1]),
    ]
    for copy in feed_copies:
        copy.start()
    for n in range(3):
        w_copy(n).wait()
        w_low_ref[:, n * width : (n + 1) * width] = w_ref[n].astype(BF16)

    def prepare(i):
        at = pl.ds(pl.multiple_of(i * tile, tile), tile)
        unit, _ = normalize(x_ref[at, :])
        act = (unit * gain_one_ref[...]).astype(BF16)
        act_ref[at, :] = act
        sums = jnp.sum(act.astype(F32).reshape(tile // BLOCK, BLOCK, width), axis=1)
        some = tile // BLOCK
        sum_ref[pl.ds(pl.multiple_of(i * some, some), some), :] = sums.astype(BF16).astype(F32)

    def project(i):
        at = pl.ds(pl.multiple_of(i * tile, tile), tile)
        act = act_ref[at, :]
        for n, ref in enumerate((q_ref, k_ref, v_ref)):
            ref[at, :] = dot(act, w_low_ref[:, n * width : (n + 1) * width]).astype(BF16)

    def project_out(i):
        for n in range(4):
            out_copy(n, i).start()

    def both(i, _):
        x_copy(i + 1).wait()
        project(i)
        prepare(i + 1)
        project_out(i)
        return 0

    x_copy(0).wait()
    prepare(0)
    lax.fori_loop(0, tiles - 2, both, 0)
    x_copy(tiles - 1).wait()
    prepare(tiles - 1)
    w_copy(3).wait()
    w_copy(4).wait()
    wo_low_ref[...] = w_ref[4].astype(BF16)
    for n, copy in enumerate(feed_copies):
        copy.wait()
        packed_ref[n] = feed_ref[n].astype(BF16)
    logits = jnp.dot(sum_ref[...], w_ref[3], precision=HIGHEST, preferred_element_type=F32)
    balance_plans(
        logits, perm_row_ref[...], mask_row_ref[...], share_ref, log_ref, chosen_ref, entropy_ref
    )
    for i in (tiles - 2, tiles - 1):
        project(i)
    for i in (tiles - 2, tiles - 1):
        project_out(i)
    pltpu.make_async_copy(share_ref, share_far, share_sem).start()

    masks = head_masks(BLOCK)
    key_row = lax.broadcasted_iota(jnp.int32, (BLOCK, GROUP_ROWS), 0)
    query_row = lax.broadcasted_iota(jnp.int32, (BLOCK, GROUP_ROWS), 1) % BLOCK
    causal = key_row <= query_row

    def score(block, g):
        partner = perm_ref[block]
        own_at = pl.ds(pl.multiple_of(block * BLOCK, BLOCK), BLOCK)
        far_at = pl.ds(pl.multiple_of(partner * BLOCK, BLOCK), BLOCK)
        lanes = slice(g * GROUP_WIDTH, (g + 1) * GROUP_WIDTH)
        queries = expand(q_ref[own_at, lanes], masks)
        keys = jnp.concatenate([k_ref[own_at, lanes], k_ref[far_at, lanes]], axis=0)
        return dot_nt(keys, queries) * FACTOR

    def mix(block, g, scores):
        partner = perm_ref[block]
        usable = (partner < block) & (mask_ref[partner] > 0)
        own_at = pl.ds(pl.multiple_of(block * BLOCK, BLOCK), BLOCK)
        far_at = pl.ds(pl.multiple_of(partner * BLOCK, BLOCK), BLOCK)
        probs_at = pl.ds(pl.multiple_of(block * 2 * BLOCK, 2 * BLOCK), 2 * BLOCK)
        lanes = slice(g * GROUP_WIDTH, (g + 1) * GROUP_WIDTH)
        own = jnp.where(causal, scores[:BLOCK], -1e30)
        far = jnp.where(usable, scores[BLOCK:], -1e30)
        top = jnp.maximum(jnp.max(own, axis=0, keepdims=True), jnp.max(far, axis=0, keepdims=True))
        powers = jnp.exp(jnp.concatenate([own, far], axis=0) - top)
        probs = (powers * (1.0 / jnp.sum(powers, axis=0, keepdims=True))).astype(BF16)
        probs_ref[probs_at, g * GROUP_ROWS : (g + 1) * GROUP_ROWS] = probs
        scaled = (v_ref[far_at, lanes].astype(F32) * chosen_ref[pl.ds(block, 1), lanes]).astype(BF16)
        values = jnp.concatenate([v_ref[own_at, lanes], scaled], axis=0)
        att_ref[own_at, lanes] = fold(dot_tn(probs, values), masks).astype(BF16)

    def attend(j):
        units = [(j * part + b, g) for b in range(part) for g in range(width // GROUP_WIDTH)]
        ahead = []
        for n in range(len(units) + AHEAD):
            if n < len(units):
                ahead.append(score(*units[n]))
            if n >= AHEAD:
                mix(*units[n - AHEAD], ahead[n - AHEAD])

    def settle(j):
        at = pl.ds(pl.multiple_of(j * some, some), some)
        second = x_ref[at, :] + dot(att_ref[at, :], wo_low_ref[...])
        second_ref[at, :] = second
        unit, _ = normalize(second)
        act_two_ref[at, :] = (unit * gain_two_ref[...]).astype(BF16)

    def settle_out(j):
        for n in range(4, 8):
            out_copy(n, j).start()

    def step(j, _):
        settle(j - 1)
        attend(j)
        settle_out(j - 1)
        return 0

    attend(0)
    lax.fori_loop(1, parts, step, 0)
    settle(parts - 1)
    settle_out(parts - 1)
    for n in range(8):
        for i in range(tiles if n < 4 else parts):
            out_copy(n, i).wait()
    pltpu.make_async_copy(share_ref, share_far, share_sem).wait()


def forward(perm, mask, other, perm_row, mask_row, gain_one, gain_two, x, wq, wk, wv, ws, wo, w_up, w_down, tile=512):
    rows, width = x.shape
    blocks = rows // BLOCK
    tiles = rows // tile
    smem = pl.BlockSpec(memory_space=pltpu.SMEM)
    vmem = pl.BlockSpec(memory_space=pltpu.VMEM)
    hbm = pl.BlockSpec(memory_space=pltpu.HBM)
    low = ((rows, width), BF16)
    probs = ((2 * rows, HEADS * BLOCK), BF16)
    full = ((rows, width), F32)
    share = ((2 * ITERS, blocks, width), F32)
    plan = ((blocks, width), F32)
    packed = ((2, width, width), BF16)
    return pl.pallas_call(
        functools.partial(forward_kernel, tile=tile),
        in_specs=[smem] * 3 + [vmem] * 4 + [hbm] * 8,
        out_specs=[hbm] * 9 + [vmem] * 5,
        out_shape=[far_shape(*s) for s in (low, low, low, low, probs, low, full, low, share)]
        + [near_shape(*s) for s in (plan, plan, plan)]
        + [far_shape((1, width), F32), near_shape(*packed)],
        scratch_shapes=[pltpu.VMEM(*full), pltpu.VMEM((5, width, width), F32), pltpu.VMEM((width, 3 * width), BF16)]
        + [pltpu.VMEM((width, width), BF16)]
        + [pltpu.VMEM(*s) for s in (low, low, low, low, probs, low, full, low, share)]
        + [
            pltpu.VMEM((2, width, width), F32),
            pltpu.SemaphoreType.DMA((tiles + 5,)),
            pltpu.SemaphoreType.DMA((8, rows // (8 * BLOCK))),
            pltpu.SemaphoreType.DMA,
            pltpu.SemaphoreType.DMA((2,)),
        ],
        compiler_params=params(40),
        cost_estimate=cost(25),
        name="forward",
    )(
        perm, mask, other, perm_row, mask_row, gain_one, gain_two, far(x), far(wq), far(wk), far(wv), far(ws), far(wo),
        far(w_up), far(w_down),
    )


def attend_back_kernel(
    perm_ref, chosen_ref, gatt_ref, q_ref, probs_ref, k_ref, v_ref,
    gq_ref, gk_ref, gv_ref, gch_ref,
    own_k_ref, far_k_ref, own_v_ref, far_v_ref, *, group, part,
):
    rows, width = gq_ref.shape
    parts = rows // (part * BLOCK)
    masks = head_masks(BLOCK)
    lanes = slice(group * width, (group + 1) * width)

    def ahead(block):
        partner = perm_ref[block]
        own_at = pl.ds(pl.multiple_of(block * BLOCK, BLOCK), BLOCK)
        far_at = pl.ds(pl.multiple_of(partner * BLOCK, BLOCK), BLOCK)
        probs_at = pl.ds(pl.multiple_of(block * 2 * BLOCK, 2 * BLOCK), 2 * BLOCK)
        grads = expand(gatt_ref[own_at, lanes], masks)
        far_values = v_ref[far_at, lanes].astype(F32)
        chosen = chosen_ref[pl.ds(block, 1), lanes]
        values = jnp.concatenate([v_ref[own_at, lanes], (far_values * chosen).astype(BF16)], axis=0)
        probs_low = probs_ref[probs_at, group * GROUP_ROWS : (group + 1) * GROUP_ROWS]
        grad_probs = dot_nt(values, grads)
        grad_values = dot(probs_low, grads)
        far_grad = grad_values[BLOCK:]
        gch_ref[pl.ds(block, 1), :] = jnp.sum(far_grad * far_values, axis=0, keepdims=True)
        own_v_ref[own_at, :] = grad_values[:BLOCK]
        far_v_ref[far_at, :] = far_grad * chosen
        return grad_probs

    def behind(block, grad_probs):
        partner = perm_ref[block]
        own_at = pl.ds(pl.multiple_of(block * BLOCK, BLOCK), BLOCK)
        far_at = pl.ds(pl.multiple_of(partner * BLOCK, BLOCK), BLOCK)
        probs_at = pl.ds(pl.multiple_of(block * 2 * BLOCK, 2 * BLOCK), 2 * BLOCK)
        queries = expand(q_ref[own_at, lanes], masks)
        keys = jnp.concatenate([k_ref[own_at, lanes], k_ref[far_at, lanes]], axis=0)
        probs = probs_ref[probs_at, group * GROUP_ROWS : (group + 1) * GROUP_ROWS].astype(F32)
        total = jnp.sum(probs * grad_probs, axis=0, keepdims=True)
        grad_scores = (probs * (grad_probs - total)).astype(BF16)
        grad_keys = dot(grad_scores, queries) * FACTOR
        gq_ref[own_at, :] = (fold(dot_tn(grad_scores, keys), masks) * FACTOR).astype(BF16)
        own_k_ref[own_at, :] = grad_keys[:BLOCK]
        far_k_ref[far_at, :] = grad_keys[BLOCK:]

    def body(j, _):
        products = []
        for n in range(part + AHEAD):
            if n < part:
                products.append(ahead(j * part + n))
            if n >= AHEAD:
                behind(j * part + n - AHEAD, products[n - AHEAD])
        return 0

    lax.fori_loop(0, parts, body, 0)
    gk_ref[...] = (own_k_ref[...] + far_k_ref[...]).astype(BF16)
    gv_ref[...] = (own_v_ref[...] + far_v_ref[...]).astype(BF16)


def attend_back(perm, q, gatt, probs, k, v, chosen, group, part=8):
    rows = q.shape[0]
    smem = pl.BlockSpec(memory_space=pltpu.SMEM)
    vmem = pl.BlockSpec(memory_space=pltpu.VMEM)
    low = ((rows, GROUP_WIDTH), BF16)
    full = ((rows, GROUP_WIDTH), F32)
    return pl.pallas_call(
        functools.partial(attend_back_kernel, group=group, part=part),
        in_specs=[smem] + [vmem] * 6,
        out_specs=[vmem] * 4,
        out_shape=[near_shape(*s) for s in (low, low, low, ((rows // BLOCK, GROUP_WIDTH), F32))],
        scratch_shapes=[pltpu.VMEM(*full)] * 4,
        compiler_params=params(12),
        cost_estimate=cost(10),
        name="attend_back",
    )(perm, near(chosen), near(gatt), near(q), near(probs), near(k), near(v))


def gelu_pair(up):
    square = up * up
    inner = 0.7978845608028654 * 0.044715
    half = 0.5 + 0.5 * jnp.tanh(up * (0.7978845608028654 + inner * square))
    value = up * half
    slope = half + (2.0 * value) * (1.0 - half) * (0.7978845608028654 + 3.0 * inner * square)
    return value, slope


def spread(out_ref, acc_ref, where, lanes):
    chunks, size = out_ref.shape[0], out_ref.shape[-2]
    for r in range(chunks):
        at = pl.multiple_of((r ^ where) * size, size)
        out_ref[r, :, lanes] = acc_ref[pl.ds(at, size), :].astype(out_ref.dtype)


class Copies:
    def __init__(self, source, target, sems, tile):
        self.source, self.target, self.sems, self.tile = source, target, sems, tile

    def copy(self, i):
        at = pl.ds(pl.multiple_of(i * self.tile, self.tile), self.tile)
        return pltpu.make_async_copy(self.source.at[at, :], self.target.at[at, :], self.sems.at[i])

    def start(self, i):
        self.copy(i).start()

    def wait(self, i):
        self.copy(i).wait()


def quarter_math(act, cot_low, weights_ref, up_acc, down_acc):
    value, slope = gelu_pair(dot(act, weights_ref[0]))
    hidden = value.astype(BF16)
    grad_up = (dot_nt(cot_low, weights_ref[1]) * slope).astype(BF16)
    up_acc[...] += dot_tn(act, grad_up)
    down_acc[...] += dot_tn(cot_low, hidden)
    return hidden, dot_nt(grad_up, weights_ref[0])


def quarter_kernel(*refs, kind, tile, tally):
    if tally:
        mask_ref, refs = refs[0], refs[1:]
    where_ref, act_ref, weights_ref = refs[:3]
    if kind == "first":
        cot_far, hidden_far, grad_ref, piece_ref, low_ref, act_ref = refs[3:9]
        hidden_ref, up_acc, down_acc, hidden_sems, cot_ref, cot_sems, act_sems = refs[9:]
    elif kind == "middle":
        low_ref, sofar_ref, hidden_far, grad_ref, piece_ref = refs[3:8]
        hidden_ref, up_acc, down_acc, hidden_sems = refs[8:]
    else:
        low_ref, sofar_ref, gain_ref, entropy_ref, cot_far, second_far, att_far, wo_far = refs[3:11]
        hidden_far, gsec_far, piece_ref, gatt_ref, gout_ref = refs[11:16]
        hidden_ref, up_acc, down_acc, hidden_sems, cot_ref, cot_sems = refs[16:22]
        second_ref, second_sems, att_ref, att_sems, gsec_ref, gsec_sems = refs[22:28]
        wo_ref, wo_low_ref, wo_sem, out_acc, gain_acc, column_ref, sum_ref, second_low_ref = refs[28:]
    rows, width = act_ref.shape
    tiles = rows // tile
    hidden_out = Copies(hidden_ref, hidden_far, hidden_sems, tile)
    ins = []
    if kind == "first":
        ins = [Copies(cot_far, cot_ref, cot_sems, tile), Copies(refs[1], act_ref, act_sems, tile)]
    if kind == "last":
        ins = [
            Copies(second_far, second_ref, second_sems, tile),
            Copies(cot_far, cot_ref, cot_sems, tile),
            Copies(att_far, att_ref, att_sems, tile),
        ]
        gsec_out = Copies(gsec_ref, gsec_far, gsec_sems, tile)
    for i in range(tiles):
        for copies in ins:
            copies.start(i)
        if kind == "last" and i == 0:
            wo_copy = pltpu.make_async_copy(wo_far, wo_ref, wo_sem)
            wo_copy.start()
    up_acc[...] = jnp.zeros_like(up_acc)
    down_acc[...] = jnp.zeros_like(down_acc)
    if kind == "last":
        out_acc[...] = jnp.zeros_like(out_acc)
        gain_acc[...] = jnp.zeros_like(gain_acc)

    def multiply(i):
        at = pl.ds(pl.multiple_of(i * tile, tile), tile)
        if kind == "first":
            low_ref[at, :] = cot_ref[at, :].astype(BF16)
        hidden, grad = quarter_math(act_ref[at, :], low_ref[at, :], weights_ref, up_acc, down_acc)
        hidden_ref[at, :] = hidden
        if kind == "first":
            grad_ref[at, :] = grad
        elif kind == "middle":
            grad_ref[at, :] = sofar_ref[at, :] + grad
        else:
            sum_ref[i % 2] = sofar_ref[at, :] + grad

    def settle(i):
        at = pl.ds(pl.multiple_of(i * tile, tile), tile)
        grad = sum_ref[i % 2]
        unit, inverse = normalize(second_ref[at, :])
        gain_acc[...] += jnp.sum(grad * unit, axis=0, keepdims=True)
        grad_second = cot_ref[at, :] + norm_grad(grad, unit, inverse, gain_ref[...])
        gsec_ref[at, :] = grad_second
        second_low_ref[...] = grad_second.astype(BF16)

    def settle_back(i):
        at = pl.ds(pl.multiple_of(i * tile, tile), tile)
        second_low = second_low_ref[...]
        gatt_ref[at, :] = dot_nt(second_low, wo_low_ref[...]).astype(BF16)
        out_acc[...] += dot_tn(att_ref[at, :], second_low)

    def body(i, _):
        for copies in ins:
            copies.wait(i - 1 if kind == "last" else i)
        if kind == "last":
            settle(i - 1)
        multiply(i)
        if kind == "last":
            settle_back(i - 1)
            gsec_out.start(i - 1)
        hidden_out.start(i)
        return 0

    if kind == "last":
        multiply(0)
        hidden_out.start(0)
        wo_copy.wait()
        wo_low_ref[...] = wo_ref[...].astype(BF16)
        lax.fori_loop(1, tiles, body, 0)
        for copies in ins:
            copies.wait(tiles - 1)
        settle(tiles - 1)
        gsec_out.start(tiles - 1)
        settle_back(tiles - 1)
    else:
        lax.fori_loop(0, tiles, body, 0)
    size = width // piece_ref.shape[0]
    spread(piece_ref.at[:, :size], up_acc, where_ref[0], slice(None))
    spread(piece_ref.at[:, size : 2 * size], down_acc, where_ref[0], slice(None))
    if tally:
        shape = (TALLY_ROWS, weights_ref.shape[2])
        mine = lax.broadcasted_iota(jnp.int32, shape, 1) == where_ref[3]
        count = jnp.sum(mask_ref[...].astype(F32), axis=1, keepdims=True)
        row = jnp.where(mine, jnp.broadcast_to(count, shape), 0.0).astype(BF16)
        for r in range(piece_ref.shape[0]):
            piece_ref[r, 2 * size :, :] = row
    if kind == "last":
        spread(gout_ref, out_acc, where_ref[2], slice(0, width))
        half = (LANES // 2, width)
        column_ref[...] = jnp.concatenate(
            [jnp.broadcast_to(gain_acc[...], half), jnp.broadcast_to(entropy_ref[...], half)], axis=0
        ).T
        spread(gout_ref, column_ref, where_ref[2], slice(width, width + LANES))
    for i in range(tiles):
        hidden_out.wait(i)
        if kind == "last":
            gsec_out.wait(i)


def feed_quarter(
    kind, where, act, weights, cot, sofar=None, extra=None, mask_row=None, row_chunks=1, out_chunks=1, tile=512
):
    rows, width = act.shape
    units = weights.shape[2]
    tiles = rows // tile
    smem = pl.BlockSpec(memory_space=pltpu.SMEM)
    vmem = pl.BlockSpec(memory_space=pltpu.VMEM)
    hbm = pl.BlockSpec(memory_space=pltpu.HBM)
    tally = mask_row is not None
    size = 2 * (width // row_chunks) + (TALLY_ROWS if tally else 0)
    piece = near_shape((row_chunks, size, units), BF16)
    low = near_shape((rows, width), BF16)
    full = near_shape((rows, width), F32)
    hidden = far_shape((rows, units), BF16)
    sems = pltpu.SemaphoreType.DMA((tiles,))
    low_buffer, full_buffer = pltpu.VMEM((rows, width), BF16), pltpu.VMEM((rows, width), F32)
    square = pltpu.VMEM((width, width), F32)
    scratch = [pltpu.VMEM((rows, units), BF16), square, square, sems]
    if kind == "first":
        operands = (far(cot),)
        in_specs = [hbm]
        out_shape, out_specs = [hidden, full, piece, low, low], [hbm] + [vmem] * 4
        scratch = scratch + [full_buffer, sems, sems]
        limit = 24
    elif kind == "middle":
        operands = (near(cot), near(sofar))
        in_specs = [vmem] * 2
        out_shape, out_specs = [hidden, full, piece], [hbm] + [vmem] * 2
        limit = 18
    else:
        full_cot, second, att, w_out, gain, entropy = extra
        operands = (near(cot), near(sofar), gain, entropy, far(full_cot), far(second), far(att), far(w_out))
        in_specs = [vmem] * 4 + [hbm] * 4
        out_piece = near_shape((out_chunks, width // out_chunks, width + LANES), BF16)
        out_shape = [hidden, far_shape((rows, width), F32), piece, low, out_piece]
        out_specs = [hbm] * 2 + [vmem] * 3
        scratch = scratch + [full_buffer, sems, full_buffer, sems, low_buffer, sems, full_buffer, sems]
        scratch = scratch + [square, pltpu.VMEM((width, width), BF16), pltpu.SemaphoreType.DMA]
        scratch = scratch + [square, pltpu.VMEM((1, width), F32), pltpu.VMEM((width, LANES), F32)]
        scratch = scratch + [pltpu.VMEM((2, tile, width), F32), pltpu.VMEM((tile, width), BF16)]
        limit = 32
    return pl.pallas_call(
        functools.partial(quarter_kernel, kind=kind, tile=tile, tally=tally),
        in_specs=([vmem] if tally else []) + [smem, hbm if kind == "first" else vmem, vmem] + in_specs,
        out_specs=out_specs,
        out_shape=out_shape,
        scratch_shapes=scratch,
        compiler_params=params(limit),
        cost_estimate=cost(9),
        name="feed_" + kind,
    )(
        *([mask_row] if tally else []), where, far(act) if kind == "first" else near(act), near(weights), *operands
    )


def output_kernel(second_ref, *refs):
    out_ref = refs[-1]
    count = (len(refs) - 1) // 2
    total = second_ref[...]
    for hidden_ref, weights_ref in zip(refs[:count], refs[count : 2 * count]):
        total = total + dot(hidden_ref[...], weights_ref[0])
    out_ref[...] = total


def layer_output(second, hidden, weights, tile=512):
    rows, width = second.shape
    units = hidden[0].shape[1]
    down = pl.BlockSpec((1, units, width), lambda *_: (1, 0, 0), pipeline_mode=pl.Buffered(1))
    return pl.pallas_call(
        output_kernel,
        grid=(rows // tile,),
        in_specs=[rows_of(tile, width)] + [rows_of(tile, units)] * len(hidden) + [down] * len(hidden),
        out_specs=rows_of(tile, width),
        out_shape=far_shape((rows, width), F32),
        compiler_params=params(16),
        cost_estimate=cost(8),
        name="layer_output",
    )(near(second), *[far(array) for array in hidden], *[near(array) for array in weights])


def head_kernel(*refs, count):
    where_ref, pen_ref, act_ref = refs[:3]
    groups = [refs[3 + 4 * g : 7 + 4 * g] for g in range(count)]
    share_ref, log_ref, sum_ref, w_ref, perm_ref, mask_ref, out_ref, tally_ref = refs[3 + 4 * count : 11 + 4 * count]
    piece_ref, gsum_ref, total_ref, glog_ref, acc_ref = refs[11 + 4 * count :]
    block_total = jnp.sum(tally_ref[...].astype(F32), axis=1, keepdims=True)
    block_total = jnp.sum(block_total, axis=0, keepdims=True)
    total_ref[...] = jnp.broadcast_to(block_total, total_ref.shape)
    coef = pen_ref[0] / (HEADS * block_total)
    blocks, width = sum_ref.shape
    cols = acc_ref.shape[1]
    wide = 2 * blocks
    first, position = lane_tiles(blocks)
    hot = position == down_rows(perm_ref[...], wide)
    weight = coef * down_rows(mask_ref[...], wide)
    act = act_ref[...]
    for g, group in enumerate(groups):
        for index in range(3):
            acc_ref[...] = dot_tn(act, group[index][...])
            at = index * width + g * cols
            spread(piece_ref, acc_ref, where_ref[2], slice(at, at + cols))
        for pair in range(cols // wide):
            at = g * cols + pair * wide
            span = slice(at, at + wide)
            plan = share_ref[2 * ITERS - 1, :, span]
            gch = segment_sum(group[3][:, pair * wide : (pair + 1) * wide], first)
            grad = plan * (jnp.where(hot, blocks * gch, 0.0) - weight * (log_ref[:, span] + 1.0))
            for level in range(2 * ITERS - 1, -1, -1):
                if level % 2:
                    total = jnp.sum(grad, axis=0, keepdims=True)
                else:
                    total = segment_sum(grad, first)
                grad = grad - share_ref[level, :, span] * total
            glog_ref[:, span] = grad
    for g in range(count):
        at = slice(g * cols, (g + 1) * cols)
        acc_ref[...] = lax.dot_general(
            sum_ref[...], glog_ref[:, at], TN, precision=HIGHEST, preferred_element_type=F32
        )
        spread(piece_ref, acc_ref, where_ref[2], slice(3 * width + g * cols, 3 * width + (g + 1) * cols))
    gsum_ref[...] = lax.dot_general(glog_ref[...], w_ref[...], NT, precision=HIGHEST, preferred_element_type=F32)
    piece_ref[:, :, 4 * width :] = out_ref[...]


def head_grads(
    where, pen_weight, act, groups, shares, plan_log, sums, w_sort, perm_row, mask_row, out_piece, tallies, chunks
):
    rows, width = act.shape
    blocks = sums.shape[0]
    cols = groups[0][0].shape[1]
    smem = pl.BlockSpec(memory_space=pltpu.SMEM)
    vmem = pl.BlockSpec(memory_space=pltpu.VMEM)
    flat = [near(array) for group in groups for array in group]
    piece = (chunks, width // chunks, 4 * width + out_piece.shape[2])
    return pl.pallas_call(
        functools.partial(head_kernel, count=len(groups)),
        in_specs=[smem] * 2 + [vmem] * (9 + len(flat)),
        out_specs=[vmem] * 3,
        out_shape=[near_shape(piece, BF16), near_shape((blocks, width), F32), near_shape((1, LANES), F32)],
        scratch_shapes=[pltpu.VMEM((blocks, width), F32), pltpu.VMEM((width, cols), F32)],
        compiler_params=params(14),
        cost_estimate=cost(6),
        name="head_grads",
    )(
        where, pen_weight, near(act), *flat, near(shares), near(plan_log), near(sums), near(w_sort), perm_row, mask_row,
        near(out_piece), tallies,
    )


def input_kernel(*refs):
    count = (len(refs) - 9) // 3
    groups = [refs[3 * g : 3 * g + 3] for g in range(count)]
    gsum_ref, x_ref, gsec_ref, gain_ref, wq_ref, wk_ref, wv_ref, out_ref, w_ref = refs[3 * count :]

    @pl.when(pl.program_id(0) == 0)
    def _():
        for which, ref in enumerate((wq_ref, wk_ref, wv_ref)):
            w_ref[which] = ref[...].astype(BF16)

    rows, width = x_ref.shape
    grad = jnp.zeros((rows, width), F32)
    for g, group in enumerate(groups):
        for which, ref in enumerate(group):
            cols = ref.shape[1]
            grad = grad + dot_nt(ref[...], w_ref[which, :, g * cols : (g + 1) * cols])
    grad = (grad.reshape(rows // BLOCK, BLOCK, width) + gsum_ref[...][:, None, :]).reshape(rows, width)
    unit, inverse = normalize(x_ref[...])
    out_ref[...] = gsec_ref[...] + norm_grad(grad, unit, inverse, gain_ref[...])


def input_grad(groups, gsum, x, gsec, gain, wq, wk, wv, tile=512):
    rows, width = x.shape
    weight = pl.BlockSpec((width, width), lambda *_: (0, 0), pipeline_mode=pl.Buffered(1))
    flat = [array for group in groups for array in group]
    return pl.pallas_call(
        input_kernel,
        grid=(rows // tile,),
        in_specs=[rows_of(tile, array.shape[1]) for array in flat]
        + [rows_of(tile // BLOCK, width)]
        + [rows_of(tile, width)] * 2
        + [whole((1, width))]
        + [weight] * 3,
        out_specs=rows_of(tile, width),
        out_shape=far_shape((rows, width), F32),
        scratch_shapes=[pltpu.VMEM((3, width, width), BF16)],
        compiler_params=params(20),
        cost_estimate=cost(10),
        name="input_grad",
    )(*[near(array) for array in flat], gsum, far(x), far(gsec), gain, far(wq), far(wk), far(wv))


def pack_kernel(core_ref, up_ref, down_ref, mine_ref):
    mine_ref[0] = up_ref[...].astype(BF16)
    mine_ref[1] = down_ref[...].astype(BF16)


def pack_weights(core, w_up, w_down):
    width, units = w_up.shape
    half = units // 2
    shape = (2, width, half)
    return pl.pallas_call(
        pack_kernel,
        grid_spec=pltpu.PrefetchScalarGridSpec(
            num_scalar_prefetch=1,
            grid=(1,),
            in_specs=[
                pl.BlockSpec((width, half), lambda step, core: (0, core[0])),
                pl.BlockSpec((half, width), lambda step, core: (core[0], 0)),
            ],
            out_specs=whole(shape),
        ),
        out_shape=near_shape(shape, BF16),
        compiler_params=params(12),
        cost_estimate=cost(2),
        name="pack_weights",
    )(core, far(w_up), far(w_down))


def finish_feed_kernel(*refs):
    where_ref, parts = refs[0], refs[1:-3]
    up_ref, down_ref, turn_ref = refs[-3:]
    some, size, units = parts[0].shape
    size = size // 2
    half = len(parts) // 2
    for flip in range(2):
        column = pl.multiple_of((where_ref[1] ^ flip) * units, units)
        for n, ref in enumerate(parts[flip * half : (flip + 1) * half]):
            for r in range(some):
                at = pl.multiple_of(((n * some + r) ^ where_ref[0]) * size, size)
                up_ref[pl.ds(at, size), pl.ds(column, units)] = ref[r, :size].astype(F32)
                turn_ref[pl.ds(at, size), :] = ref[r, size:].astype(F32)
        down_ref[pl.ds(column, units), :] = turn_ref[...].T


def finish_feed(where, parts):
    some, size, units = parts[0].shape
    width = len(parts) // 2 * some * size // 2
    vmem = pl.BlockSpec(memory_space=pltpu.VMEM)
    return pl.pallas_call(
        finish_feed_kernel,
        in_specs=[pl.BlockSpec(memory_space=pltpu.SMEM)] + [vmem] * len(parts),
        out_specs=[vmem, vmem],
        out_shape=[far_shape((width, 2 * units), F32), far_shape((2 * units, width), F32)],
        scratch_shapes=[pltpu.VMEM((width, units), F32)],
        compiler_params=params(16),
        cost_estimate=cost(3),
        name="finish_feed",
    )(where, *parts)


def finish_kernel(*refs):
    where_ref, parts = refs[0], refs[1:-22]
    weights = refs[-22:-18]
    gain_ref, total_ref = refs[-18:-16]
    fars = refs[-16:-11]
    gain_one_ref, gain_two_ref, penalty_ref = refs[-11:-8]
    nears = refs[-8:-3]
    one_ref, two_ref, sems = refs[-3:]
    width = gain_ref.shape[1]
    some, size = parts[0].shape[:2]
    total = jnp.zeros((width, LANES), F32)
    copies = []
    for index, near_ref in enumerate(nears):
        for n, part_ref in enumerate(parts):
            for r in range(some):
                rows = pl.ds(pl.multiple_of(((n * some + r) ^ where_ref[2]) * size, size), size)
                near_ref[rows, :] = part_ref[r, :, index * width : (index + 1) * width].astype(F32)
                if index == 0:
                    two_ref[rows, :] = part_ref[r, :, 5 * width :].astype(F32)
        copies.append(pltpu.make_async_copy(near_ref, fars[index], sems.at[index]))
        copies[-1].start()
    for at in range(0, width, LANES):
        span = slice(at, at + LANES)
        for grad, weight in zip(nears[:3], weights[:3]):
            total = total + grad[:, span] * weight[:, span].astype(BF16).astype(F32)
        total = total + nears[3][:, span] * weights[3][:, span]
    one_ref[...] = total
    gain_one_ref[...] = jnp.sum(one_ref[...].T, axis=0, keepdims=True) / gain_ref[...]
    turned = two_ref[...].T
    gain_two_ref[...] = turned[:1, :]
    entropy = jnp.sum(turned[LANES // 2 : LANES // 2 + 1, :], axis=1, keepdims=True)
    penalty_ref[...] = entropy / (HEADS * total_ref[:, :1])
    for copy in copies:
        copy.wait()


def finish(where, parts, wq, wk, wv, ws, gain, total):
    width = wq.shape[0]
    vmem = pl.BlockSpec(memory_space=pltpu.VMEM)
    hbm = pl.BlockSpec(memory_space=pltpu.HBM)
    square = far_shape((width, width), F32)
    row = shape_of((1, width), F32)
    return pl.pallas_call(
        finish_kernel,
        in_specs=[pl.BlockSpec(memory_space=pltpu.SMEM)] + [vmem] * (6 + len(parts)),
        out_specs=[hbm] * 5 + [vmem] * 3,
        out_shape=[square] * 5 + [row] * 2 + [shape_of((1, 1), F32)],
        scratch_shapes=[pltpu.VMEM((width, width), F32)] * 5
        + [pltpu.VMEM((width, LANES), F32)] * 2
        + [pltpu.SemaphoreType.DMA((5,))],
        compiler_params=params(16),
        cost_estimate=cost(5),
        name="finish",
    )(where, *parts, near(wq), near(wk), near(wv), near(ws), gain, total)


MP, CORE, X, Z_LOW, Z_HIGH = 1, 2, 4, 8, 16
CORE_STEP = ((CORE,), (CORE,))
FEED_STEPS = ((X,), (Z_LOW, Z_HIGH, Z_LOW + Z_HIGH))
HEAD_STEPS = ((CORE,), (MP, X, MP + X), (Z_LOW, Z_HIGH, Z_LOW + Z_HIGH))


def swap(array, flip):
    count = lax.axis_size("batch") * lax.axis_size("mp")
    return lax.ppermute(array, ("batch", "mp"), [(i, i ^ flip) for i in range(count)])


def place(steps, index):
    result = jnp.int32(0)
    for step in steps:
        for bit in reversed(step[: (len(step) + 1).bit_length() - 1]):
            result = 2 * result + ((index & bit) > 0).astype(jnp.int32)
    return result


def add_low(first, *others):
    total = first.astype(F32)
    for array in others:
        total = total + array.astype(F32)
    return total.astype(BF16)


class Walk:
    def __init__(self, pieces, steps):
        self.pieces = pieces
        self.down = list(steps)
        self.up = list(reversed(steps))
        self.parts, self.arrived = None, []

    def added(self, plan, count):
        pieces = self.pieces + [plan.after(array) for array in self.arrived]
        self.arrived = []
        size = pieces[0].shape[0] // count
        if len(pieces) == 1 and count == 1:
            return pieces
        return [
            add_low(*[piece[n * size : (n + 1) * size] for piece in pieces]) if len(pieces) > 1
            else pieces[0][n * size : (n + 1) * size]
            for n in range(count)
        ]

    def reduce(self, plan):
        flips = self.down.pop(0)
        parts = self.added(plan, len(flips) + 1)
        self.arrived = [swap(plan.after(part), flip) for part, flip in zip(parts[1:], flips)]
        self.pieces = parts[:1]
        return self.arrived

    def reduced(self, plan):
        return self.added(plan, 1)[0]

    def gather(self, plan, value):
        flips = self.up.pop(0)
        self.parts = [value]
        mine = plan.after(value)
        self.arrived = [swap(mine, flip) for flip in flips]
        return self.arrived

    def gathered(self, plan):
        parts = self.parts + [plan.after(array) for array in self.arrived]
        self.arrived = []
        return parts


class Schedule:
    def __init__(self):
        self.pending, self.launched, self.done = [], [], None

    def after(self, array):
        return lax.optimization_barrier((array, self.done))[0]

    def enter(self, small):
        tied = lax.optimization_barrier((small, *self.pending))[0]
        self.pending, self.launched = self.launched, []
        return tied

    def leave(self, *arrays):
        self.pending.extend(arrays)
        self.done = arrays[0]

    def launch(self, *arrays):
        for array in arrays:
            self.launched.extend(array if isinstance(array, list) else [array])


def local_small(
    inputs, cotangent, block_perm, block_mask, pen_weight, w_query, w_key, w_value, w_out, w_sort,
    gain_one, gain_two, w_up, w_down,
):
    _, rows, width = inputs.shape
    x = inputs.reshape(rows, width)
    cot = cotangent.reshape(rows, width)
    perm = block_perm.reshape(-1)
    mask = block_mask.reshape(-1)
    perm_row = block_perm.reshape(1, -1)
    mask_row = block_mask.reshape(1, -1)
    gain_one_row = gain_one.reshape(1, width)
    gain_two_row = gain_two.reshape(1, width)
    batch, mp = lax.axis_index("batch"), lax.axis_index("mp")
    core = batch & 1
    index = batch * 2 + mp
    where = jnp.stack([place(FEED_STEPS, index), core, place(HEAD_STEPS, index), index])
    row_chunks, out_chunks = 8, 32
    plan = Schedule()

    count = jnp.broadcast_to(jnp.sum(mask.astype(F32)), (8, LANES))
    own_a = pack_weights(core.reshape(1), w_up, w_down)
    far_a = swap(own_a, MP)
    plan.leave(own_a)
    act_one, q, k, v, probs, att, second, act_two_far, shares, sums, plan_log, chosen, entropy, own_b = forward(
        perm, mask, (1 - core).reshape(1), perm_row, mask_row, plan.enter(gain_one_row), gain_two_row, x,
        w_query, w_key, w_value, w_sort, w_out, w_up, w_down,
    )
    plan.leave(entropy)
    plan.pending.append(far_a)

    far_b = swap(plan.after(far_a), CORE)
    plan.launch(far_b)
    hid_a, sofar, other_piece, cot_low, act_two = feed_quarter(
        "first", plan.enter(where), act_two_far, far_a, cot, mask_row=mask_row, row_chunks=row_chunks
    )
    plan.leave(other_piece)

    hid_b, sofar, piece = feed_quarter(
        "middle", plan.enter(where), act_two, far_b, cot_low, sofar, mask_row=mask_row, row_chunks=row_chunks
    )
    plan.leave(piece)

    arrived = swap(plan.after(piece), CORE)
    plan.launch(arrived)
    hid_c, sofar, piece = feed_quarter(
        "middle", plan.enter(where), act_two, own_b, cot_low, sofar, row_chunks=row_chunks
    )
    plan.leave(piece)

    other = Walk([other_piece, plan.after(arrived)], FEED_STEPS)
    arrived = swap(plan.after(piece), CORE)
    plan.launch(arrived, other.reduce(plan))
    extra = (cot, second, att, w_out, gain_two_row, entropy)
    hid_d, grad_second, piece, grad_att, out_piece = feed_quarter(
        "last", plan.enter(where), act_two, own_a, cot_low, sofar, extra, None, row_chunks, out_chunks
    )
    plan.leave(grad_att)

    own = Walk([piece, plan.after(arrived)], FEED_STEPS)
    plan.launch(own.reduce(plan), other.reduce(plan))
    groups = [attend_back(plan.enter(perm), q, grad_att, probs, k, v, chosen, 0)]
    plan.leave(groups[0][3])

    other_sum = other.reduced(plan)
    crossed = swap(plan.after(other_sum), MP)
    plan.launch(crossed, own.reduce(plan))
    plan.pending.extend(own.pieces)
    groups.append(attend_back(plan.enter(perm), q, grad_att, probs, k, v, chosen, 1))
    plan.leave(groups[1][3])

    crossed = plan.after(crossed)
    rows_fed = own.pieces[0].shape[1]
    tallies = jnp.concatenate([other_sum[0, rows_fed:], crossed[0, rows_fed:]], axis=0)
    tallies = tallies.reshape(2, TALLY_ROWS, -1)[:, 0]
    own.pieces.append(crossed[:, :rows_fed])
    value = own.reduced(plan)
    plan.pending.append(value)
    piece, gsum, block_total = head_grads(
        plan.enter(where), pen_weight, act_one, groups, shares, plan_log, sums, w_sort, perm_row, mask_row, out_piece,
        tallies, out_chunks,
    )
    plan.leave(gsum)

    head = Walk([piece], HEAD_STEPS)
    plan.pending.extend(head.reduce(plan))
    own.gather(plan, value)
    plan.launch(head.reduce(plan))
    plan.pending.extend(head.pieces)
    grad_input = input_grad(
        [group[:3] for group in groups], gsum, x, grad_second, plan.enter(gain_one_row), w_query, w_key, w_value
    )
    plan.leave(grad_input)

    head.reduce(plan)
    own.gather(plan, jnp.concatenate(own.gathered(plan), axis=0))
    head.gather(plan, head.reduced(plan))
    value = jnp.concatenate(head.gathered(plan), axis=0)
    plan.pending.append(value)
    head.gather(plan, value)
    quarters = (far_a, far_b, own_b, own_a)
    output = layer_output(plan.enter(second), (hid_a, hid_b, hid_c, hid_d), quarters)
    plan.leave(output)

    parts = own.parts + own.arrived
    grad_up, grad_down = finish_feed(plan.enter(where), parts + [swap(part, CORE) for part in parts])
    plan.leave(grad_up)
    parts = head.gathered(plan)
    parts = parts + [swap(part, CORE) for part in parts]
    grad_query, grad_key, grad_value, grad_sort, grad_out, grad_gain_one, grad_gain_two, penalty = finish(
        where, parts, w_query, w_key, w_value, w_sort, gain_one_row, block_total
    )
    return (
        output.reshape(inputs.shape),
        penalty.reshape(1),
        grad_input.reshape(inputs.shape),
        grad_query,
        grad_key,
        grad_value,
        grad_out,
        grad_sort,
        grad_gain_one.reshape(width),
        grad_gain_two.reshape(width),
        grad_up,
        grad_down,
    )


def local_any(
    inputs, cotangent, block_perm, block_mask, pen_weight, w_query, w_key, w_value, w_out, w_sort,
    gain_one, gain_two, w_up, w_down,
):
    both = ("batch", "mp")
    _, rows, width = inputs.shape
    x = inputs.reshape(rows, width)
    cot = cotangent.reshape(rows, width)
    perm = block_perm.reshape(-1)
    mask = block_mask.reshape(-1)
    perm_row = block_perm.reshape(1, -1)
    mask_row = block_mask.reshape(1, -1)
    gain_one_row = gain_one.reshape(1, width)
    gain_two_row = gain_two.reshape(1, width)
    where = jnp.zeros((4,), jnp.int32)
    up_all = lax.all_gather(w_up.astype(BF16), "mp", axis=1, tiled=True)
    down_all = lax.all_gather(w_down.astype(BF16), "mp", axis=0, tiled=True)
    quarters = [
        jnp.stack([up_all[:, at : at + width], down_all[at : at + width]])
        for at in range(0, up_all.shape[1], width)
    ]
    act_one, q, k, v, probs, att, second, act_two_far, shares, sums, plan_log, chosen, entropy = forward(
        perm, mask, jnp.zeros((1,), jnp.int32), perm_row, mask_row, gain_one_row, gain_two_row, x,
        w_query, w_key, w_value, w_sort, w_out, w_query, w_query,
    )[:-1]
    tallies = jnp.broadcast_to(lax.psum(jnp.sum(mask_row).astype(F32), both) / width, (1, width))
    hidden, parts = [], []
    low, sofar = cot, None
    for index, weights in enumerate(quarters):
        if index == 0:
            hid, sofar, piece, low, act_two = feed_quarter("first", where, act_two_far, weights, low)
        elif index < len(quarters) - 1:
            hid, sofar, piece = feed_quarter("middle", where, act_two, weights, low, sofar)
        else:
            extra = (cot, second, att, w_out, gain_two_row, entropy)
            hid, grad_second, piece, grad_att, extra = feed_quarter(
                "last", where, act_two, weights, low, sofar, extra
            )
        hidden.append(hid)
        parts.append(piece[0])
    groups = [
        attend_back(perm, q, grad_att, probs, k, v, chosen, group) for group in range(width // GROUP_WIDTH)
    ]
    piece, gsum, block_total = head_grads(
        where, pen_weight, act_one, groups, shares, plan_log, sums, w_sort, perm_row, mask_row, extra, tallies, 1
    )
    grad_input = input_grad(
        [group[:3] for group in groups], gsum, x, grad_second, gain_one_row, w_query, w_key, w_value
    )
    output = layer_output(second, hidden, quarters)

    parts = jnp.concatenate(parts, axis=1).reshape(2, width, -1)
    parts = lax.psum(lax.psum_scatter(parts, "mp", scatter_dimension=2, tiled=True), "batch").astype(F32)
    grad_up, grad_down = parts[0], parts[1].T
    piece = lax.psum(piece, both)
    grad_query, grad_key, grad_value, grad_sort, grad_out, grad_gain_one, grad_gain_two, penalty = finish(
        where, [piece], w_query, w_key, w_value, w_sort, gain_one_row, block_total
    )
    return (
        output.reshape(inputs.shape),
        penalty.reshape(1),
        grad_input.reshape(inputs.shape),
        grad_query,
        grad_key,
        grad_value,
        grad_out,
        grad_sort,
        grad_gain_one.reshape(width),
        grad_gain_two.reshape(width),
        grad_up,
        grad_down,
    )


def solution(mesh):
    tokens = P(("batch", "mp"), None, None)
    blocks = P(("batch", "mp"), None)
    small = mesh.shape["batch"] == 16 and mesh.shape["mp"] == 2
    return jax.shard_map(
        local_small if small else local_any,
        mesh=mesh,
        in_specs=(tokens, tokens, blocks, blocks) + (P(),) * 8 + (P(None, "mp"), P("mp", None)),
        out_specs=(tokens, P(), tokens) + (P(),) * 7 + (P(None, "mp"), P("mp", None)),
        check_vma=False,
    )
```

```python
import functools

import jax
import jax.numpy as jnp
from jax import lax
from jax.experimental import pallas as pl
from jax.experimental.pallas import tpu as pltpu
from jax.sharding import PartitionSpec as P

HEADS = 8
HEAD_DIM = 64
BLOCK = 32
ITERS = 8
GROUP = 4
GROUP_WIDTH = GROUP * HEAD_DIM
GROUP_ROWS = GROUP * BLOCK
EPSILON = 1e-05
FACTOR = HEAD_DIM ** (-0.5)
HIGHEST = lax.Precision.HIGHEST
F32 = jnp.float32
BF16 = jnp.bfloat16
NT = (((1,), (1,)), ((), ()))
TN = (((0,), (0,)), ((), ()))
MIB = 1024 * 1024
LANES = 128
TALLY_ROWS = 16
AHEAD = 3


def dot(left, right):
    return jnp.dot(left, right, preferred_element_type=F32)


def dot_nt(left, right):
    return lax.dot_general(left, right, NT, preferred_element_type=F32)


def dot_tn(left, right):
    return lax.dot_general(left, right, TN, preferred_element_type=F32)


def shape_of(dims, dtype):
    return jax.ShapeDtypeStruct(dims, dtype)


def whole(dims):
    return pl.BlockSpec(dims, lambda *_: (0,) * len(dims))


def once(dims):
    return pl.BlockSpec(dims, lambda *_: (0,) * len(dims), pipeline_mode=pl.Buffered(1))


def rows_of(size, width):
    return pl.BlockSpec((size, width), lambda step, *_: (step, 0))


def params(mib):
    return pltpu.CompilerParams(vmem_limit_bytes=mib * MIB)


def far(array):
    return pltpu.with_memory_space_constraint(array, pltpu.HBM)


def near(array):
    return pltpu.with_memory_space_constraint(array, pltpu.VMEM)


def near_shape(dims, dtype):
    return pltpu.VMEM(dims, dtype)


def far_shape(dims, dtype):
    return pltpu.HBM(dims, dtype)


def cost(micros):
    return pl.CostEstimate(flops=int(micros * 1150000000), bytes_accessed=0, transcendentals=0)


def normalize(values):
    center = values - jnp.mean(values, axis=-1, keepdims=True)
    inverse = lax.rsqrt(jnp.mean(center * center, axis=-1, keepdims=True) + EPSILON)
    return center * inverse, inverse


def norm_grad(grad_rows, unit_rows, inverse, gain):
    scaled_rows = grad_rows * gain
    return inverse * (
        scaled_rows
        - jnp.mean(scaled_rows, axis=-1, keepdims=True)
        - unit_rows * jnp.mean(scaled_rows * unit_rows, axis=-1, keepdims=True)
    )


def segment_sum(tile, first):
    left = jnp.sum(jnp.where(first, tile, 0.0), axis=1, keepdims=True)
    right = jnp.sum(jnp.where(first, 0.0, tile), axis=1, keepdims=True)
    return jnp.where(first, left, right)


def segment_max(tile, first):
    left = jnp.max(jnp.where(first, tile, -jnp.inf), axis=1, keepdims=True)
    right = jnp.max(jnp.where(first, -jnp.inf, tile), axis=1, keepdims=True)
    return jnp.where(first, left, right)


def head_masks(rows):
    lane = lax.broadcasted_iota(jnp.int32, (rows, GROUP_WIDTH), 1)
    return [(lane >= h * HEAD_DIM) & (lane < (h + 1) * HEAD_DIM) for h in range(GROUP)]


def expand(rows, masks):
    zero = jnp.zeros_like(rows)
    return jnp.concatenate([jnp.where(mask, rows, zero) for mask in masks], axis=0)


def fold(rows, masks):
    parts = [rows[h * BLOCK : (h + 1) * BLOCK] for h in range(GROUP)]
    result = parts[GROUP - 1]
    for h in range(GROUP - 1):
        result = jnp.where(masks[h], parts[h], result)
    return result


def lane_tiles(blocks):
    lane = lax.broadcasted_iota(jnp.int32, (blocks, 2 * blocks), 1)
    return lane < blocks, jnp.where(lane < blocks, lane, lane - blocks).astype(F32)


def down_rows(row, wide):
    return jnp.broadcast_to(row.astype(F32), (wide, row.shape[1])).T


def balance_plans(logits, perm_row, mask_row, share_ref, log_ref, chosen_ref, entropy_ref):
    blocks = logits.shape[0]
    wide = 2 * blocks
    first, position = lane_tiles(blocks)
    hot = position == down_rows(perm_row, wide)
    real = down_rows(mask_row, wide) > 0.0
    for pair in range(logits.shape[1] // wide):
        span = slice(pair * wide, (pair + 1) * wide)
        tile = logits[:, span]
        for step in range(ITERS):
            top = segment_max(tile, first)
            powers = jnp.exp(tile - top)
            total = segment_sum(powers, first)
            tile = tile - (top + jnp.log(total))
            share_ref[2 * step, :, span] = powers * (1.0 / total)
            top = jnp.max(tile, axis=0, keepdims=True)
            powers = jnp.exp(tile - top)
            total = jnp.sum(powers, axis=0, keepdims=True)
            tile = tile - (top + jnp.log(total))
            if step < ITERS - 1:
                share_ref[2 * step + 1, :, span] = powers * (1.0 / total)
        plan = jnp.exp(tile)
        share_ref[2 * ITERS - 1, :, span] = plan
        log_ref[:, span] = tile
        chosen_ref[:, span] = blocks * segment_sum(jnp.where(hot, plan, 0.0), first)
        entropy_ref[:, span] = -jnp.sum(jnp.where(real, plan * tile, 0.0), axis=0, keepdims=True)


def forward_kernel(
    perm_ref, mask_ref, other_ref, perm_row_ref, mask_row_ref, gain_one_ref, gain_two_ref,
    x_far, wq_far, wk_far, wv_far, ws_far, wo_far, up_far, down_far,
    act_far, q_far, k_far, v_far, probs_far, att_far, second_far, act_two_far, share_far,
    sum_ref, log_ref, chosen_ref, entropy_ref, packed_ref,
    x_ref, w_ref, w_low_ref, wo_low_ref, act_ref, q_ref, k_ref, v_ref, probs_ref, att_ref, second_ref, act_two_ref, share_ref,
    feed_ref, in_sem, out_sem, share_sem, feed_sem, *, tile,
):
    rows, width = x_ref.shape
    tiles = rows // tile

    def x_copy(i):
        at = pl.ds(pl.multiple_of(i * tile, tile), tile)
        return pltpu.make_async_copy(x_far.at[at, :], x_ref.at[at, :], in_sem.at[i])

    def w_copy(n):
        far_ref = (wq_far, wk_far, wv_far, ws_far, wo_far)[n]
        return pltpu.make_async_copy(far_ref, w_ref.at[n], in_sem.at[tiles + n])

    outs = (
        (act_ref, act_far), (q_ref, q_far), (k_ref, k_far), (v_ref, v_far),
        (probs_ref, probs_far), (att_ref, att_far), (second_ref, second_far), (act_two_ref, act_two_far),
    )
    part = 8
    some = part * BLOCK
    parts = rows // some

    def out_copy(n, i):
        near_ref, far_ref = outs[n]
        size = near_ref.shape[0] // (tiles if n < 4 else parts)
        at = pl.ds(pl.multiple_of(i * size, size), size)
        return pltpu.make_async_copy(near_ref.at[at, :], far_ref.at[at, :], out_sem.at[n, i])

    x_copy(0).start()
    for n in range(3):
        w_copy(n).start()
    for i in range(1, tiles):
        x_copy(i).start()
    w_copy(3).start()
    w_copy(4).start()
    units = packed_ref.shape[2]
    at = pl.ds(pl.multiple_of(other_ref[0] * units, units), units)
    feed_copies = [
        pltpu.make_async_copy(up_far.at[:, at], feed_ref.at[0], feed_sem.at[0]),
        pltpu.make_async_copy(down_far.at[at, :], feed_ref.at[1], feed_sem.at[1]),
    ]
    for copy in feed_copies:
        copy.start()
    for n in range(3):
        w_copy(n).wait()
        w_low_ref[:, n * width : (n + 1) * width] = w_ref[n].astype(BF16)

    def prepare(i):
        at = pl.ds(pl.multiple_of(i * tile, tile), tile)
        unit, _ = normalize(x_ref[at, :])
        act = (unit * gain_one_ref[...]).astype(BF16)
        act_ref[at, :] = act
        sums = jnp.sum(act.astype(F32).reshape(tile // BLOCK, BLOCK, width), axis=1)
        some = tile // BLOCK
        sum_ref[pl.ds(pl.multiple_of(i * some, some), some), :] = sums.astype(BF16).astype(F32)

    def project(i):
        at = pl.ds(pl.multiple_of(i * tile, tile), tile)
        act = act_ref[at, :]
        for n, ref in enumerate((q_ref, k_ref, v_ref)):
            ref[at, :] = dot(act, w_low_ref[:, n * width : (n + 1) * width]).astype(BF16)

    def project_out(i):
        for n in range(4):
            out_copy(n, i).start()

    def both(i, _):
        x_copy(i + 1).wait()
        project(i)
        prepare(i + 1)
        project_out(i)
        return 0

    x_copy(0).wait()
    prepare(0)
    lax.fori_loop(0, tiles - 2, both, 0)
    x_copy(tiles - 1).wait()
    prepare(tiles - 1)
    w_copy(3).wait()
    w_copy(4).wait()
    wo_low_ref[...] = w_ref[4].astype(BF16)
    for n, copy in enumerate(feed_copies):
        copy.wait()
        packed_ref[n] = feed_ref[n].astype(BF16)
    logits = jnp.dot(sum_ref[...], w_ref[3], precision=HIGHEST, preferred_element_type=F32)
    balance_plans(
        logits, perm_row_ref[...], mask_row_ref[...], share_ref, log_ref, chosen_ref, entropy_ref
    )
    for i in (tiles - 2, tiles - 1):
        project(i)
    for i in (tiles - 2, tiles - 1):
        project_out(i)
    pltpu.make_async_copy(share_ref, share_far, share_sem).start()

    masks = head_masks(BLOCK)
    key_row = lax.broadcasted_iota(jnp.int32, (BLOCK, GROUP_ROWS), 0)
    query_row = lax.broadcasted_iota(jnp.int32, (BLOCK, GROUP_ROWS), 1) % BLOCK
    causal = key_row <= query_row

    def score(block, g):
        partner = perm_ref[block]
        own_at = pl.ds(pl.multiple_of(block * BLOCK, BLOCK), BLOCK)
        far_at = pl.ds(pl.multiple_of(partner * BLOCK, BLOCK), BLOCK)
        lanes = slice(g * GROUP_WIDTH, (g + 1) * GROUP_WIDTH)
        queries = expand(q_ref[own_at, lanes], masks)
        keys = jnp.concatenate([k_ref[own_at, lanes], k_ref[far_at, lanes]], axis=0)
        return dot_nt(keys, queries) * FACTOR

    def mix(block, g, scores):
        partner = perm_ref[block]
        usable = (partner < block) & (mask_ref[partner] > 0)
        own_at = pl.ds(pl.multiple_of(block * BLOCK, BLOCK), BLOCK)
        far_at = pl.ds(pl.multiple_of(partner * BLOCK, BLOCK), BLOCK)
        probs_at = pl.ds(pl.multiple_of(block * 2 * BLOCK, 2 * BLOCK), 2 * BLOCK)
        lanes = slice(g * GROUP_WIDTH, (g + 1) * GROUP_WIDTH)
        own = jnp.where(causal, scores[:BLOCK], -1e30)
        far = jnp.where(usable, scores[BLOCK:], -1e30)
        top = jnp.maximum(jnp.max(own, axis=0, keepdims=True), jnp.max(far, axis=0, keepdims=True))
        powers = jnp.exp(jnp.concatenate([own, far], axis=0) - top)
        probs = (powers * (1.0 / jnp.sum(powers, axis=0, keepdims=True))).astype(BF16)
        probs_ref[probs_at, g * GROUP_ROWS : (g + 1) * GROUP_ROWS] = probs
        scaled = (v_ref[far_at, lanes].astype(F32) * chosen_ref[pl.ds(block, 1), lanes]).astype(BF16)
        values = jnp.concatenate([v_ref[own_at, lanes], scaled], axis=0)
        att_ref[own_at, lanes] = fold(dot_tn(probs, values), masks).astype(BF16)

    def attend(j):
        units = [(j * part + b, g) for b in range(part) for g in range(width // GROUP_WIDTH)]
        ahead = []
        for n in range(len(units) + AHEAD):
            if n < len(units):
                ahead.append(score(*units[n]))
            if n >= AHEAD:
                mix(*units[n - AHEAD], ahead[n - AHEAD])

    def settle(j):
        at = pl.ds(pl.multiple_of(j * some, some), some)
        second = x_ref[at, :] + dot(att_ref[at, :], wo_low_ref[...])
        second_ref[at, :] = second
        unit, _ = normalize(second)
        act_two_ref[at, :] = (unit * gain_two_ref[...]).astype(BF16)

    def settle_out(j):
        for n in range(4, 8):
            out_copy(n, j).start()

    def step(j, _):
        settle(j - 1)
        attend(j)
        settle_out(j - 1)
        return 0

    attend(0)
    lax.fori_loop(1, parts, step, 0)
    settle(parts - 1)
    settle_out(parts - 1)
    for n in range(8):
        for i in range(tiles if n < 4 else parts):
            out_copy(n, i).wait()
    pltpu.make_async_copy(share_ref, share_far, share_sem).wait()


def forward(perm, mask, other, perm_row, mask_row, gain_one, gain_two, x, wq, wk, wv, ws, wo, w_up, w_down, tile=512):
    rows, width = x.shape
    blocks = rows // BLOCK
    tiles = rows // tile
    smem = pl.BlockSpec(memory_space=pltpu.SMEM)
    vmem = pl.BlockSpec(memory_space=pltpu.VMEM)
    hbm = pl.BlockSpec(memory_space=pltpu.HBM)
    low = ((rows, width), BF16)
    probs = ((2 * rows, HEADS * BLOCK), BF16)
    full = ((rows, width), F32)
    share = ((2 * ITERS, blocks, width), F32)
    plan = ((blocks, width), F32)
    packed = ((2, width, width), BF16)
    return pl.pallas_call(
        functools.partial(forward_kernel, tile=tile),
        in_specs=[smem] * 3 + [vmem] * 4 + [hbm] * 8,
        out_specs=[hbm] * 9 + [vmem] * 5,
        out_shape=[far_shape(*s) for s in (low, low, low, low, probs, low, full, low, share)]
        + [near_shape(*s) for s in (plan, plan, plan)]
        + [far_shape((1, width), F32), near_shape(*packed)],
        scratch_shapes=[pltpu.VMEM(*full), pltpu.VMEM((5, width, width), F32), pltpu.VMEM((width, 3 * width), BF16)]
        + [pltpu.VMEM((width, width), BF16)]
        + [pltpu.VMEM(*s) for s in (low, low, low, low, probs, low, full, low, share)]
        + [
            pltpu.VMEM((2, width, width), F32),
            pltpu.SemaphoreType.DMA((tiles + 5,)),
            pltpu.SemaphoreType.DMA((8, rows // (8 * BLOCK))),
            pltpu.SemaphoreType.DMA,
            pltpu.SemaphoreType.DMA((2,)),
        ],
        compiler_params=params(40),
        cost_estimate=cost(25),
        name="forward",
    )(
        perm, mask, other, perm_row, mask_row, gain_one, gain_two, far(x), far(wq), far(wk), far(wv), far(ws), far(wo),
        far(w_up), far(w_down),
    )


def attend_back_kernel(
    perm_ref, chosen_ref, gatt_ref, q_ref, probs_ref, k_ref, v_ref,
    gq_ref, gk_ref, gv_ref, gch_ref,
    own_k_ref, far_k_ref, own_v_ref, far_v_ref, *, group, part,
):
    rows, width = gq_ref.shape
    parts = rows // (part * BLOCK)
    masks = head_masks(BLOCK)
    lanes = slice(group * width, (group + 1) * width)

    def ahead(block):
        partner = perm_ref[block]
        own_at = pl.ds(pl.multiple_of(block * BLOCK, BLOCK), BLOCK)
        far_at = pl.ds(pl.multiple_of(partner * BLOCK, BLOCK), BLOCK)
        probs_at = pl.ds(pl.multiple_of(block * 2 * BLOCK, 2 * BLOCK), 2 * BLOCK)
        grads = expand(gatt_ref[own_at, lanes], masks)
        far_values = v_ref[far_at, lanes].astype(F32)
        chosen = chosen_ref[pl.ds(block, 1), lanes]
        values = jnp.concatenate([v_ref[own_at, lanes], (far_values * chosen).astype(BF16)], axis=0)
        probs_low = probs_ref[probs_at, group * GROUP_ROWS : (group + 1) * GROUP_ROWS]
        grad_probs = dot_nt(values, grads)
        grad_values = dot(probs_low, grads)
        far_grad = grad_values[BLOCK:]
        gch_ref[pl.ds(block, 1), :] = jnp.sum(far_grad * far_values, axis=0, keepdims=True)
        own_v_ref[own_at, :] = grad_values[:BLOCK]
        far_v_ref[far_at, :] = far_grad * chosen
        return grad_probs

    def behind(block, grad_probs):
        partner = perm_ref[block]
        own_at = pl.ds(pl.multiple_of(block * BLOCK, BLOCK), BLOCK)
        far_at = pl.ds(pl.multiple_of(partner * BLOCK, BLOCK), BLOCK)
        probs_at = pl.ds(pl.multiple_of(block * 2 * BLOCK, 2 * BLOCK), 2 * BLOCK)
        queries = expand(q_ref[own_at, lanes], masks)
        keys = jnp.concatenate([k_ref[own_at, lanes], k_ref[far_at, lanes]], axis=0)
        probs = probs_ref[probs_at, group * GROUP_ROWS : (group + 1) * GROUP_ROWS].astype(F32)
        total = jnp.sum(probs * grad_probs, axis=0, keepdims=True)
        grad_scores = (probs * (grad_probs - total)).astype(BF16)
        grad_keys = dot(grad_scores, queries) * FACTOR
        gq_ref[own_at, :] = (fold(dot_tn(grad_scores, keys), masks) * FACTOR).astype(BF16)
        own_k_ref[own_at, :] = grad_keys[:BLOCK]
        far_k_ref[far_at, :] = grad_keys[BLOCK:]

    def body(j, _):
        products = []
        for n in range(part + AHEAD):
            if n < part:
                products.append(ahead(j * part + n))
            if n >= AHEAD:
                behind(j * part + n - AHEAD, products[n - AHEAD])
        return 0

    lax.fori_loop(0, parts, body, 0)
    gk_ref[...] = (own_k_ref[...] + far_k_ref[...]).astype(BF16)
    gv_ref[...] = (own_v_ref[...] + far_v_ref[...]).astype(BF16)


def attend_back(perm, q, gatt, probs, k, v, chosen, group, part=8):
    rows = q.shape[0]
    smem = pl.BlockSpec(memory_space=pltpu.SMEM)
    vmem = pl.BlockSpec(memory_space=pltpu.VMEM)
    low = ((rows, GROUP_WIDTH), BF16)
    full = ((rows, GROUP_WIDTH), F32)
    return pl.pallas_call(
        functools.partial(attend_back_kernel, group=group, part=part),
        in_specs=[smem] + [vmem] * 6,
        out_specs=[vmem] * 4,
        out_shape=[near_shape(*s) for s in (low, low, low, ((rows // BLOCK, GROUP_WIDTH), F32))],
        scratch_shapes=[pltpu.VMEM(*full)] * 4,
        compiler_params=params(12),
        cost_estimate=cost(10),
        name="attend_back",
    )(perm, near(chosen), near(gatt), near(q), near(probs), near(k), near(v))


def gelu_pair(up):
    square = up * up
    inner = 0.7978845608028654 * 0.044715
    half = 0.5 + 0.5 * jnp.tanh(up * (0.7978845608028654 + inner * square))
    value = up * half
    slope = half + (2.0 * value) * (1.0 - half) * (0.7978845608028654 + 3.0 * inner * square)
    return value, slope


def spread(out_ref, acc_ref, where, lanes):
    chunks, size = out_ref.shape[0], out_ref.shape[-2]
    for r in range(chunks):
        at = pl.multiple_of((r ^ where) * size, size)
        out_ref[r, :, lanes] = acc_ref[pl.ds(at, size), :].astype(out_ref.dtype)


class Copies:
    def __init__(self, source, target, sems, tile):
        self.source, self.target, self.sems, self.tile = source, target, sems, tile

    def copy(self, i):
        at = pl.ds(pl.multiple_of(i * self.tile, self.tile), self.tile)
        return pltpu.make_async_copy(self.source.at[at, :], self.target.at[at, :], self.sems.at[i])

    def start(self, i):
        self.copy(i).start()

    def wait(self, i):
        self.copy(i).wait()


def quarter_math(act, cot_low, weights_ref, up_acc, down_acc):
    value, slope = gelu_pair(dot(act, weights_ref[0]))
    hidden = value.astype(BF16)
    grad_up = (dot_nt(cot_low, weights_ref[1]) * slope).astype(BF16)
    up_acc[...] += dot_tn(act, grad_up)
    down_acc[...] += dot_tn(cot_low, hidden)
    return hidden, dot_nt(grad_up, weights_ref[0])


def quarter_kernel(*refs, kind, tile, tally):
    if tally:
        mask_ref, refs = refs[0], refs[1:]
    where_ref, act_ref, weights_ref = refs[:3]
    if kind == "first":
        cot_far, hidden_far, grad_ref, piece_ref, low_ref, act_ref = refs[3:9]
        hidden_ref, up_acc, down_acc, hidden_sems, cot_ref, cot_sems, act_sems = refs[9:]
    elif kind == "middle":
        low_ref, sofar_ref, hidden_far, grad_ref, piece_ref = refs[3:8]
        hidden_ref, up_acc, down_acc, hidden_sems = refs[8:]
    else:
        low_ref, sofar_ref, gain_ref, entropy_ref, cot_far, second_far, att_far, wo_far = refs[3:11]
        hidden_far, gsec_far, piece_ref, gatt_ref, gout_ref = refs[11:16]
        hidden_ref, up_acc, down_acc, hidden_sems, cot_ref, cot_sems = refs[16:22]
        second_ref, second_sems, att_ref, att_sems, gsec_ref, gsec_sems = refs[22:28]
        wo_ref, wo_low_ref, wo_sem, out_acc, gain_acc, column_ref, sum_ref, second_low_ref = refs[28:]
    rows, width = act_ref.shape
    tiles = rows // tile
    hidden_out = Copies(hidden_ref, hidden_far, hidden_sems, tile)
    ins = []
    if kind == "first":
        ins = [Copies(cot_far, cot_ref, cot_sems, tile), Copies(refs[1], act_ref, act_sems, tile)]
    if kind == "last":
        ins = [
            Copies(second_far, second_ref, second_sems, tile),
            Copies(cot_far, cot_ref, cot_sems, tile),
            Copies(att_far, att_ref, att_sems, tile),
        ]
        gsec_out = Copies(gsec_ref, gsec_far, gsec_sems, tile)
    for i in range(tiles):
        for copies in ins:
            copies.start(i)
        if kind == "last" and i == 0:
            wo_copy = pltpu.make_async_copy(wo_far, wo_ref, wo_sem)
            wo_copy.start()
    up_acc[...] = jnp.zeros_like(up_acc)
    down_acc[...] = jnp.zeros_like(down_acc)
    if kind == "last":
        out_acc[...] = jnp.zeros_like(out_acc)
        gain_acc[...] = jnp.zeros_like(gain_acc)

    def multiply(i):
        at = pl.ds(pl.multiple_of(i * tile, tile), tile)
        if kind == "first":
            low_ref[at, :] = cot_ref[at, :].astype(BF16)
        hidden, grad = quarter_math(act_ref[at, :], low_ref[at, :], weights_ref, up_acc, down_acc)
        hidden_ref[at, :] = hidden
        if kind == "first":
            grad_ref[at, :] = grad
        elif kind == "middle":
            grad_ref[at, :] = sofar_ref[at, :] + grad
        else:
            sum_ref[i % 2] = sofar_ref[at, :] + grad

    def settle(i):
        at = pl.ds(pl.multiple_of(i * tile, tile), tile)
        grad = sum_ref[i % 2]
        unit, inverse = normalize(second_ref[at, :])
        gain_acc[...] += jnp.sum(grad * unit, axis=0, keepdims=True)
        grad_second = cot_ref[at, :] + norm_grad(grad, unit, inverse, gain_ref[...])
        gsec_ref[at, :] = grad_second
        second_low_ref[...] = grad_second.astype(BF16)

    def settle_back(i):
        at = pl.ds(pl.multiple_of(i * tile, tile), tile)
        second_low = second_low_ref[...]
        gatt_ref[at, :] = dot_nt(second_low, wo_low_ref[...]).astype(BF16)
        out_acc[...] += dot_tn(att_ref[at, :], second_low)

    def body(i, _):
        for copies in ins:
            copies.wait(i - 1 if kind == "last" else i)
        if kind == "last":
            settle(i - 1)
        multiply(i)
        if kind == "last":
            settle_back(i - 1)
            gsec_out.start(i - 1)
        hidden_out.start(i)
        return 0

    if kind == "last":
        multiply(0)
        hidden_out.start(0)
        wo_copy.wait()
        wo_low_ref[...] = wo_ref[...].astype(BF16)
        lax.fori_loop(1, tiles, body, 0)
        for copies in ins:
            copies.wait(tiles - 1)
        settle(tiles - 1)
        gsec_out.start(tiles - 1)
        settle_back(tiles - 1)
    else:
        lax.fori_loop(0, tiles, body, 0)
    size = width // piece_ref.shape[0]
    spread(piece_ref.at[:, :size], up_acc, where_ref[0], slice(None))
    spread(piece_ref.at[:, size : 2 * size], down_acc, where_ref[0], slice(None))
    if tally:
        shape = (TALLY_ROWS, weights_ref.shape[2])
        mine = lax.broadcasted_iota(jnp.int32, shape, 1) == where_ref[3]
        count = jnp.sum(mask_ref[...].astype(F32), axis=1, keepdims=True)
        row = jnp.where(mine, jnp.broadcast_to(count, shape), 0.0).astype(BF16)
        for r in range(piece_ref.shape[0]):
            piece_ref[r, 2 * size :, :] = row
    if kind == "last":
        spread(gout_ref, out_acc, where_ref[2], slice(0, width))
        half = (LANES // 2, width)
        column_ref[...] = jnp.concatenate(
            [jnp.broadcast_to(gain_acc[...], half), jnp.broadcast_to(entropy_ref[...], half)], axis=0
        ).T
        spread(gout_ref, column_ref, where_ref[2], slice(width, width + LANES))
    for i in range(tiles):
        hidden_out.wait(i)
        if kind == "last":
            gsec_out.wait(i)


def feed_quarter(
    kind, where, act, weights, cot, sofar=None, extra=None, mask_row=None, row_chunks=1, out_chunks=1, tile=512
):
    rows, width = act.shape
    units = weights.shape[2]
    tiles = rows // tile
    smem = pl.BlockSpec(memory_space=pltpu.SMEM)
    vmem = pl.BlockSpec(memory_space=pltpu.VMEM)
    hbm = pl.BlockSpec(memory_space=pltpu.HBM)
    tally = mask_row is not None
    size = 2 * (width // row_chunks) + (TALLY_ROWS if tally else 0)
    piece = near_shape((row_chunks, size, units), BF16)
    low = near_shape((rows, width), BF16)
    full = near_shape((rows, width), F32)
    hidden = far_shape((rows, units), BF16)
    sems = pltpu.SemaphoreType.DMA((tiles,))
    low_buffer, full_buffer = pltpu.VMEM((rows, width), BF16), pltpu.VMEM((rows, width), F32)
    square = pltpu.VMEM((width, width), F32)
    scratch = [pltpu.VMEM((rows, units), BF16), square, square, sems]
    if kind == "first":
        operands = (far(cot),)
        in_specs = [hbm]
        out_shape, out_specs = [hidden, full, piece, low, low], [hbm] + [vmem] * 4
        scratch = scratch + [full_buffer, sems, sems]
        limit = 24
    elif kind == "middle":
        operands = (near(cot), near(sofar))
        in_specs = [vmem] * 2
        out_shape, out_specs = [hidden, full, piece], [hbm] + [vmem] * 2
        limit = 18
    else:
        full_cot, second, att, w_out, gain, entropy = extra
        operands = (near(cot), near(sofar), gain, entropy, far(full_cot), far(second), far(att), far(w_out))
        in_specs = [vmem] * 4 + [hbm] * 4
        out_piece = near_shape((out_chunks, width // out_chunks, width + LANES), BF16)
        out_shape = [hidden, far_shape((rows, width), F32), piece, low, out_piece]
        out_specs = [hbm] * 2 + [vmem] * 3
        scratch = scratch + [full_buffer, sems, full_buffer, sems, low_buffer, sems, full_buffer, sems]
        scratch = scratch + [square, pltpu.VMEM((width, width), BF16), pltpu.SemaphoreType.DMA]
        scratch = scratch + [square, pltpu.VMEM((1, width), F32), pltpu.VMEM((width, LANES), F32)]
        scratch = scratch + [pltpu.VMEM((2, tile, width), F32), pltpu.VMEM((tile, width), BF16)]
        limit = 32
    return pl.pallas_call(
        functools.partial(quarter_kernel, kind=kind, tile=tile, tally=tally),
        in_specs=([vmem] if tally else []) + [smem, hbm if kind == "first" else vmem, vmem] + in_specs,
        out_specs=out_specs,
        out_shape=out_shape,
        scratch_shapes=scratch,
        compiler_params=params(limit),
        cost_estimate=cost(9),
        name="feed_" + kind,
    )(
        *([mask_row] if tally else []), where, far(act) if kind == "first" else near(act), near(weights), *operands
    )


def output_kernel(second_ref, *refs):
    out_ref = refs[-1]
    count = (len(refs) - 1) // 2
    total = second_ref[...]
    for hidden_ref, weights_ref in zip(refs[:count], refs[count : 2 * count]):
        total = total + dot(hidden_ref[...], weights_ref[0])
    out_ref[...] = total


def layer_output(second, hidden, weights, tile=512):
    rows, width = second.shape
    units = hidden[0].shape[1]
    down = pl.BlockSpec((1, units, width), lambda *_: (1, 0, 0), pipeline_mode=pl.Buffered(1))
    return pl.pallas_call(
        output_kernel,
        grid=(rows // tile,),
        in_specs=[rows_of(tile, width)] + [rows_of(tile, units)] * len(hidden) + [down] * len(hidden),
        out_specs=rows_of(tile, width),
        out_shape=far_shape((rows, width), F32),
        compiler_params=params(16),
        cost_estimate=cost(8),
        name="layer_output",
    )(near(second), *[far(array) for array in hidden], *[near(array) for array in weights])


def plans_back(grad, share_ref, span, first):
    for level in range(2 * ITERS - 1, -1, -1):
        if level % 2:
            total = jnp.sum(grad, axis=0, keepdims=True)
        else:
            total = segment_sum(grad, first)
        grad = grad - share_ref[level, :, span] * total
    return grad


def first_heads_kernel(
    where_ref, act_ref, gq_ref, gk_ref, gv_ref, out_ref, gch_ref, share_ref, log_ref, perm_ref, mask_ref,
    piece_ref, chosen_part_ref, penalty_part_ref, acc_ref,
):
    blocks = log_ref.shape[0]
    wide = 2 * blocks
    first, position = lane_tiles(blocks)
    hot = position == down_rows(perm_ref[...], wide)
    real = down_rows(mask_ref[...], wide)
    for pair in range(gch_ref.shape[1] // wide):
        span = slice(pair * wide, (pair + 1) * wide)
        plan = share_ref[2 * ITERS - 1, :, span]
        gch = segment_sum(gch_ref[:, span], first)
        chosen_part_ref[:, span] = plans_back(plan * jnp.where(hot, blocks * gch, 0.0), share_ref, span, first)
        penalty_part_ref[:, span] = plans_back(plan * real * (log_ref[:, span] + 1.0), share_ref, span, first)
    act = act_ref[...]
    cols = acc_ref.shape[1]
    for index, ref in enumerate((gq_ref, gk_ref, gv_ref)):
        acc_ref[...] = dot_tn(act, ref[...])
        spread(piece_ref, acc_ref, where_ref[2], slice(index * cols, (index + 1) * cols))
    piece_ref[:, :, 3 * cols :] = out_ref[...]


def first_heads(where, act, group, out_piece, shares, plan_log, perm_row, mask_row, chunks):
    width = act.shape[1]
    blocks = plan_log.shape[0]
    cols = group[0].shape[1]
    vmem = pl.BlockSpec(memory_space=pltpu.VMEM)
    return pl.pallas_call(
        first_heads_kernel,
        in_specs=[pl.BlockSpec(memory_space=pltpu.SMEM)] + [vmem] * 10,
        out_specs=[vmem] * 3,
        out_shape=[near_shape((chunks, width // chunks, 3 * cols + out_piece.shape[2]), BF16)]
        + [near_shape((blocks, cols), F32)] * 2,
        scratch_shapes=[pltpu.VMEM((width, cols), F32)],
        compiler_params=params(12),
        cost_estimate=cost(3),
        name="first_heads",
    )(
        where, near(act), *[near(array) for array in group[:3]], near(out_piece), near(group[3]), near(shares),
        near(plan_log), perm_row, mask_row,
    )


def last_heads_kernel(
    where_ref, pen_ref, act_ref, gq_ref, gk_ref, gv_ref, gch_ref,
    first_ref, chosen_part_ref, penalty_part_ref, share_ref, log_ref, sum_ref, w_ref, perm_ref, mask_ref, tally_ref,
    piece_ref, gsum_ref, total_ref, glog_ref, acc_ref,
):
    blocks, width = sum_ref.shape
    cols = acc_ref.shape[1]
    wide = 2 * blocks
    block_total = jnp.sum(tally_ref[...].astype(F32), axis=1, keepdims=True)
    block_total = jnp.sum(block_total, axis=0, keepdims=True)
    total_ref[...] = jnp.broadcast_to(block_total, total_ref.shape)
    coef = pen_ref[0] / (HEADS * block_total)
    first, position = lane_tiles(blocks)
    hot = position == down_rows(perm_ref[...], wide)
    weight = coef * down_rows(mask_ref[...], wide)
    act = act_ref[...]
    start = first_ref.shape[2]
    piece_ref[:, :, :start] = first_ref[...]
    for index, ref in enumerate((gq_ref, gk_ref, gv_ref)):
        acc_ref[...] = dot_tn(act, ref[...])
        spread(piece_ref, acc_ref, where_ref[2], slice(start + index * cols, start + (index + 1) * cols))
    glog_ref[:, :cols] = chosen_part_ref[...] - coef * penalty_part_ref[...]
    for pair in range(cols // wide):
        span = slice(cols + pair * wide, cols + (pair + 1) * wide)
        plan = share_ref[2 * ITERS - 1, :, span]
        gch = segment_sum(gch_ref[:, pair * wide : (pair + 1) * wide], first)
        grad = plan * (jnp.where(hot, blocks * gch, 0.0) - weight * (log_ref[:, span] + 1.0))
        glog_ref[:, span] = plans_back(grad, share_ref, span, first)
    for g in range(2):
        at = slice(g * cols, (g + 1) * cols)
        acc_ref[...] = lax.dot_general(
            sum_ref[...], glog_ref[:, at], TN, precision=HIGHEST, preferred_element_type=F32
        )
        spread(piece_ref, acc_ref, where_ref[2], slice(start + (3 + g) * cols, start + (4 + g) * cols))
    gsum_ref[...] = lax.dot_general(glog_ref[...], w_ref[...], NT, precision=HIGHEST, preferred_element_type=F32)


def last_heads(
    where, pen_weight, act, group, first, shares, plan_log, sums, w_sort, perm_row, mask_row, tallies, chunks
):
    width = act.shape[1]
    blocks = sums.shape[0]
    cols = group[0].shape[1]
    smem = pl.BlockSpec(memory_space=pltpu.SMEM)
    vmem = pl.BlockSpec(memory_space=pltpu.VMEM)
    gq, gk, gv, gch = group
    return pl.pallas_call(
        last_heads_kernel,
        in_specs=[smem] * 2 + [vmem] * 15,
        out_specs=[vmem] * 3,
        out_shape=[
            near_shape((chunks, width // chunks, first[0].shape[2] + 5 * cols), BF16),
            near_shape((blocks, width), F32),
            near_shape((1, LANES), F32),
        ],
        scratch_shapes=[pltpu.VMEM((blocks, width), F32), pltpu.VMEM((width, cols), F32)],
        compiler_params=params(14),
        cost_estimate=cost(5),
        name="last_heads",
    )(
        where, pen_weight, near(act), near(gq), near(gk), near(gv), near(gch),
        *[near(array) for array in first], near(shares),
        near(plan_log), near(sums), near(w_sort), perm_row, mask_row, tallies,
    )


def input_kernel(*refs):
    count = (len(refs) - 9) // 3
    groups = [refs[3 * g : 3 * g + 3] for g in range(count)]
    gsum_ref, x_ref, gsec_ref, gain_ref, wq_ref, wk_ref, wv_ref, out_ref, w_ref = refs[3 * count :]

    @pl.when(pl.program_id(0) == 0)
    def _():
        for which, ref in enumerate((wq_ref, wk_ref, wv_ref)):
            w_ref[which] = ref[...].astype(BF16)

    rows, width = x_ref.shape
    grad = jnp.zeros((rows, width), F32)
    for g, group in enumerate(groups):
        for which, ref in enumerate(group):
            cols = ref.shape[1]
            grad = grad + dot_nt(ref[...], w_ref[which, :, g * cols : (g + 1) * cols])
    grad = (grad.reshape(rows // BLOCK, BLOCK, width) + gsum_ref[...][:, None, :]).reshape(rows, width)
    unit, inverse = normalize(x_ref[...])
    out_ref[...] = gsec_ref[...] + norm_grad(grad, unit, inverse, gain_ref[...])


def input_grad(groups, gsum, x, gsec, gain, wq, wk, wv, tile=512):
    rows, width = x.shape
    weight = pl.BlockSpec((width, width), lambda *_: (0, 0), pipeline_mode=pl.Buffered(1))
    flat = [array for group in groups for array in group]
    return pl.pallas_call(
        input_kernel,
        grid=(rows // tile,),
        in_specs=[rows_of(tile, array.shape[1]) for array in flat]
        + [rows_of(tile // BLOCK, width)]
        + [rows_of(tile, width)] * 2
        + [whole((1, width))]
        + [weight] * 3,
        out_specs=rows_of(tile, width),
        out_shape=far_shape((rows, width), F32),
        scratch_shapes=[pltpu.VMEM((3, width, width), BF16)],
        compiler_params=params(20),
        cost_estimate=cost(10),
        name="input_grad",
    )(*[near(array) for array in flat], gsum, far(x), far(gsec), gain, far(wq), far(wk), far(wv))


def pack_kernel(core_ref, up_ref, down_ref, mine_ref):
    mine_ref[0] = up_ref[...].astype(BF16)
    mine_ref[1] = down_ref[...].astype(BF16)


def pack_weights(core, w_up, w_down):
    width, units = w_up.shape
    half = units // 2
    shape = (2, width, half)
    return pl.pallas_call(
        pack_kernel,
        grid_spec=pltpu.PrefetchScalarGridSpec(
            num_scalar_prefetch=1,
            grid=(1,),
            in_specs=[
                pl.BlockSpec((width, half), lambda step, core: (0, core[0])),
                pl.BlockSpec((half, width), lambda step, core: (core[0], 0)),
            ],
            out_specs=whole(shape),
        ),
        out_shape=near_shape(shape, BF16),
        compiler_params=params(12),
        cost_estimate=cost(2),
        name="pack_weights",
    )(core, far(w_up), far(w_down))


def finish_feed_kernel(*refs):
    where_ref, parts = refs[0], refs[1:-3]
    up_ref, down_ref, turn_ref = refs[-3:]
    some, size, units = parts[0].shape
    size = size // 2
    half = len(parts) // 2
    for flip in range(2):
        column = pl.multiple_of((where_ref[1] ^ flip) * units, units)
        for n, ref in enumerate(parts[flip * half : (flip + 1) * half]):
            for r in range(some):
                at = pl.multiple_of(((n * some + r) ^ where_ref[0]) * size, size)
                up_ref[pl.ds(at, size), pl.ds(column, units)] = ref[r, :size].astype(F32)
                turn_ref[pl.ds(at, size), :] = ref[r, size:].astype(F32)
        down_ref[pl.ds(column, units), :] = turn_ref[...].T


def finish_feed(where, parts):
    some, size, units = parts[0].shape
    width = len(parts) // 2 * some * size // 2
    vmem = pl.BlockSpec(memory_space=pltpu.VMEM)
    return pl.pallas_call(
        finish_feed_kernel,
        in_specs=[pl.BlockSpec(memory_space=pltpu.SMEM)] + [vmem] * len(parts),
        out_specs=[vmem, vmem],
        out_shape=[far_shape((width, 2 * units), F32), far_shape((2 * units, width), F32)],
        scratch_shapes=[pltpu.VMEM((width, units), F32)],
        compiler_params=params(16),
        cost_estimate=cost(3),
        name="finish_feed",
    )(where, *parts)


def finish_kernel(*refs):
    where_ref, parts = refs[0], refs[1:-22]
    weights = refs[-22:-18]
    gain_ref, total_ref = refs[-18:-16]
    fars = refs[-16:-11]
    gain_one_ref, gain_two_ref, penalty_ref = refs[-11:-8]
    nears = refs[-8:-3]
    one_ref, two_ref, sems = refs[-3:]
    width = gain_ref.shape[1]
    some, size = parts[0].shape[:2]
    total = jnp.zeros((width, LANES), F32)
    copies = []
    cols = width // 2
    second_at = 3 * cols + width + LANES
    spans = [[(n * cols, 0, cols), (second_at + n * cols, cols, cols)] for n in range(3)]
    spans = spans + [[(second_at + 3 * cols, 0, width)], [(3 * cols, 0, width)]]
    for index, near_ref in enumerate(nears):
        for n, part_ref in enumerate(parts):
            for r in range(some):
                rows = pl.ds(pl.multiple_of(((n * some + r) ^ where_ref[2]) * size, size), size)
                for source, target, count in spans[index]:
                    near_ref[rows, target : target + count] = part_ref[r, :, source : source + count].astype(F32)
                if index == 0:
                    at = 3 * cols + width
                    two_ref[rows, :] = part_ref[r, :, at : at + LANES].astype(F32)
        copies.append(pltpu.make_async_copy(near_ref, fars[index], sems.at[index]))
        copies[-1].start()
    for at in range(0, width, LANES):
        span = slice(at, at + LANES)
        for grad, weight in zip(nears[:3], weights[:3]):
            total = total + grad[:, span] * weight[:, span].astype(BF16).astype(F32)
        total = total + nears[3][:, span] * weights[3][:, span]
    one_ref[...] = total
    gain_one_ref[...] = jnp.sum(one_ref[...].T, axis=0, keepdims=True) / gain_ref[...]
    turned = two_ref[...].T
    gain_two_ref[...] = turned[:1, :]
    entropy = jnp.sum(turned[LANES // 2 : LANES // 2 + 1, :], axis=1, keepdims=True)
    penalty_ref[...] = entropy / (HEADS * total_ref[:, :1])
    for copy in copies:
        copy.wait()


def finish(where, parts, wq, wk, wv, ws, gain, total):
    width = wq.shape[0]
    vmem = pl.BlockSpec(memory_space=pltpu.VMEM)
    hbm = pl.BlockSpec(memory_space=pltpu.HBM)
    square = far_shape((width, width), F32)
    row = shape_of((1, width), F32)
    return pl.pallas_call(
        finish_kernel,
        in_specs=[pl.BlockSpec(memory_space=pltpu.SMEM)] + [vmem] * (6 + len(parts)),
        out_specs=[hbm] * 5 + [vmem] * 3,
        out_shape=[square] * 5 + [row] * 2 + [shape_of((1, 1), F32)],
        scratch_shapes=[pltpu.VMEM((width, width), F32)] * 5
        + [pltpu.VMEM((width, LANES), F32)] * 2
        + [pltpu.SemaphoreType.DMA((5,))],
        compiler_params=params(16),
        cost_estimate=cost(5),
        name="finish",
    )(where, *parts, near(wq), near(wk), near(wv), near(ws), gain, total)


MP, CORE, X, Z_LOW, Z_HIGH = 1, 2, 4, 8, 16
CORE_STEP = ((CORE,), (CORE,))
FEED_STEPS = ((X,), (Z_LOW, Z_HIGH, Z_LOW + Z_HIGH))
HEAD_STEPS = ((CORE,), (MP, X, MP + X), (Z_LOW, Z_HIGH, Z_LOW + Z_HIGH))


def swap(array, flip):
    count = lax.axis_size("batch") * lax.axis_size("mp")
    return lax.ppermute(array, ("batch", "mp"), [(i, i ^ flip) for i in range(count)])


def place(steps, index):
    result = jnp.int32(0)
    for step in steps:
        for bit in reversed(step[: (len(step) + 1).bit_length() - 1]):
            result = 2 * result + ((index & bit) > 0).astype(jnp.int32)
    return result


def add_low(first, *others):
    total = first.astype(F32)
    for array in others:
        total = total + array.astype(F32)
    return total.astype(BF16)


class Walk:
    def __init__(self, pieces, steps):
        self.pieces = pieces
        self.down = list(steps)
        self.up = list(reversed(steps))
        self.parts, self.arrived = None, []

    def added(self, plan, count):
        pieces = self.pieces + [plan.after(array) for array in self.arrived]
        self.arrived = []
        size = pieces[0].shape[0] // count
        if len(pieces) == 1 and count == 1:
            return pieces
        return [
            add_low(*[piece[n * size : (n + 1) * size] for piece in pieces]) if len(pieces) > 1
            else pieces[0][n * size : (n + 1) * size]
            for n in range(count)
        ]

    def reduce(self, plan):
        flips = self.down.pop(0)
        parts = self.added(plan, len(flips) + 1)
        self.arrived = [swap(plan.after(part), flip) for part, flip in zip(parts[1:], flips)]
        self.pieces = parts[:1]
        return self.arrived

    def reduced(self, plan):
        return self.added(plan, 1)[0]

    def gather(self, plan, value):
        flips = self.up.pop(0)
        self.parts = [value]
        mine = plan.after(value)
        self.arrived = [swap(mine, flip) for flip in flips]
        return self.arrived

    def gathered(self, plan):
        parts = self.parts + [plan.after(array) for array in self.arrived]
        self.arrived = []
        return parts


class Schedule:
    def __init__(self):
        self.pending, self.launched, self.done = [], [], None

    def after(self, array):
        return lax.optimization_barrier((array, self.done))[0]

    def enter(self, small):
        tied = lax.optimization_barrier((small, *self.pending))[0]
        self.pending, self.launched = self.launched, []
        return tied

    def leave(self, *arrays):
        self.pending.extend(arrays)
        self.done = arrays[0]

    def launch(self, *arrays):
        for array in arrays:
            self.launched.extend(array if isinstance(array, list) else [array])


def local_small(
    inputs, cotangent, block_perm, block_mask, pen_weight, w_query, w_key, w_value, w_out, w_sort,
    gain_one, gain_two, w_up, w_down,
):
    _, rows, width = inputs.shape
    x = inputs.reshape(rows, width)
    cot = cotangent.reshape(rows, width)
    perm = block_perm.reshape(-1)
    mask = block_mask.reshape(-1)
    perm_row = block_perm.reshape(1, -1)
    mask_row = block_mask.reshape(1, -1)
    gain_one_row = gain_one.reshape(1, width)
    gain_two_row = gain_two.reshape(1, width)
    batch, mp = lax.axis_index("batch"), lax.axis_index("mp")
    core = batch & 1
    index = batch * 2 + mp
    where = jnp.stack([place(FEED_STEPS, index), core, place(HEAD_STEPS, index), index])
    row_chunks, out_chunks = 8, 32
    plan = Schedule()

    count = jnp.broadcast_to(jnp.sum(mask.astype(F32)), (8, LANES))
    own_a = pack_weights(core.reshape(1), w_up, w_down)
    far_a = swap(own_a, MP)
    plan.leave(own_a)
    act_one, q, k, v, probs, att, second, act_two_far, shares, sums, plan_log, chosen, entropy, own_b = forward(
        perm, mask, (1 - core).reshape(1), perm_row, mask_row, plan.enter(gain_one_row), gain_two_row, x,
        w_query, w_key, w_value, w_sort, w_out, w_up, w_down,
    )
    plan.leave(entropy)
    plan.pending.append(far_a)

    far_b = swap(plan.after(far_a), CORE)
    plan.launch(far_b)
    hid_a, sofar, other_piece, cot_low, act_two = feed_quarter(
        "first", plan.enter(where), act_two_far, far_a, cot, mask_row=mask_row, row_chunks=row_chunks
    )
    plan.leave(other_piece)

    hid_b, sofar, piece = feed_quarter(
        "middle", plan.enter(where), act_two, far_b, cot_low, sofar, mask_row=mask_row, row_chunks=row_chunks
    )
    plan.leave(piece)

    arrived = swap(plan.after(piece), CORE)
    plan.launch(arrived)
    hid_c, sofar, piece = feed_quarter(
        "middle", plan.enter(where), act_two, own_b, cot_low, sofar, row_chunks=row_chunks
    )
    plan.leave(piece)

    other = Walk([other_piece, plan.after(arrived)], FEED_STEPS)
    arrived = swap(plan.after(piece), CORE)
    plan.launch(arrived, other.reduce(plan))
    extra = (cot, second, att, w_out, gain_two_row, entropy)
    hid_d, grad_second, piece, grad_att, out_piece = feed_quarter(
        "last", plan.enter(where), act_two, own_a, cot_low, sofar, extra, None, row_chunks, out_chunks
    )
    plan.leave(grad_att)

    own = Walk([piece, plan.after(arrived)], FEED_STEPS)
    plan.launch(own.reduce(plan), other.reduce(plan))
    groups = [attend_back(plan.enter(perm), q, grad_att, probs, k, v, chosen, 0)]
    held, plan.pending = plan.pending, []
    plan.leave(groups[0][3])
    firsts = first_heads(
        plan.enter(where), act_one, groups[0], out_piece, shares, plan_log, perm_row, mask_row, out_chunks
    )
    plan.leave(firsts[0])
    plan.pending.extend(held)

    other_sum = other.reduced(plan)
    crossed = swap(plan.after(other_sum), MP)
    plan.launch(crossed, own.reduce(plan))
    plan.pending.extend(own.pieces)
    groups.append(attend_back(plan.enter(perm), q, grad_att, probs, k, v, chosen, 1))
    plan.leave(groups[1][3])

    crossed = plan.after(crossed)
    rows_fed = own.pieces[0].shape[1]
    tallies = jnp.concatenate([other_sum[0, rows_fed:], crossed[0, rows_fed:]], axis=0)
    tallies = tallies.reshape(2, TALLY_ROWS, -1)[:, 0]
    own.pieces.append(crossed[:, :rows_fed])
    value = own.reduced(plan)
    plan.pending.append(value)
    piece, gsum, block_total = last_heads(
        plan.enter(where), pen_weight, act_one, groups[1], firsts, shares, plan_log, sums, w_sort,
        perm_row, mask_row, tallies, out_chunks,
    )
    plan.leave(gsum)

    head = Walk([piece], HEAD_STEPS)
    plan.pending.extend(head.reduce(plan))
    own.gather(plan, value)
    plan.launch(head.reduce(plan))
    plan.pending.extend(head.pieces)
    grad_input = input_grad(
        [group[:3] for group in groups], gsum, x, grad_second, plan.enter(gain_one_row), w_query, w_key, w_value
    )
    plan.leave(grad_input)

    head.reduce(plan)
    own.gather(plan, jnp.concatenate(own.gathered(plan), axis=0))
    head.gather(plan, head.reduced(plan))
    value = jnp.concatenate(head.gathered(plan), axis=0)
    plan.pending.append(value)
    head.gather(plan, value)
    quarters = (far_a, far_b, own_b, own_a)
    output = layer_output(plan.enter(second), (hid_a, hid_b, hid_c, hid_d), quarters)
    plan.leave(output)

    parts = own.parts + own.arrived
    grad_up, grad_down = finish_feed(plan.enter(where), parts + [swap(part, CORE) for part in parts])
    plan.leave(grad_up)
    parts = head.gathered(plan)
    parts = parts + [swap(part, CORE) for part in parts]
    grad_query, grad_key, grad_value, grad_sort, grad_out, grad_gain_one, grad_gain_two, penalty = finish(
        where, parts, w_query, w_key, w_value, w_sort, gain_one_row, block_total
    )
    return (
        output.reshape(inputs.shape),
        penalty.reshape(1),
        grad_input.reshape(inputs.shape),
        grad_query,
        grad_key,
        grad_value,
        grad_out,
        grad_sort,
        grad_gain_one.reshape(width),
        grad_gain_two.reshape(width),
        grad_up,
        grad_down,
    )


def local_any(
    inputs, cotangent, block_perm, block_mask, pen_weight, w_query, w_key, w_value, w_out, w_sort,
    gain_one, gain_two, w_up, w_down,
):
    both = ("batch", "mp")
    _, rows, width = inputs.shape
    x = inputs.reshape(rows, width)
    cot = cotangent.reshape(rows, width)
    perm = block_perm.reshape(-1)
    mask = block_mask.reshape(-1)
    perm_row = block_perm.reshape(1, -1)
    mask_row = block_mask.reshape(1, -1)
    gain_one_row = gain_one.reshape(1, width)
    gain_two_row = gain_two.reshape(1, width)
    where = jnp.zeros((4,), jnp.int32)
    up_all = lax.all_gather(w_up.astype(BF16), "mp", axis=1, tiled=True)
    down_all = lax.all_gather(w_down.astype(BF16), "mp", axis=0, tiled=True)
    quarters = [
        jnp.stack([up_all[:, at : at + width], down_all[at : at + width]])
        for at in range(0, up_all.shape[1], width)
    ]
    act_one, q, k, v, probs, att, second, act_two_far, shares, sums, plan_log, chosen, entropy = forward(
        perm, mask, jnp.zeros((1,), jnp.int32), perm_row, mask_row, gain_one_row, gain_two_row, x,
        w_query, w_key, w_value, w_sort, w_out, w_query, w_query,
    )[:-1]
    tallies = jnp.broadcast_to(lax.psum(jnp.sum(mask_row).astype(F32), both) / width, (1, width))
    hidden, parts = [], []
    low, sofar = cot, None
    for index, weights in enumerate(quarters):
        if index == 0:
            hid, sofar, piece, low, act_two = feed_quarter("first", where, act_two_far, weights, low)
        elif index < len(quarters) - 1:
            hid, sofar, piece = feed_quarter("middle", where, act_two, weights, low, sofar)
        else:
            extra = (cot, second, att, w_out, gain_two_row, entropy)
            hid, grad_second, piece, grad_att, extra = feed_quarter(
                "last", where, act_two, weights, low, sofar, extra
            )
        hidden.append(hid)
        parts.append(piece[0])
    groups = [
        attend_back(perm, q, grad_att, probs, k, v, chosen, group) for group in range(width // GROUP_WIDTH)
    ]
    firsts = first_heads(where, act_one, groups[0], extra, shares, plan_log, perm_row, mask_row, 1)
    piece, gsum, block_total = last_heads(
        where, pen_weight, act_one, groups[1], firsts, shares, plan_log, sums, w_sort, perm_row, mask_row,
        tallies, 1,
    )
    grad_input = input_grad(
        [group[:3] for group in groups], gsum, x, grad_second, gain_one_row, w_query, w_key, w_value
    )
    output = layer_output(second, hidden, quarters)

    parts = jnp.concatenate(parts, axis=1).reshape(2, width, -1)
    parts = lax.psum(lax.psum_scatter(parts, "mp", scatter_dimension=2, tiled=True), "batch").astype(F32)
    grad_up, grad_down = parts[0], parts[1].T
    piece = lax.psum(piece, both)
    grad_query, grad_key, grad_value, grad_sort, grad_out, grad_gain_one, grad_gain_two, penalty = finish(
        where, [piece], w_query, w_key, w_value, w_sort, gain_one_row, block_total
    )
    return (
        output.reshape(inputs.shape),
        penalty.reshape(1),
        grad_input.reshape(inputs.shape),
        grad_query,
        grad_key,
        grad_value,
        grad_out,
        grad_sort,
        grad_gain_one.reshape(width),
        grad_gain_two.reshape(width),
        grad_up,
        grad_down,
    )


def solution(mesh):
    tokens = P(("batch", "mp"), None, None)
    blocks = P(("batch", "mp"), None)
    small = mesh.shape["batch"] == 16 and mesh.shape["mp"] == 2
    return jax.shard_map(
        local_small if small else local_any,
        mesh=mesh,
        in_specs=(tokens, tokens, blocks, blocks) + (P(),) * 8 + (P(None, "mp"), P("mp", None)),
        out_specs=(tokens, P(), tokens) + (P(),) * 7 + (P(None, "mp"), P("mp", None)),
        check_vma=False,
    )
```
